32 devices in a mesh: gx: 4 (over z), gy: 8 (over y, x, core).
Axes of the slice: x: 2, y: 2, z: 4, core: 2. Of those that a mesh axis runs over, the one named last changes fastest.
Arguments:
- queries: bfloat16 [512, 1536], P(('gx', 'gy')), may hold values from -40 to 40
- new_kv: bfloat16 [512, 1024], P(('gx', 'gy')), may hold values from -6 to 6
- cache_pool: bfloat16 [4096, 16, 1024], P(('gx', 'gy')), may hold values from -6 to 6
- cache_len: int32 [512], P(('gx', 'gy')), may hold values from 1 to 512, as said below
- local_pages: int32 [256, 32], P(('gx', 'gy')), may hold values from 0 to 127
- anchor: int32 [256], P(('gx', 'gy')), may hold values from 0 to 7, as said below
- push_pages: int32 [512, 32], P(('gx', 'gy')), may hold values from 0 to 127
- prefill_attn: bfloat16 [3584, 1536], P(('gx', 'gy')), may hold values from -4 to 4
- residual: bfloat16 [4096, 1536], P(('gx', 'gy')), may hold values from -7 to 7
- out_weight: bfloat16 [1536, 1536], P('gx'), may hold values from -0.15625 to 0.15625
- norm_gain: bfloat16 [1536], replicated, may hold values from 0.099609375 to 1.8984375
- router: bfloat16 [1536, 32], replicated, may hold values from -4 to 4
- routes: int32 [4096, 8], P(('gx', 'gy')), may hold values from 0 to 31, all different within a row; in each aligned block of 128 rows (0 to 127, 128 to 255, ...) at most 48 rows name the same one
- gate_up: bfloat16 [1536, 32, 1024], P('gx', 'gy'), may hold values from -0.15625 to 0.15625
- down_proj: bfloat16 [1536, 32, 512], P('gx', 'gy'), may hold values from -0.25 to 0.25
Outputs:
- attended: bfloat16 [512, 1536], P(('gx', 'gy'))
- layer_out: float32 [4096, 1536], P(('gx', 'gy'))
The draws below stay inside these ranges and needn't reach their ends.
Inputs may be any that keep to these rules, and one draw needn't show every extreme that they name: `cache_len`: every device holds a request with exactly 512 cached tokens. The last 8 requests of a device continue from the device in the same gx row whose gy column is anchor, never from the device itself; one column sends at most 2 of them to one device, and some column sends exactly 2 to each device. `routes`: no expert is named by more than 48 of the rows of one device.
All inputs are finite; a program needn't handle non-finite values.
Results may differ from the reference program's by a relative error of at most 0.0038.
Values may be sent and summed in bfloat16 or wider, within the bound.
No kernel may reach another device: no remote copies, remote signals or barrier semaphores. Data moves between devices by JAX's collectives and lax.ppermute only.
A program may use at most 192 MiB of HBM per device.

```python
import math
import jax
import jax.numpy as jnp
import numpy as np
from jax import lax

D = 1536
HEADS = 24
KV_HEADS = 8
HEAD = 64
EXPERTS = 32
FF = 512
TOP = 8
PAGE = 16
MAXLEN = 512
R_DEV = 16
P_DEV = 112
ROWS_DEV = 128
NPAGE = 32
LOCAL = 8
MOVED = 8
SLOT = 2
CAP = 48
POOL_DEV = 128
REQS = 512
PREFILL = 3584
ROWS = 4096
N_GX = 4
N_GY = 8


def draw_queries(key, part):
    normal_noise = jax.random.normal(jax.random.fold_in(key, 1), (REQS, D), jnp.float32)
    values = jnp.clip(normal_noise, -6.0, 6.0)
    return values.astype(jnp.bfloat16)


def draw_cache_pool(key, part):
    page_count = REQS // R_DEV * POOL_DEV
    kv_width = 2 * KV_HEADS * HEAD
    dims_all = (page_count, PAGE, kv_width)
    values = jnp.clip(jax.random.normal(jax.random.fold_in(key, 3), dims_all, jnp.float32), -6.0, 6.0)
    return values.astype(jnp.bfloat16)


def draw_residual(key, part):
    normal_noise = jax.random.normal(jax.random.fold_in(key, 4), (ROWS, D), jnp.float32)
    values = jnp.clip(normal_noise, -6.0, 6.0)
    return values.astype(jnp.bfloat16)


def draw_router(key, part):
    normal_noise = jax.random.normal(jax.random.fold_in(key, 6), (D, EXPERTS), jnp.float32)
    values = jnp.clip(normal_noise, -6.0, 6.0) / math.sqrt(D)
    return values.astype(jnp.bfloat16)


def draw_cache_len(key, part):
    devices = REQS // R_DEV
    limits = jax.random.randint(jax.random.fold_in(key, 21), (devices, 1), MAXLEN // 4, MAXLEN + 1)
    raw_draw = jax.random.randint(jax.random.fold_in(key, 22), (devices, R_DEV), 0, MAXLEN)
    lengths = 1 + raw_draw * limits // MAXLEN
    longest = jax.random.randint(jax.random.fold_in(key, 23), (devices, 1), 0, R_DEV)
    lengths = jnp.where(jnp.arange(R_DEV)[None, :] == longest, MAXLEN, lengths)
    return lengths.reshape(REQS).astype(jnp.int32)


def draw_anchor(key, part):
    devices = REQS // R_DEV
    device_keys = jax.random.split(jax.random.fold_in(key, 31), devices)

    def one_device(device_key):
        first_key, second_key = jax.random.split(device_key)
        order_draw = jax.random.permutation(first_key, N_GY - 1) + 1
        offsets = jnp.tile(order_draw, SLOT)[:MOVED]
        return jax.random.permutation(second_key, offsets)
    offsets = jax.vmap(one_device)(device_keys)
    columns = jnp.arange(devices) % N_GY
    return ((columns[:, None] + offsets) % N_GY).reshape(devices * MOVED).astype(jnp.int32)


def set_ends(drawn, key, least, top_value):
    shape = drawn.shape
    spot = [jax.random.randint(jax.random.fold_in(key, axis), (), 0, shape[axis]) for axis in range(len(shape))]
    drawn = drawn.at[tuple(spot)].set(least)
    longest = shape.index(max(shape))
    spot[longest] = (spot[longest] + 1) % shape[longest]
    return drawn.at[tuple(spot)].set(top_value)


def steps_of(rng, extent, cuts, smallest, high):
    loudness, own = 1.0, jax.random.fold_in(rng, 6)
    for dim, blocks in cuts:
        draws = jnp.exp(jax.random.uniform(jax.random.fold_in(own, dim), (blocks,), jnp.float32, smallest / len(cuts), high / len(cuts)))
        loudness = loudness * jnp.repeat(draws, extent[dim] // blocks).reshape([-1 if axis == dim else 1 for axis in range(len(extent))])
    return loudness


def routed_block(rng, own, number, rows, amount, top, limit, skew):
    order = jax.random.permutation(rng, amount)
    heavy_load, common = shares(amount, rows * top, limit, skew, True), shares(amount, rows * top, limit, skew, False)
    places = jnp.arange(amount)

    def named(sizes, offset_by):
        used = int((sizes > 0).sum())
        fixed = max(1, used // 4)
        moved = fixed + (places - fixed + offset_by * (used - fixed)) % max(1, amount - fixed)
        return jnp.zeros((amount,), jnp.int32).at[order[jnp.where(places < fixed, places, moved)]].set(jnp.asarray(sizes, jnp.int32))

    sizes = jnp.where(number % 4 == 0, named(heavy_load, number // 4), named(common, number - number // 4 - 1))
    mixed = jax.random.permutation(jax.random.fold_in(own, 3), amount)
    giver, sink = mixed[0:amount // 2 * 2:2], mixed[1:amount // 2 * 2:2]
    margin = jnp.minimum(sizes[giver] - 1, limit - sizes[sink]) // 2
    margin = jnp.where((giver == order[0]) | (sink == order[0]) | (sizes[sink] == 0), 0, jnp.maximum(margin, 0))
    moved = jax.random.randint(jax.random.fold_in(own, 4), (amount // 2,), 0, 1 << 20) % (margin + 1)
    sizes = sizes.at[giver].add(-moved).at[sink].add(moved)
    members = jnp.searchsorted(jnp.cumsum(sizes), jnp.arange(rows * top), side="right").astype(jnp.int32)
    listing = members.reshape(top, rows).T
    listing = listing[jax.random.permutation(jax.random.fold_in(own, 1), rows)]
    offset_by = jax.random.randint(jax.random.fold_in(own, 2), (rows, 1), 0, top)
    return jnp.take_along_axis(listing, (jnp.arange(top)[None, :] + offset_by) % top, axis=1)


def shares(amount, total, reach, skew, full):
    loads = [(1 << 20) // math.isqrt(standing ** skew) + 1 for standing in range(1, amount + 1)]
    largest = reach if full else min(reach, max(-(-total // amount), total * loads[0] // sum(loads)))
    least = 1 if total - largest >= amount - 1 else 0
    given, rest = [largest] + [least] * (amount - 1), total - largest - least * (amount - 1)
    while rest > 0:
        movable = [i for i in range(1, amount) if given[i] < largest] or [i for i in range(1, amount) if given[i] < reach]
        whole, remaining = sum([loads[i] for i in movable]), rest
        for i in movable:
            extra = min(reach - given[i], max(1, remaining * loads[i] // whole), rest)
            given[i] = given[i] + extra
            rest = rest - extra
    return np.array(given)


def scatter_about(key, extent, deviation, limit, pieces=(), kind=jnp.bfloat16):
    factor_of = steps_of(key, extent, pieces, -0.22, 0.18) if pieces else 1.0
    result = jax.random.normal(key, extent, jnp.float32) * deviation * factor_of
    return jnp.minimum(jnp.maximum(result, -limit), limit).astype(kind)


def setup_inputs(seed: int = 0) -> dict:
    keys = jax.random.split(jax.random.key(seed), 16)
    queries = draw_queries(jax.random.fold_in(keys[15], 71), 0)
    new_kv = scatter_about(keys[1], (REQS, 2 * KV_HEADS * HEAD), 1.0, 6.0, ((0, 32),))
    cache_pool = draw_cache_pool(jax.random.fold_in(keys[15], 71), 0)
    cache_len = draw_cache_len(jax.random.fold_in(keys[15], 71), 0)
    local_pages = set_ends(jax.random.randint(keys[4], (REQS // R_DEV * LOCAL, NPAGE), 0, POOL_DEV), jax.random.fold_in(keys[4], 1), 0, POOL_DEV - 1).astype(jnp.int32)
    anchor = draw_anchor(jax.random.fold_in(keys[15], 71), 0)
    push_pages = set_ends(jax.random.randint(keys[6], (REQS // R_DEV * N_GY * SLOT, NPAGE), 0, POOL_DEV), jax.random.fold_in(keys[6], 1), 0, POOL_DEV - 1).astype(jnp.int32)
    prefill_attn = scatter_about(keys[7], (PREFILL, D), 0.5, 4.0, ((0, 32),))
    residual = draw_residual(jax.random.fold_in(keys[15], 71), 0)
    out_weight = scatter_about(keys[9], (D, D), D ** -0.5, 0.15625, ((0, 4),))
    norm_gain = jnp.clip(1.0 + 0.18 * jax.random.normal(keys[10], (D,), jnp.float32), 0.099609375, 1.8984375).astype(jnp.bfloat16)
    router = draw_router(jax.random.fold_in(keys[15], 71), 0)
    routes_keys = jax.random.split(jax.random.fold_in(keys[12], 1), ROWS // ROWS_DEV)
    routes_turns = jax.random.permutation(jax.random.fold_in(keys[12], 3), ROWS // ROWS_DEV)
    routes = jax.vmap(lambda own, number: routed_block(jax.random.fold_in(keys[12], 2), own, number, ROWS_DEV, EXPERTS, TOP, CAP, 2))(routes_keys, routes_turns).reshape((ROWS, TOP))
    gate_up = scatter_about(keys[13], (D, EXPERTS, 2 * FF), D ** -0.5, 0.15625, ((0, 4), (1, 8)))
    down_proj = scatter_about(keys[14], (D, EXPERTS, FF), FF ** -0.5, 0.25, ((0, 4), (1, 8)))
    return {"queries": queries, "new_kv": new_kv, "cache_pool": cache_pool, "cache_len": cache_len, "local_pages": local_pages, "anchor": anchor, "push_pages": push_pages, "prefill_attn": prefill_attn, "residual": residual, "out_weight": out_weight, "norm_gain": norm_gain, "router": router, "routes": routes, "gate_up": gate_up, "down_proj": down_proj}


def partial_attend(query_heads, keyval, lengths):
    count_req, positions, kv_width = keyval.shape
    kv_count = query_heads.shape[1]
    head_size = query_heads.shape[3]
    half_width = kv_count * head_size
    key_rows = keyval[:, :, :half_width].reshape(count_req, positions, kv_count, head_size)
    value_rows = keyval[:, :, half_width:].reshape(count_req, positions, kv_count, head_size)
    scores = jnp.einsum('nkgh,ntkh->nkgt', query_heads.astype(jnp.float32), key_rows.astype(jnp.float32)) * (1.0 / math.sqrt(head_size))
    valid = (jnp.arange(positions)[None, :] < lengths[:, None])[:, None, None, :]
    masked = jnp.where(valid, scores, -1e+30)
    cache_max = lax.optimization_barrier(jnp.max(masked, axis=3))
    expos = jnp.where(valid, jnp.exp(masked - cache_max[..., None]), 0.0)
    totals = lax.optimization_barrier(jnp.sum(expos, axis=3))
    weights = lax.optimization_barrier(expos.astype(jnp.bfloat16)).astype(jnp.float32)
    mixture = jnp.einsum('nkgt,ntkh->nkgh', weights, value_rows.astype(jnp.float32))
    return (cache_max, totals, mixture)

def finish(query_heads, fresh, cache_max, totals, mixture):
    count_req, kv_count, group_size, head_size = query_heads.shape
    half_width = kv_count * head_size
    own_key = fresh[:, :half_width].reshape(count_req, kv_count, head_size)
    own_value = fresh[:, half_width:].reshape(count_req, kv_count, head_size).astype(jnp.float32)
    own_score = jnp.einsum('nkgh,nkh->nkg', query_heads.astype(jnp.float32), own_key.astype(jnp.float32)) * (1.0 / math.sqrt(head_size))
    highest = jnp.maximum(cache_max, own_score)
    old_share = jnp.exp(cache_max - highest)
    new_share = jnp.exp(own_score - highest)
    weighted = old_share[..., None] * mixture + new_share[..., None] * own_value[:, :, None, :]
    output = weighted / (old_share * totals + new_share)[..., None]
    return output.reshape(count_req, kv_count * group_size * head_size).astype(jnp.bfloat16)

def reference(queries, new_kv, cache_pool, cache_len, local_pages, anchor, push_pages, prefill_attn, residual, out_weight, norm_gain, router, routes, gate_up, down_proj):
    devices = N_GX * N_GY
    group_size = HEADS // KV_HEADS
    kv_width = 2 * KV_HEADS * HEAD
    pool_all = cache_pool.reshape(devices, POOL_DEV, PAGE, kv_width)
    local_all = local_pages.reshape(devices, LOCAL, NPAGE)
    anchor_all = anchor.reshape(devices, MOVED)
    push_all = push_pages.reshape(devices, N_GY, SLOT, NPAGE)
    matches = (anchor_all[:, :, None] == jnp.arange(N_GY, dtype=jnp.int32)[None, None, :]).astype(jnp.int32)
    earlier = lax.optimization_barrier(jnp.sum((jnp.cumsum(matches, axis=1) - 1) * matches, axis=2)).astype(jnp.int32)
    query_all = queries.reshape(devices, R_DEV, KV_HEADS, group_size, HEAD)
    length_all = cache_len.reshape(devices, R_DEV)
    fresh_all = new_kv.reshape(devices, R_DEV, kv_width)

    def attend_device(device_index):
        gx_row = device_index // N_GY
        gy_column = device_index % N_GY
        own_pool = pool_all[device_index]
        local_kv = own_pool[local_all[device_index]].reshape(LOCAL, MAXLEN, kv_width)
        sources = (gx_row * N_GY + anchor_all[device_index]).astype(jnp.int32)
        page_ids = push_all[sources, gy_column, earlier[device_index]]
        moved_kv = pool_all[sources[:, None], page_ids].reshape(MOVED, MAXLEN, kv_width)
        keyval = jnp.concatenate([local_kv, moved_kv], axis=0)
        cache_max, totals, mixture = partial_attend(query_all[device_index], keyval, length_all[device_index])
        return finish(query_all[device_index], fresh_all[device_index], cache_max, totals, mixture)
    attended = lax.map(attend_device, jnp.arange(devices, dtype=jnp.int32)).reshape(REQS, D)
    tokens = jnp.concatenate([attended.reshape(devices, R_DEV, D), prefill_attn.reshape(devices, P_DEV, D)], axis=1).reshape(ROWS, D)
    stream = residual.astype(jnp.float32) + jnp.dot(tokens, out_weight, preferred_element_type=jnp.float32)
    normed = (stream * lax.rsqrt(lax.optimization_barrier(jnp.mean(stream * stream, axis=1, keepdims=True)) + 1e-06) * norm_gain.astype(jnp.float32)).astype(jnp.bfloat16)
    logits = jnp.dot(normed, router, preferred_element_type=jnp.float32)
    chosen_logits = jnp.take_along_axis(logits, routes, axis=1)
    gate_weights = jax.nn.softmax(chosen_logits, axis=1)
    pair_weights = jnp.transpose(gate_up, (1, 0, 2)).astype(jnp.float32)
    down_weights = jnp.transpose(down_proj, (1, 2, 0)).astype(jnp.float32)
    normed_all = normed.reshape(devices, ROWS_DEV, D)
    routes_all = routes.reshape(devices, ROWS_DEV * TOP)
    gates_all = gate_weights.reshape(devices, ROWS_DEV, TOP)

    def experts_device(device_index):
        routes_dev = routes_all[device_index]
        route_hits = (routes_dev[:, None] == jnp.arange(EXPERTS, dtype=jnp.int32)[None, :]).astype(jnp.int32)
        places = lax.optimization_barrier(jnp.sum((jnp.cumsum(route_hits, axis=0) - 1) * route_hits, axis=1)).astype(jnp.int32)
        targets = (routes_dev * CAP + places).astype(jnp.int32)
        repeated = jnp.repeat(normed_all[device_index], TOP, axis=0)
        slab = jnp.zeros((EXPERTS * CAP, D), jnp.bfloat16).at[targets].set(repeated).reshape(EXPERTS, CAP, D)
        gate_pair = jnp.einsum('ecd,edf->ecf', slab.astype(jnp.float32), pair_weights)
        hidden = (jax.nn.silu(gate_pair[..., :FF]) * gate_pair[..., FF:]).astype(jnp.bfloat16)
        expert_rows = jnp.einsum('ecf,efd->ecd', hidden.astype(jnp.float32), down_weights).astype(jnp.bfloat16)
        picked = expert_rows.reshape(EXPERTS * CAP, D)[targets]
        picked = lax.optimization_barrier(picked).astype(jnp.float32).reshape(ROWS_DEV, TOP, D)
        return lax.optimization_barrier(jnp.sum(gates_all[device_index][:, :, None] * picked, axis=1))
    mixed = lax.map(experts_device, jnp.arange(devices, dtype=jnp.int32)).reshape(ROWS, D)
    layer_out = stream + mixed
    return (attended, layer_out)
```

```python
import functools
import math

import jax
import jax.numpy as jnp
from jax import lax
from jax.experimental import pallas as pl
from jax.experimental.pallas import tpu as pltpu
from jax.sharding import PartitionSpec as P

D = 1536
HEADS = 24
KV_HEADS = 8
HEAD = 64
GROUP = HEADS // KV_HEADS
EXPERTS = 32
FF = 512
TOP = 8
PAGE = 16
MAXLEN = 512
NPAGE = 32
R_DEV = 16
LOCAL = 8
MOVED = 8
CAP = 48
LANES = 128
WIDE = D + LANES
PAIRS = KV_HEADS // 2
BIG = 1e30
BF = jnp.bfloat16
F32 = jnp.float32


def vmem():
    return pl.BlockSpec(memory_space=pltpu.VMEM)


def smem():
    return pl.BlockSpec(memory_space=pltpu.SMEM)


def cost(flops, moved):
    return pl.CostEstimate(flops=flops, bytes_accessed=moved, transcendentals=0)


def attend_kernel(ask_ref, query_ref, table_ref, key_ref, value_ref, mix_ref, stat_ref, counts):
    step = pl.program_id(0)
    slots = table_ref.shape[0]
    pages = counts.shape[1] // PAGE

    @pl.when(step == 0)
    def _():
        lengths = ask_ref[:, D:].astype(jnp.int32)
        full, rest = lengths[:, 0:1], lengths[:, 1:2]
        table = table_ref[...]
        page = lax.broadcasted_iota(jnp.int32, (slots, pages), 1)
        whole = jnp.zeros((slots, pages), F32)
        part = jnp.zeros((slots, pages), F32)
        for p in range(NPAGE):
            hit = table[:, p : p + 1] == page
            whole += jnp.where(hit & (full > p), 1.0, 0.0)
            part += jnp.where(hit & (full == p), 1.0, 0.0)
        row = lax.broadcasted_iota(jnp.int32, (pages, pages * PAGE), 1)
        spread = jnp.where(
            row // PAGE == lax.broadcasted_iota(jnp.int32, (pages, pages * PAGE), 0), 1.0, 0.0
        ).astype(BF)
        whole = jnp.dot(whole.astype(BF), spread, preferred_element_type=F32)
        part = jnp.dot(part.astype(BF), spread, preferred_element_type=F32)
        place = lax.broadcasted_iota(jnp.int32, (slots, pages * PAGE), 1) % PAGE
        counts[...] = whole + jnp.where(place < rest, part, 0.0)

    lane = lax.broadcasted_iota(jnp.int32, (slots, LANES), 1)
    rows = []
    for j in range(2 * GROUP):
        side, chunk, half = j // GROUP, j // 2, j % 2
        part = query_ref[:, chunk * LANES : (chunk + 1) * LANES].astype(F32) * (1.0 / math.sqrt(HEAD))
        if side != half:
            part = pltpu.roll(part, HEAD, 1)
        rows.append(jnp.where((lane < HEAD) == (side == 0), part, 0.0).astype(BF))
    heads = jnp.concatenate(rows, axis=0)
    scores = lax.dot_general(
        heads, key_ref[...], (((1,), (1,)), ((), ())), preferred_element_type=F32
    )
    count = jnp.concatenate([counts[...]] * (2 * GROUP), axis=0)
    masked = jnp.where(count > 0.0, scores, -BIG)
    highest = jnp.max(masked, axis=1, keepdims=True)
    expos = jnp.exp(masked - highest)
    totals = jnp.sum(expos * count, axis=1, keepdims=True)
    weights = (expos.astype(BF).astype(F32) * count).astype(BF)
    mixture = jnp.dot(weights, value_ref[...], preferred_element_type=F32)

    @pl.when(step == 0)
    def _():
        stat_ref[...] = jnp.zeros_like(stat_ref)

    stat = stat_ref[...]
    for j in range(2 * GROUP):
        head = step * 2 * GROUP + j
        take = slice(j * slots, (j + 1) * slots)
        stat = jnp.where(lane == head, highest[take], stat)
        stat = jnp.where(lane == head + 64, totals[take], stat)
    stat_ref[...] = stat
    for chunk in range(GROUP):
        halves = []
        for half in range(2):
            j = 2 * chunk + half
            part = mixture[j * slots : (j + 1) * slots]
            if j // GROUP != half:
                part = pltpu.roll(part, HEAD, 1)
            halves.append(part)
        mix_ref[:, chunk * LANES : (chunk + 1) * LANES] = jnp.where(lane < HEAD, halves[0], halves[1])


def attend(ask, table, pool):
    slots = ask.shape[0]
    tokens = pool.shape[0]
    width = 2 * GROUP * HEAD
    return pl.pallas_call(
        attend_kernel,
        grid=(PAIRS,),
        in_specs=[
            pl.BlockSpec((slots, WIDE), lambda s: (0, 0)),
            pl.BlockSpec((slots, width), lambda s: (0, s)),
            pl.BlockSpec((slots, NPAGE), lambda s: (0, 0)),
            pl.BlockSpec((tokens, LANES), lambda s: (0, s)),
            pl.BlockSpec((tokens, LANES), lambda s: (0, PAIRS + s)),
        ],
        out_specs=[
            pl.BlockSpec((slots, width), lambda s: (0, s)),
            pl.BlockSpec((slots, LANES), lambda s: (0, 0)),
        ],
        out_shape=[
            jax.ShapeDtypeStruct((slots, D), F32),
            jax.ShapeDtypeStruct((slots, LANES), F32),
        ],
        scratch_shapes=[pltpu.VMEM((slots, tokens), F32)],
        compiler_params=pltpu.CompilerParams(vmem_limit_bytes=48 * 1024 * 1024),
        cost_estimate=cost(10**9, 24 * 10**6),
        name="attend",
    )(ask, ask, table, pool, pool)


def stream_kernel(
    chosen_ref, query_ref, fresh_ref, mix_ref, stat_ref, back_ref, prefill_ref, residual_ref,
    out_ref, gain_ref, router_ref, routes_ref,
    attended_ref, stream_ref, send_ref, tokens,
):
    count = query_ref.shape[0]
    lane = lax.broadcasted_iota(jnp.int32, (count, LANES), 1)
    low = lane < HEAD
    picked = [back_ref[pl.ds(chosen_ref[m], 1), :] for m in range(MOVED)]
    picked = jnp.concatenate(picked, axis=0)
    mix = jnp.concatenate([mix_ref[:LOCAL, :], picked[:, :D]], axis=0)
    stat = jnp.concatenate([stat_ref[:LOCAL, :], picked[:, D:]], axis=0)
    fresh = fresh_ref[...].astype(F32)

    def spread(first, second, base):
        sides = []
        for half, head in enumerate((first, second)):
            part = fresh[:, base + head // 2 * LANES : base + head // 2 * LANES + LANES]
            sides.append(pltpu.roll(part, HEAD, 1) if head % 2 != half else part)
        return jnp.where(low, sides[0], sides[1])

    def both(first, second):
        return jnp.where(low, first, second)

    for chunk in range(HEADS // 2):
        first, second = 2 * chunk, 2 * chunk + 1
        span = slice(chunk * LANES, (chunk + 1) * LANES)
        keys = spread(first // GROUP, second // GROUP, 0)
        values = spread(first // GROUP, second // GROUP, KV_HEADS * HEAD)
        product = query_ref[:, span].astype(F32) * keys
        scale = 1.0 / math.sqrt(HEAD)
        own = both(
            jnp.sum(jnp.where(low, product, 0.0), axis=1, keepdims=True) * scale,
            jnp.sum(jnp.where(low, 0.0, product), axis=1, keepdims=True) * scale,
        )
        cache_max = both(stat[:, first : first + 1], stat[:, second : second + 1])
        total = both(stat[:, 64 + first : 65 + first], stat[:, 64 + second : 65 + second])
        highest = jnp.maximum(cache_max, own)
        old = jnp.exp(cache_max - highest)
        new = jnp.exp(own - highest)
        output = (old * mix[:, span] + new * values) / (old * total + new)
        tokens[:count, span] = output.astype(BF)
    attended_ref[...] = tokens[:count, :]
    tokens[count:, :] = prefill_ref[...]
    stream = residual_ref[...].astype(F32) + jnp.dot(
        tokens[...], out_ref[...], preferred_element_type=F32
    )
    stream_ref[...] = stream
    normed = (
        stream
        * lax.rsqrt(jnp.mean(stream * stream, axis=1, keepdims=True) + 1e-06)
        * gain_ref[...].astype(F32)
    ).astype(BF)
    send_ref[:, :D] = normed
    logits = jnp.dot(normed, router_ref[...], preferred_element_type=F32)
    rows = logits.shape[0]
    expert = lax.broadcasted_iota(jnp.int32, (rows, LANES), 1)
    routes = routes_ref[...]
    named = expert == routes[:, 0:1]
    for k in range(1, TOP):
        named = named | (expert == routes[:, k : k + 1])
    masked = jnp.where(named, logits, -BIG)
    expos = jnp.where(named, jnp.exp(masked - jnp.max(masked, axis=1, keepdims=True)), 0.0)
    gates = expos / jnp.sum(expos, axis=1, keepdims=True)
    coarse = gates.astype(BF).astype(F32)
    fine = pltpu.roll(gates - coarse, 64, 1)
    send_ref[:, D:] = jnp.where(expert < 64, coarse, fine).astype(BF)


def make_stream(
    chosen, queries, fresh, mix, stat, back, prefill, residual, out_weight, gain, router, routes
):
    rows = residual.shape[0]
    count = queries.shape[0]
    return pl.pallas_call(
        stream_kernel,
        in_specs=[smem()] + [vmem()] * 11,
        out_specs=[vmem()] * 3,
        out_shape=[
            jax.ShapeDtypeStruct((count, D), BF),
            jax.ShapeDtypeStruct((rows, D), F32),
            jax.ShapeDtypeStruct((rows, WIDE), BF),
        ],
        scratch_shapes=[pltpu.VMEM((rows, D), BF)],
        compiler_params=pltpu.CompilerParams(vmem_limit_bytes=48 * 1024 * 1024),
        cost_estimate=cost(2 * 10**9, 24 * 10**6),
        name="stream",
    )(chosen, queries, fresh, mix, stat, back, prefill, residual, out_weight, gain, router, routes)


def expert_kernel(shards, place_ref, first_ref, second_ref, third_ref, *rest):
    weights, (keep_ref, away_ref, rows_ref, hidden_ref) = rest[: 2 * shards], rest[2 * shards :]
    part = D // shards
    one = first_ref.shape[0]
    rows_ref[:one, :] = first_ref[...]
    rows_ref[one : 2 * one, :] = second_ref[...]
    rows_ref[2 * one :, :] = third_ref[...]
    half = 2 * one
    for block, out_ref in enumerate((keep_ref, away_ref)):
        span = slice(block * half, (block + 1) * half)
        gates = rows_ref[span, D:].astype(F32)
        gates = gates + pltpu.roll(gates, 64, 1)
        lane = lax.broadcasted_iota(jnp.int32, gates.shape, 1)
        for side in range(2):
            total = None
            for s in range(shards):
                at = pl.multiple_of(place_ref[s] * part, LANES)
                term = jnp.dot(
                    rows_ref[span, pl.ds(at, part)],
                    weights[side * shards + s][:, : 2 * FF],
                    preferred_element_type=F32,
                )
                total = term if total is None else total + term
            gate = total[:, :FF]
            hidden_ref[side] = (gate / (1.0 + jnp.exp(-gate)) * total[:, FF:]).astype(BF)
        share = [
            jnp.sum(jnp.where(lane == place_ref[shards + side], gates, 0.0), axis=1, keepdims=True)
            for side in range(2)
        ]
        for s in range(shards):
            at = pl.multiple_of(place_ref[s] * part, LANES)
            total = None
            for side in range(2):
                made = lax.dot_general(
                    hidden_ref[side],
                    weights[side * shards + s][:, 2 * FF :],
                    (((1,), (1,)), ((), ())),
                    preferred_element_type=F32,
                )
                made = share[side] * made.astype(BF).astype(F32)
                total = made if total is None else total + made
            out_ref[:, pl.ds(at, part)] = total.astype(BF)


def run_experts(place, first, second, third, weights):
    shards = len(weights) // 2
    one = first.shape[0]
    return pl.pallas_call(
        functools.partial(expert_kernel, shards),
        in_specs=[smem()] + [vmem()] * (3 + 2 * shards),
        out_specs=[vmem()] * 2,
        out_shape=[jax.ShapeDtypeStruct((2 * one, D), BF)] * 2,
        scratch_shapes=[pltpu.VMEM((4 * one, WIDE), BF), pltpu.VMEM((2, 2 * one, FF), BF)],
        compiler_params=pltpu.CompilerParams(vmem_limit_bytes=52 * 1024 * 1024),
        cost_estimate=cost(5 * 10**9, 12 * 10**6),
        name="experts",
    )(place, first, second, third, *weights)


def swap(x, axis, how):
    return lax.ppermute(x, axis, [(i, how(i)) for i in range(lax.axis_size(axis))])


def near(j):
    return j ^ (2 if j % 2 == 0 else 4)


def far(j):
    return j ^ (4 if j % 2 == 0 else 2)


def exchange_experts(gate_up, down_proj):
    planes = lax.axis_size("gx")
    row = lax.axis_index("gx")
    blocks = []
    for k in range(planes):
        slot = row ^ k
        block = jnp.concatenate(
            [
                lax.dynamic_index_in_dim(gate_up, slot, axis=1, keepdims=False),
                lax.dynamic_index_in_dim(down_proj, slot, axis=1, keepdims=False),
            ],
            axis=1,
        )
        blocks.append(swap(block, "gx", lambda i, k=k: i ^ k) if k else block)
    return blocks + [swap(block, "gy", lambda j: j ^ 1) for block in blocks]


def swapped_experts(send, stream, gate_up, down_proj):
    planes = lax.axis_size("gx")
    row, column = lax.axis_index("gx"), lax.axis_index("gy")
    weights = exchange_experts(gate_up, down_proj)
    place = jnp.stack(
        [row ^ k for k in range(planes)]
        + [column * planes + row, (column ^ 1) * planes + row]
    ).astype(jnp.int32)
    rows = send.shape[0]
    chunks = []
    for k in range(planes):
        mine = swap(send, "gx", lambda i, k=k: i ^ k) if k else send
        second = swap(mine, "gy", near)
        third = swap(jnp.concatenate([mine, second], axis=0), "gy", far)
        chunks.append((mine, second, third))
    result = stream
    for k in reversed(range(planes)):
        keep, away = run_experts(place, *chunks[k], weights)
        arrived = swap(away, "gy", far)
        total = keep.astype(F32) + arrived.astype(F32)
        arrived = swap(total[rows:].astype(BF), "gy", near)
        total = total[:rows] + arrived.astype(F32)
        if k:
            total = swap(total.astype(BF), "gx", lambda i, k=k: i ^ k).astype(F32)
        result = result + total
    return result


def gathered_experts(send, stream, routes, gate_up, down_proj):
    columns = lax.axis_size("gy")
    normed = send[:, :D]
    gates = send[:, D : D + EXPERTS].astype(F32) + send[:, D + 64 : D + 64 + EXPERTS].astype(F32)
    gate_weights = jnp.take_along_axis(gates, routes, axis=1)
    row_count = normed.shape[0]
    full_pair = lax.all_gather(gate_up, "gx", axis=0, tiled=True)
    full_down = lax.all_gather(down_proj, "gx", axis=0, tiled=True)
    flat_routes = routes.reshape(row_count * TOP)
    route_hits = (flat_routes[:, None] == jnp.arange(EXPERTS, dtype=jnp.int32)[None, :]).astype(
        jnp.int32
    )
    places = jnp.sum((jnp.cumsum(route_hits, axis=0) - 1) * route_hits, axis=1)
    targets = flat_routes * CAP + places
    repeated = jnp.repeat(normed, TOP, axis=0)
    experts_dev = full_pair.shape[1]
    outgoing_rows = (
        jnp.zeros((EXPERTS * CAP, D), BF)
        .at[targets]
        .set(repeated)
        .reshape(columns, experts_dev, CAP, D)
    )
    arrived = lax.all_to_all(outgoing_rows, "gy", split_axis=0, concat_axis=0, tiled=True)
    gate_pair = jnp.einsum("secd,def->secf", arrived, full_pair, preferred_element_type=F32)
    hidden = (jax.nn.silu(gate_pair[..., :FF]) * gate_pair[..., FF:]).astype(BF)
    expert_rows = jnp.einsum(
        "secf,def->secd", hidden, full_down, preferred_element_type=F32
    ).astype(BF)
    returned = lax.all_to_all(expert_rows, "gy", split_axis=0, concat_axis=0, tiled=True).reshape(
        EXPERTS * CAP, D
    )
    picked = returned[targets].astype(F32).reshape(row_count, TOP, D)
    return stream + jnp.sum(gate_weights[:, :, None] * picked, axis=1)


def gather_out(out_weight):
    columns = lax.axis_size("gy")
    share = out_weight.shape[0] // columns
    mine = lax.dynamic_slice_in_dim(out_weight, lax.axis_index("gy") * share, share, axis=0)
    return lax.all_gather(mine, ("gx", "gy"), axis=0, tiled=True)


def body(
    queries,
    new_kv,
    cache_pool,
    cache_len,
    local_pages,
    anchor,
    push_pages,
    prefill_attn,
    residual,
    out_weight,
    norm_gain,
    router,
    routes,
    gate_up,
    down_proj,
):
    columns = lax.axis_size("gy")
    slot_count = (MOVED + columns - 2) // (columns - 1)
    pool = cache_pool.reshape(-1, cache_pool.shape[2])
    matches = (anchor[:, None] == jnp.arange(columns, dtype=jnp.int32)[None, :]).astype(jnp.int32)
    earlier = jnp.sum((jnp.cumsum(matches, axis=0) - 1) * matches, axis=1)
    chosen = anchor * slot_count + earlier
    lengths = jnp.stack([cache_len // PAGE, cache_len % PAGE], axis=1).astype(BF)
    ask = jnp.concatenate([queries, jnp.pad(lengths, ((0, 0), (0, LANES - 2)))], axis=1)
    slots = columns * slot_count
    where = (chosen[None, :] == jnp.arange(slots, dtype=jnp.int32)[:, None]).astype(BF)
    outgoing = jnp.dot(where, ask[LOCAL:], preferred_element_type=F32).astype(BF)
    incoming = lax.all_to_all(
        outgoing.reshape(columns, slot_count, WIDE), "gy", split_axis=0, concat_axis=0, tiled=True
    ).reshape(slots, WIDE)
    mix, stat = attend(
        jnp.concatenate([ask[:LOCAL], incoming], axis=0),
        jnp.concatenate([local_pages, push_pages], axis=0),
        pool,
    )
    answers = jnp.concatenate([mix[LOCAL:], stat[LOCAL:]], axis=1).reshape(
        columns, slot_count, WIDE
    )
    back = lax.all_to_all(answers, "gy", split_axis=0, concat_axis=0, tiled=True).reshape(
        slots, WIDE
    )
    attended, stream, send = make_stream(
        chosen,
        queries,
        new_kv,
        mix,
        stat,
        back,
        prefill_attn,
        residual,
        gather_out(out_weight),
        norm_gain.reshape(1, D),
        jnp.pad(router, ((0, 0), (0, LANES - EXPERTS))),
        routes,
    )
    planes = lax.axis_size("gx")
    if columns == 8 and planes & (planes - 1) == 0 and gate_up.shape[1] == planes:
        layer_out = swapped_experts(send, stream, gate_up, down_proj)
    else:
        layer_out = gathered_experts(send, stream, routes, gate_up, down_proj)
    return (attended, layer_out)


def solution(mesh):
    placed = (
        P(("gx", "gy"), None),
        P(("gx", "gy"), None),
        P(("gx", "gy"), None, None),
        P(("gx", "gy")),
        P(("gx", "gy"), None),
        P(("gx", "gy")),
        P(("gx", "gy"), None),
        P(("gx", "gy"), None),
        P(("gx", "gy"), None),
        P("gx", None),
        P(),
        P(),
        P(("gx", "gy"), None),
        P("gx", "gy", None),
        P("gx", "gy", None),
    )
    return jax.shard_map(
        body,
        mesh=mesh,
        in_specs=placed,
        out_specs=(P(("gx", "gy"), None), P(("gx", "gy"), None)),
        check_vma=False,
    )
```

```python
import functools
import math

import jax
import jax.numpy as jnp
from jax import lax
from jax.experimental import pallas as pl
from jax.experimental.pallas import tpu as pltpu
from jax.sharding import PartitionSpec as P

D = 1536
HEADS = 24
KV_HEADS = 8
HEAD = 64
GROUP = HEADS // KV_HEADS
EXPERTS = 32
FF = 512
TOP = 8
PAGE = 16
MAXLEN = 512
NPAGE = 32
R_DEV = 16
LOCAL = 8
MOVED = 8
CAP = 48
LANES = 128
WIDE = D + LANES
PAIRS = KV_HEADS // 2
BIG = 1e30
BF = jnp.bfloat16
F32 = jnp.float32


def vmem():
    return pl.BlockSpec(memory_space=pltpu.VMEM)


def smem():
    return pl.BlockSpec(memory_space=pltpu.SMEM)


def cost(flops, moved):
    return pl.CostEstimate(flops=flops, bytes_accessed=moved, transcendentals=0)


def attend_kernel(ask_ref, query_ref, table_ref, key_ref, value_ref, mix_ref, stat_ref, counts):
    step = pl.program_id(0)
    slots = table_ref.shape[0]
    pages = counts.shape[1] // PAGE

    @pl.when(step == 0)
    def _():
        lengths = ask_ref[:, D:].astype(jnp.int32)
        full, rest = lengths[:, 0:1], lengths[:, 1:2]
        table = table_ref[...]
        page = lax.broadcasted_iota(jnp.int32, (slots, pages), 1)
        whole = jnp.zeros((slots, pages), F32)
        part = jnp.zeros((slots, pages), F32)
        for p in range(NPAGE):
            hit = table[:, p : p + 1] == page
            whole += jnp.where(hit & (full > p), 1.0, 0.0)
            part += jnp.where(hit & (full == p), 1.0, 0.0)
        row = lax.broadcasted_iota(jnp.int32, (pages, pages * PAGE), 1)
        spread = jnp.where(
            row // PAGE == lax.broadcasted_iota(jnp.int32, (pages, pages * PAGE), 0), 1.0, 0.0
        ).astype(BF)
        whole = jnp.dot(whole.astype(BF), spread, preferred_element_type=F32)
        part = jnp.dot(part.astype(BF), spread, preferred_element_type=F32)
        place = lax.broadcasted_iota(jnp.int32, (slots, pages * PAGE), 1) % PAGE
        counts[...] = whole + jnp.where(place < rest, part, 0.0)

    lane = lax.broadcasted_iota(jnp.int32, (slots, LANES), 1)
    rows = []
    for j in range(2 * GROUP):
        side, chunk, half = j // GROUP, j // 2, j % 2
        part = query_ref[:, chunk * LANES : (chunk + 1) * LANES].astype(F32) * (1.0 / math.sqrt(HEAD))
        if side != half:
            part = pltpu.roll(part, HEAD, 1)
        rows.append(jnp.where((lane < HEAD) == (side == 0), part, 0.0).astype(BF))
    heads = jnp.concatenate(rows, axis=0)
    scores = lax.dot_general(
        heads, key_ref[...], (((1,), (1,)), ((), ())), preferred_element_type=F32
    )
    count = jnp.concatenate([counts[...]] * (2 * GROUP), axis=0)
    masked = jnp.where(count > 0.0, scores, -BIG)
    highest = jnp.max(masked, axis=1, keepdims=True)
    expos = jnp.exp(masked - highest)
    totals = jnp.sum(expos * count, axis=1, keepdims=True)
    weights = (expos.astype(BF).astype(F32) * count).astype(BF)
    mixture = jnp.dot(weights, value_ref[...], preferred_element_type=F32)

    @pl.when(step == 0)
    def _():
        stat_ref[...] = jnp.zeros_like(stat_ref)

    stat = stat_ref[...]
    for j in range(2 * GROUP):
        head = step * 2 * GROUP + j
        take = slice(j * slots, (j + 1) * slots)
        stat = jnp.where(lane == head, highest[take], stat)
        stat = jnp.where(lane == head + 64, totals[take], stat)
    stat_ref[...] = stat
    for chunk in range(GROUP):
        halves = []
        for half in range(2):
            j = 2 * chunk + half
            part = mixture[j * slots : (j + 1) * slots]
            if j // GROUP != half:
                part = pltpu.roll(part, HEAD, 1)
            halves.append(part)
        mix_ref[:, chunk * LANES : (chunk + 1) * LANES] = jnp.where(lane < HEAD, halves[0], halves[1])


def attend(ask, table, pool):
    slots = ask.shape[0]
    tokens = pool.shape[0]
    width = 2 * GROUP * HEAD
    return pl.pallas_call(
        attend_kernel,
        grid=(PAIRS,),
        in_specs=[
            pl.BlockSpec((slots, WIDE), lambda s: (0, 0)),
            pl.BlockSpec((slots, width), lambda s: (0, s)),
            pl.BlockSpec((slots, NPAGE), lambda s: (0, 0)),
            pl.BlockSpec((tokens, LANES), lambda s: (0, s)),
            pl.BlockSpec((tokens, LANES), lambda s: (0, PAIRS + s)),
        ],
        out_specs=[
            pl.BlockSpec((slots, width), lambda s: (0, s)),
            pl.BlockSpec((slots, LANES), lambda s: (0, 0)),
        ],
        out_shape=[
            jax.ShapeDtypeStruct((slots, D), F32),
            jax.ShapeDtypeStruct((slots, LANES), F32),
        ],
        scratch_shapes=[pltpu.VMEM((slots, tokens), F32)],
        compiler_params=pltpu.CompilerParams(vmem_limit_bytes=48 * 1024 * 1024),
        cost_estimate=cost(10**9, 24 * 10**6),
        name="attend",
    )(ask, ask, table, pool, pool)


def stream_kernel(
    pieces, chosen_ref, at_ref, query_ref, fresh_ref, mix_ref, stat_ref, back_ref, prefill_ref,
    residual_ref, gain_ref, router_ref, routes_ref, *rest
):
    parts, rest = rest[: len(pieces)], rest[len(pieces) :]
    attended_ref, stream_ref, send_ref, tokens, out_ref, sems = rest
    copies = []
    for part, (blocks, rows) in zip(parts, pieces):
        for block in range(blocks):
            n = len(copies)
            at = pl.multiple_of(at_ref[n], 16)
            copy = pltpu.make_async_copy(
                part.at[pl.ds(block * rows, rows)], out_ref.at[pl.ds(at, rows)], sems.at[n]
            )
            copy.start()
            copies.append(copy)
    count = query_ref.shape[0]
    lane = lax.broadcasted_iota(jnp.int32, (count, LANES), 1)
    low = lane < HEAD
    picked = [back_ref[pl.ds(chosen_ref[m], 1), :] for m in range(MOVED)]
    picked = jnp.concatenate(picked, axis=0)
    mix = jnp.concatenate([mix_ref[:LOCAL, :], picked[:, :D]], axis=0)
    stat = jnp.concatenate([stat_ref[:LOCAL, :], picked[:, D:]], axis=0)
    fresh = fresh_ref[...].astype(F32)

    def spread(first, second, base):
        sides = []
        for half, head in enumerate((first, second)):
            part = fresh[:, base + head // 2 * LANES : base + head // 2 * LANES + LANES]
            sides.append(pltpu.roll(part, HEAD, 1) if head % 2 != half else part)
        return jnp.where(low, sides[0], sides[1])

    def both(first, second):
        return jnp.where(low, first, second)

    for chunk in range(HEADS // 2):
        first, second = 2 * chunk, 2 * chunk + 1
        span = slice(chunk * LANES, (chunk + 1) * LANES)
        keys = spread(first // GROUP, second // GROUP, 0)
        values = spread(first // GROUP, second // GROUP, KV_HEADS * HEAD)
        product = query_ref[:, span].astype(F32) * keys
        scale = 1.0 / math.sqrt(HEAD)
        own = both(
            jnp.sum(jnp.where(low, product, 0.0), axis=1, keepdims=True) * scale,
            jnp.sum(jnp.where(low, 0.0, product), axis=1, keepdims=True) * scale,
        )
        cache_max = both(stat[:, first : first + 1], stat[:, second : second + 1])
        total = both(stat[:, 64 + first : 65 + first], stat[:, 64 + second : 65 + second])
        highest = jnp.maximum(cache_max, own)
        old = jnp.exp(cache_max - highest)
        new = jnp.exp(own - highest)
        output = (old * mix[:, span] + new * values) / (old * total + new)
        tokens[:count, span] = output.astype(BF)
    attended_ref[...] = tokens[:count, :]
    tokens[count:, :] = prefill_ref[...]
    for copy in copies:
        copy.wait()
    stream = residual_ref[...].astype(F32) + jnp.dot(
        tokens[...], out_ref[...], preferred_element_type=F32
    )
    stream_ref[...] = stream
    normed = (
        stream
        * lax.rsqrt(jnp.mean(stream * stream, axis=1, keepdims=True) + 1e-06)
        * gain_ref[...].astype(F32)
    ).astype(BF)
    send_ref[:, :D] = normed
    logits = jnp.dot(normed, router_ref[...], preferred_element_type=F32)
    rows = logits.shape[0]
    expert = lax.broadcasted_iota(jnp.int32, (rows, LANES), 1)
    routes = routes_ref[...]
    named = expert == routes[:, 0:1]
    for k in range(1, TOP):
        named = named | (expert == routes[:, k : k + 1])
    masked = jnp.where(named, logits, -BIG)
    expos = jnp.where(named, jnp.exp(masked - jnp.max(masked, axis=1, keepdims=True)), 0.0)
    gates = expos / jnp.sum(expos, axis=1, keepdims=True)
    coarse = gates.astype(BF).astype(F32)
    fine = pltpu.roll(gates - coarse, 64, 1)
    send_ref[:, D:] = jnp.where(expert < 64, coarse, fine).astype(BF)


def make_stream(
    chosen, queries, fresh, mix, stat, back, prefill, residual, out_parts, gain, router, routes
):
    rows = residual.shape[0]
    count = queries.shape[0]
    at, parts, pieces = out_parts
    return pl.pallas_call(
        functools.partial(stream_kernel, pieces),
        in_specs=[smem()] * 2 + [vmem()] * 10 + [pl.BlockSpec(memory_space=pl.ANY)] * len(parts),
        out_specs=[vmem()] * 3,
        out_shape=[
            jax.ShapeDtypeStruct((count, D), BF),
            jax.ShapeDtypeStruct((rows, D), F32),
            jax.ShapeDtypeStruct((rows, WIDE), BF),
        ],
        scratch_shapes=[
            pltpu.VMEM((rows, D), BF),
            pltpu.VMEM((D, D), BF),
            pltpu.SemaphoreType.DMA((sum(blocks for blocks, _ in pieces),)),
        ],
        compiler_params=pltpu.CompilerParams(vmem_limit_bytes=48 * 1024 * 1024),
        cost_estimate=cost(2 * 10**9, 24 * 10**6),
        name="stream",
    )(chosen, at, queries, fresh, mix, stat, back, prefill, residual, gain, router, routes, *parts)


def expert_kernel(shards, place_ref, first_ref, second_ref, third_ref, *rest):
    weights, rest = rest[: 2 * shards], rest[2 * shards :]
    keep_ref, away_ref, rows_ref, held_ref, sems = rest
    part = D // shards
    one = first_ref.shape[0]
    copies = []
    for n in range(2 * shards):
        at = pl.multiple_of(place_ref[n % shards] * part, LANES)
        copy = pltpu.make_async_copy(
            weights[n], held_ref.at[n // shards, pl.ds(at, part)], sems.at[n]
        )
        copy.start()
        copies.append(copy)
    rows_ref[:one, :] = first_ref[...]
    rows_ref[one : 2 * one, :] = second_ref[...]
    rows_ref[2 * one :, :] = third_ref[...]
    gates = rows_ref[:, D:].astype(F32)
    gates = gates + pltpu.roll(gates, 64, 1)
    lane = lax.broadcasted_iota(jnp.int32, gates.shape, 1)
    total = None
    for side in range(2):
        for copy in copies[side * shards : (side + 1) * shards]:
            copy.wait()
        pair = jnp.dot(
            rows_ref[:, :D], held_ref[side, :, : 2 * FF], preferred_element_type=F32
        )
        gate = pair[:, :FF]
        hidden = (gate / (1.0 + jnp.exp(-gate)) * pair[:, FF:]).astype(BF)
        share = jnp.sum(
            jnp.where(lane == place_ref[shards + side], gates, 0.0), axis=1, keepdims=True
        )
        made = lax.dot_general(
            hidden,
            held_ref[side, :, 2 * FF :],
            (((1,), (1,)), ((), ())),
            preferred_element_type=F32,
        )
        made = share * made.astype(BF).astype(F32)
        total = made if total is None else total + made
    keep_ref[...] = total[: 2 * one].astype(BF)
    away_ref[...] = total[2 * one :].astype(BF)


def run_experts(place, first, second, third, weights):
    shards = len(weights) // 2
    one = first.shape[0]
    return pl.pallas_call(
        functools.partial(expert_kernel, shards),
        in_specs=[smem()]
        + [vmem()] * 3
        + [pl.BlockSpec(memory_space=pl.ANY)] * (2 * shards),
        out_specs=[vmem()] * 2,
        out_shape=[jax.ShapeDtypeStruct((2 * one, D), BF)] * 2,
        scratch_shapes=[
            pltpu.VMEM((4 * one, WIDE), BF),
            pltpu.VMEM((2, D, 3 * FF), BF),
            pltpu.SemaphoreType.DMA((2 * shards,)),
        ],
        compiler_params=pltpu.CompilerParams(vmem_limit_bytes=52 * 1024 * 1024),
        cost_estimate=cost(5 * 10**9, 12 * 10**6),
        name="experts",
    )(place, first, second, third, *weights)


def pack_kernel(slot_ref, gate_ref, down_ref, *rest):
    outs, (held_ref, sems) = rest[:-2], rest[-2:]
    depth, experts = gate_ref.shape[:2]
    step = 16

    @pl.loop(0, depth // step)
    def _(n):
        at = pl.ds(pl.multiple_of(n * step, step), step)
        gate = gate_ref[at]
        down = down_ref[at]
        for e in range(experts):
            held_ref[e, at, : 2 * FF] = gate[:, e, :]
            held_ref[e, at, 2 * FF :] = down[:, e, :]

    copies = []
    for k, out in enumerate(outs):
        copy = pltpu.make_async_copy(held_ref.at[slot_ref[k]], out, sems.at[k])
        copy.start()
        copies.append(copy)
    for copy in copies:
        copy.wait()


def pack_experts(slots, gate_up, down_proj):
    depth, experts = gate_up.shape[:2]
    return pl.pallas_call(
        pack_kernel,
        in_specs=[smem()] + [vmem()] * 2,
        out_specs=[pl.BlockSpec(memory_space=pl.ANY)] * experts,
        out_shape=[jax.ShapeDtypeStruct((depth, 3 * FF), BF)] * experts,
        scratch_shapes=[
            pltpu.VMEM((experts, depth, 3 * FF), BF),
            pltpu.SemaphoreType.DMA((experts,)),
        ],
        compiler_params=pltpu.CompilerParams(vmem_limit_bytes=32 * 1024 * 1024),
        cost_estimate=cost(10**6, 10 * 10**6),
        name="pack",
    )(slots, gate_up, down_proj)


def swap(x, axis, how):
    return lax.ppermute(x, axis, [(i, how(i)) for i in range(lax.axis_size(axis))])


def near(j):
    return j ^ (2 if j % 2 == 0 else 4)


def far(j):
    return j ^ (4 if j % 2 == 0 else 2)


def exchange_experts(gate_up, down_proj):
    planes = lax.axis_size("gx")
    row = lax.axis_index("gx")
    slots = jnp.stack([row ^ k for k in range(planes)]).astype(jnp.int32)
    blocks = pack_experts(slots, gate_up, down_proj)
    blocks = [
        swap(block, "gx", lambda i, k=k: i ^ k) if k else block for k, block in enumerate(blocks)
    ]
    return blocks + [swap(block, "gy", lambda j: j ^ 1) for block in blocks]


def swapped_experts(send, stream, gate_up, down_proj):
    planes = lax.axis_size("gx")
    row, column = lax.axis_index("gx"), lax.axis_index("gy")
    weights = exchange_experts(gate_up, down_proj)
    place = jnp.stack(
        [row ^ k for k in range(planes)]
        + [column * planes + row, (column ^ 1) * planes + row]
    ).astype(jnp.int32)
    rows = send.shape[0]
    chunks = []
    for k in range(planes):
        mine = swap(send, "gx", lambda i, k=k: i ^ k) if k else send
        second = swap(mine, "gy", near)
        third = swap(jnp.concatenate([mine, second], axis=0), "gy", far)
        chunks.append((mine, second, third))
    result = stream
    for k in reversed(range(planes)):
        keep, away = run_experts(place, *chunks[k], weights)
        arrived = swap(away, "gy", far)
        total = keep.astype(F32) + arrived.astype(F32)
        arrived = swap(total[rows:].astype(BF), "gy", near)
        total = total[:rows] + arrived.astype(F32)
        if k:
            total = swap(total.astype(BF), "gx", lambda i, k=k: i ^ k).astype(F32)
        result = result + total
    return result


def gathered_experts(send, stream, routes, gate_up, down_proj):
    columns = lax.axis_size("gy")
    normed = send[:, :D]
    gates = send[:, D : D + EXPERTS].astype(F32) + send[:, D + 64 : D + 64 + EXPERTS].astype(F32)
    gate_weights = jnp.take_along_axis(gates, routes, axis=1)
    row_count = normed.shape[0]
    full_pair = lax.all_gather(gate_up, "gx", axis=0, tiled=True)
    full_down = lax.all_gather(down_proj, "gx", axis=0, tiled=True)
    flat_routes = routes.reshape(row_count * TOP)
    route_hits = (flat_routes[:, None] == jnp.arange(EXPERTS, dtype=jnp.int32)[None, :]).astype(
        jnp.int32
    )
    places = jnp.sum((jnp.cumsum(route_hits, axis=0) - 1) * route_hits, axis=1)
    targets = flat_routes * CAP + places
    repeated = jnp.repeat(normed, TOP, axis=0)
    experts_dev = full_pair.shape[1]
    outgoing_rows = (
        jnp.zeros((EXPERTS * CAP, D), BF)
        .at[targets]
        .set(repeated)
        .reshape(columns, experts_dev, CAP, D)
    )
    arrived = lax.all_to_all(outgoing_rows, "gy", split_axis=0, concat_axis=0, tiled=True)
    gate_pair = jnp.einsum("secd,def->secf", arrived, full_pair, preferred_element_type=F32)
    hidden = (jax.nn.silu(gate_pair[..., :FF]) * gate_pair[..., FF:]).astype(BF)
    expert_rows = jnp.einsum(
        "secf,def->secd", hidden, full_down, preferred_element_type=F32
    ).astype(BF)
    returned = lax.all_to_all(expert_rows, "gy", split_axis=0, concat_axis=0, tiled=True).reshape(
        EXPERTS * CAP, D
    )
    picked = returned[targets].astype(F32).reshape(row_count, TOP, D)
    return stream + jnp.sum(gate_weights[:, :, None] * picked, axis=1)


def gather_out(out_weight):
    columns = lax.axis_size("gy")
    share = out_weight.shape[0] // columns
    mine = lax.dynamic_slice_in_dim(out_weight, lax.axis_index("gy") * share, share, axis=0)
    whole = lax.all_gather(mine, ("gx", "gy"), axis=0, tiled=True)
    return jnp.zeros((1,), jnp.int32), [whole], ((1, whole.shape[0]),)


def swap_out(out_weight):
    planes, columns = lax.axis_size("gx"), lax.axis_size("gy")
    row, column = lax.axis_index("gx"), lax.axis_index("gy")
    depth = out_weight.shape[0]
    share = depth // columns
    mine = lax.dynamic_slice_in_dim(out_weight, column * share, share, axis=0)
    first = jnp.concatenate(
        [swap(mine, "gx", lambda i, k=k: i ^ k) for k in range(1, planes)], axis=0
    )
    second = swap(first, "gy", near)
    third = swap(jnp.concatenate([first, second], axis=0), "gy", far)
    parts = [first, second, third]
    parts = [out_weight] + parts + [swap(part, "gy", lambda j: j ^ 1) for part in parts]
    near_of = lambda j: jnp.where(j % 2 == 0, j ^ 2, j ^ 4)
    far_of = lambda j: jnp.where(j % 2 == 0, j ^ 4, j ^ 2)
    at = [row * depth]
    for own in (column, column ^ 1):
        for source in (own, near_of(own), far_of(own), near_of(far_of(own))):
            at += [(row ^ k) * depth + source * share for k in range(1, planes)]
    one = (planes - 1, share)
    two = (2 * (planes - 1), share)
    return jnp.stack(at).astype(jnp.int32), parts, ((1, depth), one, one, two, one, one, two)


def body(
    queries,
    new_kv,
    cache_pool,
    cache_len,
    local_pages,
    anchor,
    push_pages,
    prefill_attn,
    residual,
    out_weight,
    norm_gain,
    router,
    routes,
    gate_up,
    down_proj,
):
    columns = lax.axis_size("gy")
    slot_count = (MOVED + columns - 2) // (columns - 1)
    pool = cache_pool.reshape(-1, cache_pool.shape[2])
    matches = (anchor[:, None] == jnp.arange(columns, dtype=jnp.int32)[None, :]).astype(jnp.int32)
    earlier = jnp.sum((jnp.cumsum(matches, axis=0) - 1) * matches, axis=1)
    chosen = anchor * slot_count + earlier
    lengths = jnp.stack([cache_len // PAGE, cache_len % PAGE], axis=1).astype(BF)
    ask = jnp.concatenate([queries, jnp.pad(lengths, ((0, 0), (0, LANES - 2)))], axis=1)
    slots = columns * slot_count
    where = (chosen[None, :] == jnp.arange(slots, dtype=jnp.int32)[:, None]).astype(BF)
    outgoing = jnp.dot(where, ask[LOCAL:], preferred_element_type=F32).astype(BF)
    incoming = lax.all_to_all(
        outgoing.reshape(columns, slot_count, WIDE), "gy", split_axis=0, concat_axis=0, tiled=True
    ).reshape(slots, WIDE)
    mix, stat = attend(
        jnp.concatenate([ask[:LOCAL], incoming], axis=0),
        jnp.concatenate([local_pages, push_pages], axis=0),
        pool,
    )
    answers = jnp.concatenate([mix[LOCAL:], stat[LOCAL:]], axis=1).reshape(
        columns, slot_count, WIDE
    )
    back = lax.all_to_all(answers, "gy", split_axis=0, concat_axis=0, tiled=True).reshape(
        slots, WIDE
    )
    planes = lax.axis_size("gx")
    swapped = columns == 8 and planes & (planes - 1) == 0 and gate_up.shape[1] == planes
    attended, stream, send = make_stream(
        chosen,
        queries,
        new_kv,
        mix,
        stat,
        back,
        prefill_attn,
        residual,
        swap_out(out_weight) if swapped else gather_out(out_weight),
        norm_gain.reshape(1, D),
        jnp.pad(router, ((0, 0), (0, LANES - EXPERTS))),
        routes,
    )
    if swapped:
        layer_out = swapped_experts(send, stream, gate_up, down_proj)
    else:
        layer_out = gathered_experts(send, stream, routes, gate_up, down_proj)
    return (attended, layer_out)


def solution(mesh):
    placed = (
        P(("gx", "gy"), None),
        P(("gx", "gy"), None),
        P(("gx", "gy"), None, None),
        P(("gx", "gy")),
        P(("gx", "gy"), None),
        P(("gx", "gy")),
        P(("gx", "gy"), None),
        P(("gx", "gy"), None),
        P(("gx", "gy"), None),
        P("gx", None),
        P(),
        P(),
        P(("gx", "gy"), None),
        P("gx", "gy", None),
        P("gx", "gy", None),
    )
    return jax.shard_map(
        body,
        mesh=mesh,
        in_specs=placed,
        out_specs=(P(("gx", "gy"), None), P(("gx", "gy"), None)),
        check_vma=False,
    )
```

```python
import functools
import math

import jax
import jax.numpy as jnp
from jax import lax
from jax.experimental import pallas as pl
from jax.experimental.pallas import tpu as pltpu
from jax.sharding import PartitionSpec as P

D = 1536
HEADS = 24
KV_HEADS = 8
HEAD = 64
GROUP = HEADS // KV_HEADS
EXPERTS = 32
FF = 512
TOP = 8
PAGE = 16
MAXLEN = 512
NPAGE = 32
R_DEV = 16
LOCAL = 8
MOVED = 8
CAP = 48
LANES = 128
WIDE = D + LANES
PAIRS = KV_HEADS // 2
BIG = 1e30
HIDDEN_COST = 6 * 10**9
DOWN_COST = 10**6
BF = jnp.bfloat16
F32 = jnp.float32


def vmem():
    return pl.BlockSpec(memory_space=pltpu.VMEM)


def smem():
    return pl.BlockSpec(memory_space=pltpu.SMEM)


def cost(flops, moved):
    return pl.CostEstimate(flops=flops, bytes_accessed=moved, transcendentals=0)


def attend_kernel(
    me_ref, own_ref, asks_ref, table_ref, key_ref, value_ref, mix_ref, stat_ref, counts, ask_ref
):
    step = pl.program_id(0)
    slots = table_ref.shape[0]
    pages = counts.shape[1] // PAGE

    @pl.when(step == 0)
    def _():
        away = slots - LOCAL
        code = asks_ref[:, D:].astype(jnp.int32)
        sender = lax.broadcasted_iota(jnp.int32, (code.shape[0], 1), 0) // MOVED
        each = away // (code.shape[0] // MOVED)
        slot = jnp.where(code[:, 2:3] == me_ref[0], sender * each + code[:, 3:4], -1)
        take = lax.broadcasted_iota(jnp.int32, (code.shape[0], away), 1) == slot
        take = jnp.where(take, 1.0, 0.0).astype(BF)
        ask_ref[:LOCAL, :] = own_ref[...].astype(F32)
        ask_ref[LOCAL:, :] = lax.dot_general(
            take, asks_ref[...], (((0,), (0,)), ((), ())), preferred_element_type=F32
        )
        lengths = ask_ref[:, D:].astype(jnp.int32)
        full, rest = lengths[:, 0:1], lengths[:, 1:2]
        table = table_ref[...]
        page = lax.broadcasted_iota(jnp.int32, (slots, pages), 1)
        whole = jnp.zeros((slots, pages), F32)
        part = jnp.zeros((slots, pages), F32)
        for p in range(NPAGE):
            hit = table[:, p : p + 1] == page
            whole += jnp.where(hit & (full > p), 1.0, 0.0)
            part += jnp.where(hit & (full == p), 1.0, 0.0)
        row = lax.broadcasted_iota(jnp.int32, (pages, pages * PAGE), 1)
        spread = jnp.where(
            row // PAGE == lax.broadcasted_iota(jnp.int32, (pages, pages * PAGE), 0), 1.0, 0.0
        ).astype(BF)
        whole = jnp.dot(whole.astype(BF), spread, preferred_element_type=F32)
        part = jnp.dot(part.astype(BF), spread, preferred_element_type=F32)
        place = lax.broadcasted_iota(jnp.int32, (slots, pages * PAGE), 1) % PAGE
        counts[...] = whole + jnp.where(place < rest, part, 0.0)

    lane = lax.broadcasted_iota(jnp.int32, (slots, LANES), 1)
    rows = []
    for j in range(2 * GROUP):
        side, chunk, half = j // GROUP, j // 2, j % 2
        at = pl.multiple_of(step * (2 * GROUP * HEAD) + chunk * LANES, LANES)
        part = ask_ref[:, pl.ds(at, LANES)] * (1.0 / math.sqrt(HEAD))
        if side != half:
            part = pltpu.roll(part, HEAD, 1)
        rows.append(jnp.where((lane < HEAD) == (side == 0), part, 0.0).astype(BF))
    heads = jnp.concatenate(rows, axis=0)
    scores = lax.dot_general(
        heads, key_ref[...], (((1,), (1,)), ((), ())), preferred_element_type=F32
    )
    count = jnp.concatenate([counts[...]] * (2 * GROUP), axis=0)
    masked = jnp.where(count > 0.0, scores, -BIG)
    highest = jnp.max(masked, axis=1, keepdims=True)
    expos = jnp.exp(masked - highest)
    totals = jnp.sum(expos * count, axis=1, keepdims=True)
    weights = (expos.astype(BF).astype(F32) * count).astype(BF)
    mixture = jnp.dot(weights, value_ref[...], preferred_element_type=F32)

    @pl.when(step == 0)
    def _():
        stat_ref[...] = jnp.zeros_like(stat_ref)

    stat = stat_ref[...]
    for j in range(2 * GROUP):
        head = step * 2 * GROUP + j
        take = slice(j * slots, (j + 1) * slots)
        stat = jnp.where(lane == head, highest[take], stat)
        stat = jnp.where(lane == head + 64, totals[take], stat)
    stat_ref[...] = stat
    for chunk in range(GROUP):
        halves = []
        for half in range(2):
            j = 2 * chunk + half
            part = mixture[j * slots : (j + 1) * slots]
            if j // GROUP != half:
                part = pltpu.roll(part, HEAD, 1)
            halves.append(part)
        mix_ref[:, chunk * LANES : (chunk + 1) * LANES] = jnp.where(lane < HEAD, halves[0], halves[1])


def attend(me, own, asks, table, pool):
    slots = table.shape[0]
    tokens = pool.shape[0]
    width = 2 * GROUP * HEAD
    return pl.pallas_call(
        attend_kernel,
        grid=(PAIRS,),
        in_specs=[
            smem(),
            pl.BlockSpec(own.shape, lambda s: (0, 0)),
            pl.BlockSpec(asks.shape, lambda s: (0, 0)),
            pl.BlockSpec((slots, NPAGE), lambda s: (0, 0)),
            pl.BlockSpec((tokens, LANES), lambda s: (0, s)),
            pl.BlockSpec((tokens, LANES), lambda s: (0, PAIRS + s)),
        ],
        out_specs=[
            pl.BlockSpec((slots, width), lambda s: (0, s)),
            pl.BlockSpec((slots, LANES), lambda s: (0, 0)),
        ],
        out_shape=[
            jax.ShapeDtypeStruct((slots, D), F32),
            jax.ShapeDtypeStruct((slots, LANES), F32),
        ],
        scratch_shapes=[pltpu.VMEM((slots, tokens), F32), pltpu.VMEM((slots, WIDE), F32)],
        compiler_params=pltpu.CompilerParams(vmem_limit_bytes=48 * 1024 * 1024),
        cost_estimate=cost(7 * 10**9, 10**5),
        name="attend",
    )(me, own, asks, table, pool, pool)


def stream_kernel(
    pieces, chosen_ref, at_ref, query_ref, fresh_ref, mix_ref, stat_ref, back_ref, prefill_ref,
    residual_ref, gain_ref, router_ref, routes_ref, *rest
):
    parts, rest = rest[: len(pieces)], rest[len(pieces) :]
    attended_ref, stream_ref, send_ref, tokens, out_ref, sems = rest
    copies = []
    for part, (blocks, rows) in zip(parts, pieces):
        for block in range(blocks):
            n = len(copies)
            at = pl.multiple_of(at_ref[n], 16)
            copy = pltpu.make_async_copy(
                part.at[pl.ds(block * rows, rows)], out_ref.at[pl.ds(at, rows)], sems.at[n]
            )
            copy.start()
            copies.append(copy)
    count = query_ref.shape[0]
    lane = lax.broadcasted_iota(jnp.int32, (count, LANES), 1)
    low = lane < HEAD
    picked = [back_ref[pl.ds(chosen_ref[m], 1), :] for m in range(MOVED)]
    picked = jnp.concatenate(picked, axis=0)
    mix = jnp.concatenate([mix_ref[:LOCAL, :], picked[:, :D]], axis=0)
    stat = jnp.concatenate([stat_ref[:LOCAL, :], picked[:, D:]], axis=0)
    fresh = fresh_ref[...].astype(F32)

    def spread(first, second, base):
        sides = []
        for half, head in enumerate((first, second)):
            part = fresh[:, base + head // 2 * LANES : base + head // 2 * LANES + LANES]
            sides.append(pltpu.roll(part, HEAD, 1) if head % 2 != half else part)
        return jnp.where(low, sides[0], sides[1])

    def both(first, second):
        return jnp.where(low, first, second)

    for chunk in range(HEADS // 2):
        first, second = 2 * chunk, 2 * chunk + 1
        span = slice(chunk * LANES, (chunk + 1) * LANES)
        keys = spread(first // GROUP, second // GROUP, 0)
        values = spread(first // GROUP, second // GROUP, KV_HEADS * HEAD)
        product = query_ref[:, span].astype(F32) * keys
        scale = 1.0 / math.sqrt(HEAD)
        own = both(
            jnp.sum(jnp.where(low, product, 0.0), axis=1, keepdims=True) * scale,
            jnp.sum(jnp.where(low, 0.0, product), axis=1, keepdims=True) * scale,
        )
        cache_max = both(stat[:, first : first + 1], stat[:, second : second + 1])
        total = both(stat[:, 64 + first : 65 + first], stat[:, 64 + second : 65 + second])
        highest = jnp.maximum(cache_max, own)
        old = jnp.exp(cache_max - highest)
        new = jnp.exp(own - highest)
        output = (old * mix[:, span] + new * values) / (old * total + new)
        tokens[:count, span] = output.astype(BF)
    attended_ref[...] = tokens[:count, :]
    tokens[count:, :] = prefill_ref[...]
    for copy in copies:
        copy.wait()
    stream = residual_ref[...].astype(F32) + jnp.dot(
        tokens[...], out_ref[...], preferred_element_type=F32
    )
    stream_ref[...] = stream
    normed = (
        stream
        * lax.rsqrt(jnp.mean(stream * stream, axis=1, keepdims=True) + 1e-06)
        * gain_ref[...].astype(F32)
    ).astype(BF)
    send_ref[:, :D] = normed
    logits = jnp.dot(normed, router_ref[...], preferred_element_type=F32)
    rows = logits.shape[0]
    expert = lax.broadcasted_iota(jnp.int32, (rows, LANES), 1)
    routes = routes_ref[...]
    named = expert == routes[:, 0:1]
    for k in range(1, TOP):
        named = named | (expert == routes[:, k : k + 1])
    masked = jnp.where(named, logits, -BIG)
    expos = jnp.where(named, jnp.exp(masked - jnp.max(masked, axis=1, keepdims=True)), 0.0)
    gates = expos / jnp.sum(expos, axis=1, keepdims=True)
    coarse = gates.astype(BF).astype(F32)
    fine = pltpu.roll(gates - coarse, 64, 1)
    send_ref[:, D:] = jnp.where(expert < 64, coarse, fine).astype(BF)


def make_stream(
    chosen, queries, fresh, mix, stat, back, prefill, residual, out_parts, gain, router, routes
):
    rows = residual.shape[0]
    count = queries.shape[0]
    at, parts, pieces = out_parts
    return pl.pallas_call(
        functools.partial(stream_kernel, pieces),
        in_specs=[smem()] * 2 + [vmem()] * 10 + [pl.BlockSpec(memory_space=pl.ANY)] * len(parts),
        out_specs=[vmem()] * 3,
        out_shape=[
            jax.ShapeDtypeStruct((count, D), BF),
            jax.ShapeDtypeStruct((rows, D), F32),
            jax.ShapeDtypeStruct((rows, WIDE), BF),
        ],
        scratch_shapes=[
            pltpu.VMEM((rows, D), BF),
            pltpu.VMEM((D, D), BF),
            pltpu.SemaphoreType.DMA((sum(blocks for blocks, _ in pieces),)),
        ],
        compiler_params=pltpu.CompilerParams(vmem_limit_bytes=48 * 1024 * 1024),
        cost_estimate=cost(8 * 10**9, 10**5),
        name="stream",
    )(chosen, at, queries, fresh, mix, stat, back, prefill, residual, gain, router, routes, *parts)


def hidden_kernel(place_ref, first_ref, second_ref, mine_ref, other_ref, hidden_ref, share_ref, rows_ref):
    rows = first_ref.shape[0]
    rows_ref[:rows, :] = first_ref[...]
    rows_ref[rows:, :] = second_ref[...]
    gates = rows_ref[:, D:].astype(F32)
    gates = gates + pltpu.roll(gates, 64, 1)
    lane = lax.broadcasted_iota(jnp.int32, gates.shape, 1)
    shares = []
    for side, held_ref in enumerate((mine_ref, other_ref)):
        named = jnp.where(lane == place_ref[side], gates, 0.0)
        shares.append(jnp.sum(named, axis=1, keepdims=True))
        pair = jnp.dot(rows_ref[:, :D], held_ref[...], preferred_element_type=F32)
        gate = pair[:, :FF]
        hidden_ref[:, side * FF : (side + 1) * FF] = (
            gate / (1.0 + jnp.exp(-gate)) * pair[:, FF:]
        ).astype(BF)
    share_ref[...] = jnp.where(lane == 0, shares[0], shares[1])


def make_hidden(place, first, second, mine, other):
    rows = 2 * first.shape[0]
    return pl.pallas_call(
        hidden_kernel,
        in_specs=[smem()] + [vmem()] * 4,
        out_specs=[vmem()] * 2,
        out_shape=[
            jax.ShapeDtypeStruct((rows, 2 * FF), BF),
            jax.ShapeDtypeStruct((rows, LANES), F32),
        ],
        scratch_shapes=[pltpu.VMEM((rows, WIDE), BF)],
        compiler_params=pltpu.CompilerParams(vmem_limit_bytes=28 * 1024 * 1024),
        cost_estimate=cost(HIDDEN_COST, 10**5),
        name="hidden",
    )(place, first, second, mine, other)


def down_kernel(hidden_ref, share_ref, mine_ref, other_ref, keep_ref, away_ref):
    total = None
    for side, held_ref in enumerate((mine_ref, other_ref)):
        made = lax.dot_general(
            hidden_ref[:, side * FF : (side + 1) * FF],
            held_ref[...],
            (((1,), (1,)), ((), ())),
            preferred_element_type=F32,
        )
        made = share_ref[:, side : side + 1] * made.astype(BF).astype(F32)
        total = made if total is None else total + made
    rows = keep_ref.shape[0]
    keep_ref[...] = total[:rows].astype(BF)
    away_ref[...] = total[rows:].astype(BF)


def make_down(hidden, share, mine, other):
    rows = hidden.shape[0]
    return pl.pallas_call(
        down_kernel,
        in_specs=[vmem()] * 4,
        out_specs=[vmem()] * 2,
        out_shape=[jax.ShapeDtypeStruct((rows // 2, D), BF)] * 2,
        compiler_params=pltpu.CompilerParams(vmem_limit_bytes=28 * 1024 * 1024),
        cost_estimate=cost(DOWN_COST, 10**5),
        name="down",
    )(hidden, share, mine, other)


def pack_kernel(gate_ref, down_ref, pair_out, down_out):
    depth, experts = gate_ref.shape[:2]
    step = 16

    @pl.loop(0, depth // step)
    def _(n):
        at = pl.ds(pl.multiple_of(n * step, step), step)
        gate = gate_ref[at]
        down = down_ref[at]
        for e in range(experts):
            pair_out[e, at, :] = gate[:, e, :]
            down_out[e, at, :] = down[:, e, :]


def pack_experts(gate_up, down_proj):
    depth, experts = gate_up.shape[:2]
    return pl.pallas_call(
        pack_kernel,
        in_specs=[vmem()] * 2,
        out_specs=[vmem()] * 2,
        out_shape=[jax.ShapeDtypeStruct((experts, depth, n * FF), BF) for n in (2, 1)],
        compiler_params=pltpu.CompilerParams(vmem_limit_bytes=32 * 1024 * 1024),
        cost_estimate=cost(7 * 10**9, 10**5),
        name="pack",
    )(gate_up, down_proj)


def swap(x, axis, how):
    return lax.ppermute(x, axis, [(i, how(i)) for i in range(lax.axis_size(axis))])


def near(j):
    return j ^ (2 if j % 2 == 0 else 4)


def beside(j):
    return j ^ 1


def far(j):
    return j ^ (4 if j % 2 == 0 else 2)


def exchange(packed):
    whole = lax.all_to_all(packed, "gx", split_axis=0, concat_axis=0, tiled=True)
    return whole.reshape(-1, packed.shape[2])


def after(x, *others):
    return lax.optimization_barrier((x, others))[0]


def swapped_experts(send, stream, pair, down):
    planes = lax.axis_size("gx")
    row, column = lax.axis_index("gx"), lax.axis_index("gy")
    place = jnp.stack([column * planes + row, beside(column) * planes + row]).astype(jnp.int32)
    rows = send.shape[0]
    across = lambda x, k: swap(x, "gx", lambda i: i ^ k)
    firsts = [jnp.concatenate([send, swap(send, "gy", near)], axis=0)]
    moved = [across(after(send, firsts[0]) if k == 1 else send, k) for k in range(1, planes)]
    other_pair = swap(after(pair, firsts[0]), "gy", beside)
    down = exchange(after(down, *moved))
    firsts += [jnp.concatenate([mine, swap(mine, "gy", near)], axis=0) for mine in moved]
    chunks = [[first, swap(first, "gy", far)] for first in firsts]
    hidden = []
    for chunk in chunks:
        chunk = after(chunk, *hidden[-1:])
        hidden.append(make_hidden(place, *chunk, pair, other_pair))
    down, hidden = lax.optimization_barrier((down, hidden))
    other_down = swap(down, "gy", beside)
    order = list(reversed(range(planes)))
    made, last = {}, ()
    for k in order:
        made[k] = make_down(*after(hidden[k], *last), down, other_down)
        last = made[k]
    arrived = {k: swap(made[k][1], "gy", far) for k in order}
    total, ends = {}, {}
    for n in range(planes + 2):
        if n < planes:
            k = order[n]
            keep, came = after((made[k][0], arrived[k]), *last)
            total[k] = keep.astype(F32) + came.astype(F32)
            send_on = total[k][rows:].astype(BF)
            last = (send_on,)
            ends[k] = swap(send_on, "gy", near)
        if 1 <= n <= planes:
            k = order[n - 1]
            keep, came = after((total[k][:rows], ends[k]), *last)
            total[k] = keep + came.astype(F32)
            if k:
                send_on = total[k].astype(BF)
                last = (send_on,)
                ends[k] = across(send_on, k)
    result = stream + total[0]
    for k in range(1, planes):
        result = result + ends[k].astype(F32)
    return result


def gathered_experts(send, stream, routes, gate_up, down_proj):
    columns = lax.axis_size("gy")
    normed = send[:, :D]
    gates = send[:, D : D + EXPERTS].astype(F32) + send[:, D + 64 : D + 64 + EXPERTS].astype(F32)
    gate_weights = jnp.take_along_axis(gates, routes, axis=1)
    row_count = normed.shape[0]
    full_pair = lax.all_gather(gate_up, "gx", axis=0, tiled=True)
    full_down = lax.all_gather(down_proj, "gx", axis=0, tiled=True)
    flat_routes = routes.reshape(row_count * TOP)
    route_hits = (flat_routes[:, None] == jnp.arange(EXPERTS, dtype=jnp.int32)[None, :]).astype(
        jnp.int32
    )
    places = jnp.sum((jnp.cumsum(route_hits, axis=0) - 1) * route_hits, axis=1)
    targets = flat_routes * CAP + places
    repeated = jnp.repeat(normed, TOP, axis=0)
    experts_dev = full_pair.shape[1]
    outgoing_rows = (
        jnp.zeros((EXPERTS * CAP, D), BF)
        .at[targets]
        .set(repeated)
        .reshape(columns, experts_dev, CAP, D)
    )
    arrived = lax.all_to_all(outgoing_rows, "gy", split_axis=0, concat_axis=0, tiled=True)
    gate_pair = jnp.einsum("secd,def->secf", arrived, full_pair, preferred_element_type=F32)
    hidden = (jax.nn.silu(gate_pair[..., :FF]) * gate_pair[..., FF:]).astype(BF)
    expert_rows = jnp.einsum(
        "secf,def->secd", hidden, full_down, preferred_element_type=F32
    ).astype(BF)
    returned = lax.all_to_all(expert_rows, "gy", split_axis=0, concat_axis=0, tiled=True).reshape(
        EXPERTS * CAP, D
    )
    picked = returned[targets].astype(F32).reshape(row_count, TOP, D)
    return stream + jnp.sum(gate_weights[:, :, None] * picked, axis=1)


def gather_out(out_weight):
    columns = lax.axis_size("gy")
    share = out_weight.shape[0] // columns
    mine = lax.dynamic_slice_in_dim(out_weight, lax.axis_index("gy") * share, share, axis=0)
    whole = lax.all_gather(mine, ("gx", "gy"), axis=0, tiled=True)
    return jnp.zeros((1,), jnp.int32), [whole], ((1, whole.shape[0]),)


def start_out(out_weight):
    planes, columns = lax.axis_size("gx"), lax.axis_size("gy")
    share = out_weight.shape[0] // columns
    mine = lax.dynamic_slice_in_dim(out_weight, lax.axis_index("gy") * share, share, axis=0)
    return [swap(mine, "gx", lambda i, k=k: i ^ k) for k in range(1, planes)]


def swap_out(out_weight, first):
    planes, columns = lax.axis_size("gx"), lax.axis_size("gy")
    row, column = lax.axis_index("gx"), lax.axis_index("gy")
    depth = out_weight.shape[0]
    share = depth // columns
    second = swap(first, "gy", near)
    third = swap(jnp.concatenate([first, second], axis=0), "gy", far)
    parts = [first, second, third]
    parts = [out_weight] + parts + [swap(part, "gy", beside) for part in parts]
    near_of = lambda j: jnp.where(j % 2 == 0, j ^ 2, j ^ 4)
    far_of = lambda j: jnp.where(j % 2 == 0, j ^ 4, j ^ 2)
    at = [row * depth]
    for own in (column, column ^ 1):
        for source in (own, near_of(own), far_of(own), near_of(far_of(own))):
            at += [(row ^ k) * depth + source * share for k in range(1, planes)]
    one = (planes - 1, share)
    two = (2 * (planes - 1), share)
    return jnp.stack(at).astype(jnp.int32), parts, ((1, depth), one, one, two, one, one, two)


def body(
    queries,
    new_kv,
    cache_pool,
    cache_len,
    local_pages,
    anchor,
    push_pages,
    prefill_attn,
    residual,
    out_weight,
    norm_gain,
    router,
    routes,
    gate_up,
    down_proj,
):
    columns = lax.axis_size("gy")
    slot_count = (MOVED + columns - 2) // (columns - 1)
    pool = cache_pool.reshape(-1, cache_pool.shape[2])
    matches = (anchor[:, None] == jnp.arange(columns, dtype=jnp.int32)[None, :]).astype(jnp.int32)
    earlier = jnp.sum((jnp.cumsum(matches, axis=0) - 1) * matches, axis=1)
    slots = columns * slot_count
    column = lax.axis_index("gy")
    chosen = anchor * slots + column * slot_count + earlier
    extra = jnp.stack([cache_len[LOCAL:] // PAGE, cache_len[LOCAL:] % PAGE, anchor, earlier], axis=1)
    extra = jnp.pad(extra.astype(BF), ((0, 0), (0, LANES - 4)))
    asks = lax.all_gather(
        jnp.concatenate([queries[LOCAL:], extra], axis=1), "gy", axis=0, tiled=True
    )
    extra = jnp.stack([cache_len[:LOCAL] // PAGE, cache_len[:LOCAL] % PAGE], axis=1)
    extra = jnp.pad(extra.astype(BF), ((0, 0), (0, LANES - 2)))
    own = jnp.concatenate([queries[:LOCAL], extra], axis=1)
    planes = lax.axis_size("gx")
    swapped = columns == 8 and planes & (planes - 1) == 0 and gate_up.shape[1] == planes
    if swapped:
        out_parts = start_out(out_weight)
        pair, down = pack_experts(gate_up, down_proj)
        out_parts, pair, down = lax.optimization_barrier((out_parts, pair, down))
        pair = exchange(pair)
        out_parts = swap_out(out_weight, jnp.concatenate(out_parts, axis=0))
    else:
        out_parts = gather_out(out_weight)
    mix, stat = attend(
        column.astype(jnp.int32).reshape(1),
        own,
        asks,
        jnp.concatenate([local_pages, push_pages], axis=0),
        pool,
    )
    answers = jnp.concatenate([mix[LOCAL:], stat[LOCAL:]], axis=1)
    back = lax.all_gather(answers, "gy", axis=0, tiled=True)
    attended, stream, send = make_stream(
        chosen,
        queries,
        new_kv,
        mix,
        stat,
        back,
        prefill_attn,
        residual,
        out_parts,
        norm_gain.reshape(1, D),
        jnp.pad(router, ((0, 0), (0, LANES - EXPERTS))),
        routes,
    )
    if swapped:
        layer_out = swapped_experts(send, stream, pair, down)
    else:
        layer_out = gathered_experts(send, stream, routes, gate_up, down_proj)
    return (attended, layer_out)


def solution(mesh):
    placed = (
        P(("gx", "gy"), None),
        P(("gx", "gy"), None),
        P(("gx", "gy"), None, None),
        P(("gx", "gy")),
        P(("gx", "gy"), None),
        P(("gx", "gy")),
        P(("gx", "gy"), None),
        P(("gx", "gy"), None),
        P(("gx", "gy"), None),
        P("gx", None),
        P(),
        P(),
        P(("gx", "gy"), None),
        P("gx", "gy", None),
        P("gx", "gy", None),
    )
    return jax.shard_map(
        body,
        mesh=mesh,
        in_specs=placed,
        out_specs=(P(("gx", "gy"), None), P(("gx", "gy"), None)),
        check_vma=False,
    )
```

```python
import functools
import math

import jax
import jax.numpy as jnp
from jax import lax
from jax.experimental import pallas as pl
from jax.experimental.pallas import tpu as pltpu
from jax.sharding import PartitionSpec as P

D = 1536
HEADS = 24
KV_HEADS = 8
HEAD = 64
GROUP = HEADS // KV_HEADS
EXPERTS = 32
FF = 512
TOP = 8
PAGE = 16
MAXLEN = 512
NPAGE = 32
R_DEV = 16
LOCAL = 8
MOVED = 8
CAP = 48
LANES = 128
WIDE = D + LANES
PAIRS = KV_HEADS // 2
BIG = 1e30
HIDDEN_COST = 10**6
DOWN_COST = 10**6
VMEM_LIMIT = 60 * 1024 * 1024
BF = jnp.bfloat16
F32 = jnp.float32


def vmem():
    return pl.BlockSpec(memory_space=pltpu.VMEM)


def smem():
    return pl.BlockSpec(memory_space=pltpu.SMEM)


def anywhere():
    return pl.BlockSpec(memory_space=pl.ANY)


def cost(flops, moved):
    return pl.CostEstimate(flops=flops, bytes_accessed=moved, transcendentals=0)


def attend_kernel(
    me_ref, own_ref, asks_ref, table_ref, key_ref, value_ref, here_ref, reply_ref, counts, ask_ref
):
    step = pl.program_id(0)
    slots = table_ref.shape[0]
    pages = counts.shape[1] // PAGE

    @pl.when(step == 0)
    def _():
        away = slots - LOCAL
        code = asks_ref[:, D:].astype(jnp.int32)
        sender = lax.broadcasted_iota(jnp.int32, (code.shape[0], 1), 0) // MOVED
        each = away // (code.shape[0] // MOVED)
        slot = jnp.where(code[:, 2:3] == me_ref[0], sender * each + code[:, 3:4], -1)
        take = lax.broadcasted_iota(jnp.int32, (code.shape[0], away), 1) == slot
        take = jnp.where(take, 1.0, 0.0).astype(BF)
        ask_ref[:LOCAL, :] = own_ref[...].astype(F32)
        ask_ref[LOCAL:, :] = lax.dot_general(
            take, asks_ref[...], (((0,), (0,)), ((), ())), preferred_element_type=F32
        )
        lengths = ask_ref[:, D:].astype(jnp.int32)
        full, rest = lengths[:, 0:1], lengths[:, 1:2]
        table = table_ref[...]
        page = lax.broadcasted_iota(jnp.int32, (slots, pages), 1)
        whole = jnp.zeros((slots, pages), F32)
        part = jnp.zeros((slots, pages), F32)
        for p in range(NPAGE):
            hit = table[:, p : p + 1] == page
            whole += jnp.where(hit & (full > p), 1.0, 0.0)
            part += jnp.where(hit & (full == p), 1.0, 0.0)
        row = lax.broadcasted_iota(jnp.int32, (pages, pages * PAGE), 1)
        spread = jnp.where(
            row // PAGE == lax.broadcasted_iota(jnp.int32, (pages, pages * PAGE), 0), 1.0, 0.0
        ).astype(BF)
        whole = jnp.dot(whole.astype(BF), spread, preferred_element_type=F32)
        part = jnp.dot(part.astype(BF), spread, preferred_element_type=F32)
        place = lax.broadcasted_iota(jnp.int32, (slots, pages * PAGE), 1) % PAGE
        counts[...] = whole + jnp.where(place < rest, part, 0.0)

    lane = lax.broadcasted_iota(jnp.int32, (slots, LANES), 1)
    rows = []
    for j in range(2 * GROUP):
        side, chunk, half = j // GROUP, j // 2, j % 2
        at = pl.multiple_of(step * (2 * GROUP * HEAD) + chunk * LANES, LANES)
        part = ask_ref[:, pl.ds(at, LANES)] * (1.0 / math.sqrt(HEAD))
        if side != half:
            part = pltpu.roll(part, HEAD, 1)
        rows.append(jnp.where((lane < HEAD) == (side == 0), part, 0.0).astype(BF))
    heads = jnp.concatenate(rows, axis=0)
    scores = lax.dot_general(
        heads, key_ref[...], (((1,), (1,)), ((), ())), preferred_element_type=F32
    )
    count = jnp.concatenate([counts[...]] * (2 * GROUP), axis=0)
    masked = jnp.where(count > 0.0, scores, -BIG)
    highest = jnp.max(masked, axis=1, keepdims=True)
    expos = jnp.exp(masked - highest)
    totals = jnp.sum(expos * count, axis=1, keepdims=True)
    weights = (expos.astype(BF).astype(F32) * count).astype(BF)
    mixture = jnp.dot(weights, value_ref[...], preferred_element_type=F32)

    def put(at, value):
        here_ref[:, pl.ds(at, LANES)] = value[:LOCAL]
        reply_ref[:, pl.ds(at, LANES)] = value[LOCAL:]

    @pl.when(step == 0)
    def _():
        put(D, jnp.zeros((slots, LANES), F32))

    stat = jnp.concatenate([here_ref[:, D:], reply_ref[:, D:]], axis=0)
    for j in range(2 * GROUP):
        head = step * 2 * GROUP + j
        take = slice(j * slots, (j + 1) * slots)
        stat = jnp.where(lane == head, highest[take], stat)
        stat = jnp.where(lane == head + 64, totals[take], stat)
    put(D, stat)
    for chunk in range(GROUP):
        halves = []
        for half in range(2):
            j = 2 * chunk + half
            part = mixture[j * slots : (j + 1) * slots]
            if j // GROUP != half:
                part = pltpu.roll(part, HEAD, 1)
            halves.append(part)
        at = pl.multiple_of(step * (2 * GROUP * HEAD) + chunk * LANES, LANES)
        put(at, jnp.where(lane < HEAD, halves[0], halves[1]))


def attend(me, own, asks, table, pool):
    slots = table.shape[0]
    tokens = pool.shape[0]
    return pl.pallas_call(
        attend_kernel,
        grid=(PAIRS,),
        in_specs=[
            smem(),
            pl.BlockSpec(own.shape, lambda s: (0, 0)),
            pl.BlockSpec(asks.shape, lambda s: (0, 0)),
            pl.BlockSpec((slots, NPAGE), lambda s: (0, 0)),
            pl.BlockSpec((tokens, LANES), lambda s: (0, s)),
            pl.BlockSpec((tokens, LANES), lambda s: (0, PAIRS + s)),
        ],
        out_specs=[
            pl.BlockSpec((LOCAL, WIDE), lambda s: (0, 0)),
            pl.BlockSpec((slots - LOCAL, WIDE), lambda s: (0, 0)),
        ],
        out_shape=[
            jax.ShapeDtypeStruct((LOCAL, WIDE), F32),
            jax.ShapeDtypeStruct((slots - LOCAL, WIDE), F32),
        ],
        scratch_shapes=[pltpu.VMEM((slots, tokens), F32), pltpu.VMEM((slots, WIDE), F32)],
        compiler_params=pltpu.CompilerParams(vmem_limit_bytes=VMEM_LIMIT),
        cost_estimate=cost(7 * 10**9, 10**5),
        name="attend",
    )(me, own, asks, table, pool, pool)


def stream_kernel(
    pieces, chosen_ref, at_ref, query_ref, fresh_ref, here_ref, back_ref, prefill_ref,
    residual_ref, gain_ref, router_ref, routes_ref, *rest
):
    parts, rest = rest[: len(pieces)], rest[len(pieces) :]
    attended_ref, stream_ref, send_ref, tokens, out_ref, sems = rest
    copies = []
    for part, (blocks, rows) in zip(parts, pieces):
        for block in range(blocks):
            n = len(copies)
            at = pl.multiple_of(at_ref[n], 16)
            copy = pltpu.make_async_copy(
                part.at[pl.ds(block * rows, rows)], out_ref.at[pl.ds(at, rows)], sems.at[n]
            )
            copy.start()
            copies.append(copy)
    count = query_ref.shape[0]
    lane = lax.broadcasted_iota(jnp.int32, (count, LANES), 1)
    low = lane < HEAD
    picked = [back_ref[pl.ds(chosen_ref[m], 1), :] for m in range(MOVED)]
    picked = jnp.concatenate(picked, axis=0)
    mix = jnp.concatenate([here_ref[:, :D], picked[:, :D]], axis=0)
    stat = jnp.concatenate([here_ref[:, D:], picked[:, D:]], axis=0)
    fresh = fresh_ref[...].astype(F32)

    def spread(first, second, base):
        sides = []
        for half, head in enumerate((first, second)):
            part = fresh[:, base + head // 2 * LANES : base + head // 2 * LANES + LANES]
            sides.append(pltpu.roll(part, HEAD, 1) if head % 2 != half else part)
        return jnp.where(low, sides[0], sides[1])

    def both(first, second):
        return jnp.where(low, first, second)

    for chunk in range(HEADS // 2):
        first, second = 2 * chunk, 2 * chunk + 1
        span = slice(chunk * LANES, (chunk + 1) * LANES)
        keys = spread(first // GROUP, second // GROUP, 0)
        values = spread(first // GROUP, second // GROUP, KV_HEADS * HEAD)
        product = query_ref[:, span].astype(F32) * keys
        scale = 1.0 / math.sqrt(HEAD)
        own = both(
            jnp.sum(jnp.where(low, product, 0.0), axis=1, keepdims=True) * scale,
            jnp.sum(jnp.where(low, 0.0, product), axis=1, keepdims=True) * scale,
        )
        cache_max = both(stat[:, first : first + 1], stat[:, second : second + 1])
        total = both(stat[:, 64 + first : 65 + first], stat[:, 64 + second : 65 + second])
        highest = jnp.maximum(cache_max, own)
        old = jnp.exp(cache_max - highest)
        new = jnp.exp(own - highest)
        output = (old * mix[:, span] + new * values) / (old * total + new)
        tokens[:count, span] = output.astype(BF)
    attended_ref[...] = tokens[:count, :]
    tokens[count:, :] = prefill_ref[...]
    for copy in copies:
        copy.wait()
    stream = residual_ref[...].astype(F32) + jnp.dot(
        tokens[...], out_ref[...], preferred_element_type=F32
    )
    stream_ref[...] = stream
    normed = (
        stream
        * lax.rsqrt(jnp.mean(stream * stream, axis=1, keepdims=True) + 1e-06)
        * gain_ref[...].astype(F32)
    ).astype(BF)
    send_ref[:, :D] = normed
    logits = jnp.dot(normed, router_ref[...], preferred_element_type=F32)
    rows = logits.shape[0]
    expert = lax.broadcasted_iota(jnp.int32, (rows, LANES), 1)
    routes = routes_ref[...]
    named = expert == routes[:, 0:1]
    for k in range(1, TOP):
        named = named | (expert == routes[:, k : k + 1])
    masked = jnp.where(named, logits, -BIG)
    expos = jnp.where(named, jnp.exp(masked - jnp.max(masked, axis=1, keepdims=True)), 0.0)
    gates = expos / jnp.sum(expos, axis=1, keepdims=True)
    coarse = gates.astype(BF).astype(F32)
    fine = pltpu.roll(gates - coarse, 64, 1)
    send_ref[:, D:] = jnp.where(expert < 64, coarse, fine).astype(BF)


def make_stream(
    chosen, queries, fresh, here, back, prefill, residual, out_parts, gain, router, routes
):
    rows = residual.shape[0]
    count = queries.shape[0]
    at, parts, pieces, _ = out_parts
    return pl.pallas_call(
        functools.partial(stream_kernel, pieces),
        in_specs=[smem()] * 2 + [vmem()] * 9 + [pl.BlockSpec(memory_space=pltpu.HBM)] * len(parts),
        out_specs=[vmem()] * 3,
        out_shape=[
            jax.ShapeDtypeStruct((count, D), BF),
            jax.ShapeDtypeStruct((rows, D), F32),
            jax.ShapeDtypeStruct((rows, WIDE), BF),
        ],
        scratch_shapes=[
            pltpu.VMEM((rows, D), BF),
            pltpu.VMEM((D, D), BF),
            pltpu.SemaphoreType.DMA((sum(blocks for blocks, _ in pieces),)),
        ],
        compiler_params=pltpu.CompilerParams(vmem_limit_bytes=VMEM_LIMIT),
        cost_estimate=cost(8 * 10**9, 10**5),
        name="stream",
    )(chosen, at, queries, fresh, here, back, prefill, residual, gain, router, routes, *parts)


def hidden_kernel(place_ref, first_ref, second_ref, mine_ref, other_ref, *rest):
    hidden_ref, share_ref, rows_ref = rest[-3:]
    rows = first_ref.shape[0]
    rows_ref[:rows, :] = first_ref[...]
    rows_ref[rows:, :] = second_ref[...]
    gates = rows_ref[:, D:].astype(F32)
    gates = gates + pltpu.roll(gates, 64, 1)
    lane = lax.broadcasted_iota(jnp.int32, gates.shape, 1)
    shares = []
    for side, held_ref in enumerate((mine_ref, other_ref)):
        named = jnp.where(lane == place_ref[side], gates, 0.0)
        shares.append(jnp.sum(named, axis=1, keepdims=True))
        pair = jnp.dot(rows_ref[:, :D], held_ref[...], preferred_element_type=F32)
        gate = pair[:, :FF]
        hidden_ref[:, side * FF : (side + 1) * FF] = (
            gate / (1.0 + jnp.exp(-gate)) * pair[:, FF:]
        ).astype(BF)
    share_ref[...] = jnp.where(lane == 0, shares[0], shares[1])


def make_hidden(place, first, second, mine, other, *earlier):
    rows = 2 * first.shape[0]
    return pl.pallas_call(
        hidden_kernel,
        in_specs=[smem()] + [vmem()] * 4 + [anywhere()] * len(earlier),
        out_specs=[vmem()] * 2,
        out_shape=[
            jax.ShapeDtypeStruct((rows, 2 * FF), BF),
            jax.ShapeDtypeStruct((rows, LANES), F32),
        ],
        scratch_shapes=[pltpu.VMEM((rows, WIDE), BF)],
        compiler_params=pltpu.CompilerParams(vmem_limit_bytes=28 * 1024 * 1024),
        cost_estimate=cost(HIDDEN_COST, 10**5),
        name="hidden",
    )(place, first, second, mine, other, *earlier)


def down_kernel(hidden_ref, share_ref, mine_ref, other_ref, *rest):
    keep_ref, away_ref = rest[-2:]
    total = None
    for side, held_ref in enumerate((mine_ref, other_ref)):
        made = lax.dot_general(
            hidden_ref[:, side * FF : (side + 1) * FF],
            held_ref[...],
            (((1,), (1,)), ((), ())),
            preferred_element_type=F32,
        )
        made = share_ref[:, side : side + 1] * made.astype(BF).astype(F32)
        total = made if total is None else total + made
    rows = keep_ref.shape[0]
    keep_ref[...] = total[:rows].astype(BF)
    away_ref[...] = total[rows:].astype(BF)


def make_down(hidden, share, mine, other, *earlier):
    rows = hidden.shape[0]
    return pl.pallas_call(
        down_kernel,
        in_specs=[vmem()] * 4 + [anywhere()] * len(earlier),
        out_specs=[vmem()] * 2,
        out_shape=[jax.ShapeDtypeStruct((rows // 2, D), BF)] * 2,
        compiler_params=pltpu.CompilerParams(vmem_limit_bytes=28 * 1024 * 1024),
        cost_estimate=cost(DOWN_COST, 10**5),
        name="down",
    )(hidden, share, mine, other, *earlier)


def pack_kernel(gate_ref, down_ref, pair_out, down_out):
    for n in range(gate_ref.shape[0] // 16):
        at = slice(n * 16, (n + 1) * 16)
        gate = gate_ref[at]
        down = down_ref[at]
        for e in range(gate_ref.shape[1]):
            pair_out[e, at, :] = gate[:, e, :]
            down_out[e, at, :] = down[:, e, :]


def pack_experts(gate_up, down_proj):
    depth, experts = gate_up.shape[:2]
    step = depth // 8
    block = lambda n: pl.BlockSpec((step, experts, n * FF), lambda s: (s, 0, 0))
    packed = lambda n: pl.BlockSpec((experts, step, n * FF), lambda s: (0, s, 0))
    return pl.pallas_call(
        pack_kernel,
        grid=(depth // step,),
        in_specs=[block(2), block(1)],
        out_specs=[packed(2), packed(1)],
        out_shape=[jax.ShapeDtypeStruct((experts, depth, n * FF), BF) for n in (2, 1)],
        compiler_params=pltpu.CompilerParams(vmem_limit_bytes=VMEM_LIMIT),
        cost_estimate=cost(7 * 10**9, 10**5),
        name="pack",
    )(gate_up, down_proj)


def swap(x, axis, how):
    return lax.ppermute(x, axis, [(i, how(i)) for i in range(lax.axis_size(axis))])


def near(j):
    return j ^ (2 if j % 2 == 0 else 4)


def beside(j):
    return j ^ 1


def far(j):
    return j ^ (4 if j % 2 == 0 else 2)


def exchange(packed):
    whole = lax.all_to_all(packed, "gx", split_axis=0, concat_axis=0, tiled=True)
    return whole.reshape(-1, packed.shape[2])


def after(x, *others):
    return lax.optimization_barrier((x, others))[0]


def small_call(kernel, name, arrays, earlier, outs, flops=10**6):
    return pl.pallas_call(
        kernel,
        in_specs=[vmem()] * len(arrays) + [anywhere()] * len(earlier),
        out_specs=[vmem()] * len(outs),
        out_shape=[jax.ShapeDtypeStruct(*out) for out in outs],
        compiler_params=pltpu.CompilerParams(vmem_limit_bytes=16 * 1024 * 1024),
        cost_estimate=cost(flops, 10**5),
        name=name,
    )(*arrays, *earlier)


def stack_kernel(count, *refs):
    out_ref, at = refs[-1], 0
    for ref in refs[:count]:
        out_ref[at : at + ref.shape[0], :] = ref[...]
        at += ref.shape[0]


def stack_rows(arrays, *earlier, flops=10**6):
    shape = (sum(x.shape[0] for x in arrays), arrays[0].shape[1])
    kernel = functools.partial(stack_kernel, len(arrays))
    return small_call(kernel, "stack", arrays, earlier, [(shape, BF)], flops)[0]


def join_kernel(keep_ref, came_ref, *rest):
    part_ref, pass_ref = rest[-2:]
    rows = part_ref.shape[0]
    total = keep_ref[...].astype(F32) + came_ref[...].astype(F32)
    part_ref[...] = total[:rows]
    pass_ref[...] = total[rows:].astype(BF)


def join(keep, came, *earlier):
    shape = (keep.shape[0] // 2, keep.shape[1])
    return small_call(join_kernel, "join", [keep, came], earlier, [(shape, F32), (shape, BF)])


def close_kernel(part_ref, came_ref, *rest):
    rest[-1][...] = (part_ref[...] + came_ref[...].astype(F32)).astype(BF)


def close(part, came, *earlier):
    return small_call(close_kernel, "close", [part, came], earlier, [(part.shape, BF)])[0]


def finish_kernel(stream_ref, part_ref, *rest):
    total = stream_ref[...] + part_ref[...]
    for ref in rest[:-1]:
        total = total + ref[...].astype(F32)
    rest[-1][...] = total


def swapped_experts(send, stream, pair, down):
    planes = lax.axis_size("gx")
    row, column = lax.axis_index("gx"), lax.axis_index("gy")
    place = jnp.stack([column * planes + row, beside(column) * planes + row]).astype(jnp.int32)
    across = lambda x, k: swap(x, "gx", lambda i: i ^ k)

    first = [stack_rows([send, swap(send, "gy", near)])]
    mine = [send] + [across(send, k) for k in range(1, planes)]
    other_pair = swap(after(pair, first[0]), "gy", beside)
    first += [
        stack_rows([mine[k], swap(mine[k], "gy", near)], flops=10**6)
        for k in range(1, planes)
    ]
    second = [swap(x, "gy", far) for x in first]
    hidden, last = [], ()
    for k in range(planes):
        hidden.append(make_hidden(place, first[k], second[k], pair, other_pair, *last))
        last = (hidden[k][1],)
    down = exchange(after(down, second[0], *first[1:]))
    down = after(down, hidden[-1][1])
    other_down = swap(down, "gy", beside)

    made, arrived, parts, ends = {}, {}, {}, {}
    last = ()

    def put(k):
        made[k] = make_down(*hidden[k], down, other_down, *last)
        arrived[k] = swap(made[k][1], "gy", far)
        return (made[k][0],)

    def turn(k, *earlier):
        parts[k], passed = join(made[k][0], arrived[k], *last, *earlier)
        ends[k] = swap(passed, "gy", near)
        return (passed,)

    def leave(k):
        passed = close(parts[k], ends[k], *last)
        ends[k] = across(passed, k)
        return (passed,)

    order = list(reversed(range(planes)))
    last = put(order[0])
    last = put(order[1])
    last = turn(order[0])
    for n in range(2, planes):
        last = put(order[n])
        last = leave(order[n - 2])
        last = turn(order[n - 1]) if n < 3 else turn(order[n - 1], ends[order[0]])
    last = leave(order[-2])
    last = turn(order[-1])
    arrays = [stream, parts[0], ends[0]] + [ends[k] for k in range(1, planes)]
    return small_call(finish_kernel, "finish", arrays, (), [(stream.shape, F32)])[0]


def gathered_experts(send, stream, routes, gate_up, down_proj):
    columns = lax.axis_size("gy")
    normed = send[:, :D]
    gates = send[:, D : D + EXPERTS].astype(F32) + send[:, D + 64 : D + 64 + EXPERTS].astype(F32)
    gate_weights = jnp.take_along_axis(gates, routes, axis=1)
    row_count = normed.shape[0]
    full_pair = lax.all_gather(gate_up, "gx", axis=0, tiled=True)
    full_down = lax.all_gather(down_proj, "gx", axis=0, tiled=True)
    flat_routes = routes.reshape(row_count * TOP)
    route_hits = (flat_routes[:, None] == jnp.arange(EXPERTS, dtype=jnp.int32)[None, :]).astype(
        jnp.int32
    )
    places = jnp.sum((jnp.cumsum(route_hits, axis=0) - 1) * route_hits, axis=1)
    targets = flat_routes * CAP + places
    repeated = jnp.repeat(normed, TOP, axis=0)
    experts_dev = full_pair.shape[1]
    outgoing_rows = (
        jnp.zeros((EXPERTS * CAP, D), BF)
        .at[targets]
        .set(repeated)
        .reshape(columns, experts_dev, CAP, D)
    )
    arrived = lax.all_to_all(outgoing_rows, "gy", split_axis=0, concat_axis=0, tiled=True)
    gate_pair = jnp.einsum("secd,def->secf", arrived, full_pair, preferred_element_type=F32)
    hidden = (jax.nn.silu(gate_pair[..., :FF]) * gate_pair[..., FF:]).astype(BF)
    expert_rows = jnp.einsum(
        "secf,def->secd", hidden, full_down, preferred_element_type=F32
    ).astype(BF)
    returned = lax.all_to_all(expert_rows, "gy", split_axis=0, concat_axis=0, tiled=True).reshape(
        EXPERTS * CAP, D
    )
    picked = returned[targets].astype(F32).reshape(row_count, TOP, D)
    return stream + jnp.sum(gate_weights[:, :, None] * picked, axis=1)


def gather_out(out_weight):
    columns = lax.axis_size("gy")
    share = out_weight.shape[0] // columns
    mine = lax.dynamic_slice_in_dim(out_weight, lax.axis_index("gy") * share, share, axis=0)
    whole = lax.all_gather(mine, ("gx", "gy"), axis=0, tiled=True)
    return jnp.zeros((1,), jnp.int32), [whole], ((1, whole.shape[0]),), whole


def start_out(out_weight):
    planes, columns = lax.axis_size("gx"), lax.axis_size("gy")
    share = out_weight.shape[0] // columns
    mine = lax.dynamic_slice_in_dim(out_weight, lax.axis_index("gy") * share, share, axis=0)
    return [swap(mine, "gx", lambda i, k=k: i ^ k) for k in range(1, planes)]


def swap_out(out_weight, first, asks):
    planes, columns = lax.axis_size("gx"), lax.axis_size("gy")
    row, column = lax.axis_index("gx"), lax.axis_index("gy")
    depth = out_weight.shape[0]
    share = depth // columns
    second = swap(first, "gy", near)
    both = stack_rows([first, second], asks)
    third = swap(both, "gy", far)
    parts = [first, second, third]
    near_of = lambda j: jnp.where(j % 2 == 0, j ^ 2, j ^ 4)
    far_of = lambda j: jnp.where(j % 2 == 0, j ^ 4, j ^ 2)
    at = [row * depth]
    for own in (column, column ^ 1):
        for source in (own, near_of(own), far_of(own), near_of(far_of(own))):
            at += [(row ^ k) * depth + source * share for k in range(1, planes)]
    one = (planes - 1, share)
    two = (2 * (planes - 1), share)
    at = jnp.stack(at).astype(jnp.int32)
    return at, parts, ((1, depth), one, one, two, one, one, two), both


def body(
    queries,
    new_kv,
    cache_pool,
    cache_len,
    local_pages,
    anchor,
    push_pages,
    prefill_attn,
    residual,
    out_weight,
    norm_gain,
    router,
    routes,
    gate_up,
    down_proj,
):
    columns = lax.axis_size("gy")
    slot_count = (MOVED + columns - 2) // (columns - 1)
    pool = cache_pool.reshape(-1, cache_pool.shape[2])
    matches = (anchor[:, None] == jnp.arange(columns, dtype=jnp.int32)[None, :]).astype(jnp.int32)
    earlier = jnp.sum((jnp.cumsum(matches, axis=0) - 1) * matches, axis=1)
    slots = columns * slot_count
    column = lax.axis_index("gy")
    chosen = anchor * slots + column * slot_count + earlier
    extra = jnp.stack([cache_len[LOCAL:] // PAGE, cache_len[LOCAL:] % PAGE, anchor, earlier], axis=1)
    extra = jnp.pad(extra.astype(BF), ((0, 0), (0, LANES - 4)))
    asks = lax.all_gather(
        jnp.concatenate([queries[LOCAL:], extra], axis=1), "gy", axis=0, tiled=True
    )
    extra = jnp.stack([cache_len[:LOCAL] // PAGE, cache_len[:LOCAL] % PAGE], axis=1)
    extra = jnp.pad(extra.astype(BF), ((0, 0), (0, LANES - 2)))
    own = jnp.concatenate([queries[:LOCAL], extra], axis=1)
    planes = lax.axis_size("gx")
    swapped = columns == 8 and planes & (planes - 1) == 0 and gate_up.shape[1] == planes
    if swapped:
        out_parts = start_out(out_weight)
        pair, down = pack_experts(gate_up, down_proj)
        out_parts, pair, down = lax.optimization_barrier((out_parts, pair, down))
        pair = exchange(pair)
        out_parts = swap_out(out_weight, stack_rows(out_parts), asks)
        asks = after(asks, out_parts[3])
    else:
        out_parts = gather_out(out_weight)
    here, reply = attend(
        column.astype(jnp.int32).reshape(1),
        own,
        asks,
        jnp.concatenate([local_pages, push_pages], axis=0),
        pool,
    )
    if swapped:
        at, parts, pieces, _ = out_parts
        others = [swap(part, "gy", beside) for part in after(parts, reply)]
        out_parts = (at, [out_weight] + parts + others, pieces, None)
    back = lax.all_gather(reply, "gy", axis=0, tiled=True)
    attended, stream, send = make_stream(
        chosen,
        queries,
        new_kv,
        here,
        back,
        prefill_attn,
        residual,
        out_parts,
        norm_gain.reshape(1, D),
        jnp.pad(router, ((0, 0), (0, LANES - EXPERTS))),
        routes,
    )
    if swapped:
        layer_out = swapped_experts(send, stream, pair, down)
    else:
        layer_out = gathered_experts(send, stream, routes, gate_up, down_proj)
    return (attended, layer_out)


def solution(mesh):
    placed = (
        P(("gx", "gy"), None),
        P(("gx", "gy"), None),
        P(("gx", "gy"), None, None),
        P(("gx", "gy")),
        P(("gx", "gy"), None),
        P(("gx", "gy")),
        P(("gx", "gy"), None),
        P(("gx", "gy"), None),
        P(("gx", "gy"), None),
        P("gx", None),
        P(),
        P(),
        P(("gx", "gy"), None),
        P("gx", "gy", None),
        P("gx", "gy", None),
    )
    return jax.shard_map(
        body,
        mesh=mesh,
        in_specs=placed,
        out_specs=(P(("gx", "gy"), None), P(("gx", "gy"), None)),
        check_vma=False,
    )
```

```python
import functools
import math

import jax
import jax.numpy as jnp
from jax import lax
from jax.experimental import pallas as pl
from jax.experimental.pallas import tpu as pltpu
from jax.sharding import PartitionSpec as P

D = 1536
HEADS = 24
KV_HEADS = 8
HEAD = 64
GROUP = HEADS // KV_HEADS
EXPERTS = 32
FF = 512
TOP = 8
PAGE = 16
MAXLEN = 512
NPAGE = 32
R_DEV = 16
LOCAL = 8
MOVED = 8
CAP = 48
LANES = 128
WIDE = D + LANES
PAIRS = KV_HEADS // 2
BIG = 1e30
HIDDEN_COST = 10**6
DOWN_COST = 10**6
VMEM_LIMIT = 60 * 1024 * 1024
BF = jnp.bfloat16
F32 = jnp.float32


def vmem():
    return pl.BlockSpec(memory_space=pltpu.VMEM)


def smem():
    return pl.BlockSpec(memory_space=pltpu.SMEM)


def anywhere():
    return pl.BlockSpec(memory_space=pl.ANY)


def cost(flops, moved):
    return pl.CostEstimate(flops=flops, bytes_accessed=moved, transcendentals=0)


def attend_kernel(
    me_ref, own_ref, asks_ref, table_ref, key_ref, value_ref, here_ref, reply_ref, counts, ask_ref
):
    step = pl.program_id(0)
    slots = table_ref.shape[0]
    pages = counts.shape[1] // PAGE

    @pl.when(step == 0)
    def _():
        away = slots - LOCAL
        code = asks_ref[:, D:].astype(jnp.int32)
        sender = lax.broadcasted_iota(jnp.int32, (code.shape[0], 1), 0) // MOVED
        each = away // (code.shape[0] // MOVED)
        slot = jnp.where(code[:, 2:3] == me_ref[0], sender * each + code[:, 3:4], -1)
        take = lax.broadcasted_iota(jnp.int32, (code.shape[0], away), 1) == slot
        take = jnp.where(take, 1.0, 0.0).astype(BF)
        ask_ref[:LOCAL, :] = own_ref[...].astype(F32)
        ask_ref[LOCAL:, :] = lax.dot_general(
            take, asks_ref[...], (((0,), (0,)), ((), ())), preferred_element_type=F32
        )
        lengths = ask_ref[:, D:].astype(jnp.int32)
        full, rest = lengths[:, 0:1], lengths[:, 1:2]
        table = table_ref[...]
        page = lax.broadcasted_iota(jnp.int32, (slots, pages), 1)
        whole = jnp.zeros((slots, pages), F32)
        part = jnp.zeros((slots, pages), F32)
        for p in range(NPAGE):
            hit = table[:, p : p + 1] == page
            whole += jnp.where(hit & (full > p), 1.0, 0.0)
            part += jnp.where(hit & (full == p), 1.0, 0.0)
        row = lax.broadcasted_iota(jnp.int32, (pages, pages * PAGE), 1)
        spread = jnp.where(
            row // PAGE == lax.broadcasted_iota(jnp.int32, (pages, pages * PAGE), 0), 1.0, 0.0
        ).astype(BF)
        whole = jnp.dot(whole.astype(BF), spread, preferred_element_type=F32)
        part = jnp.dot(part.astype(BF), spread, preferred_element_type=F32)
        place = lax.broadcasted_iota(jnp.int32, (slots, pages * PAGE), 1) % PAGE
        counts[...] = whole + jnp.where(place < rest, part, 0.0)

    lane = lax.broadcasted_iota(jnp.int32, (slots, LANES), 1)
    rows = []
    for j in range(2 * GROUP):
        side, chunk, half = j // GROUP, j // 2, j % 2
        at = pl.multiple_of(step * (2 * GROUP * HEAD) + chunk * LANES, LANES)
        part = ask_ref[:, pl.ds(at, LANES)] * (1.0 / math.sqrt(HEAD))
        if side != half:
            part = pltpu.roll(part, HEAD, 1)
        rows.append(jnp.where((lane < HEAD) == (side == 0), part, 0.0).astype(BF))
    heads = jnp.concatenate(rows, axis=0)
    scores = lax.dot_general(
        heads, key_ref[...], (((1,), (1,)), ((), ())), preferred_element_type=F32
    )
    count = jnp.concatenate([counts[...]] * (2 * GROUP), axis=0)
    masked = jnp.where(count > 0.0, scores, -BIG)
    highest = jnp.max(masked, axis=1, keepdims=True)
    expos = jnp.exp(masked - highest)
    totals = jnp.sum(expos * count, axis=1, keepdims=True)
    weights = (expos.astype(BF).astype(F32) * count).astype(BF)
    mixture = jnp.dot(weights, value_ref[...], preferred_element_type=F32)

    def put(at, value):
        here_ref[:, pl.ds(at, LANES)] = value[:LOCAL]
        reply_ref[:, pl.ds(at, LANES)] = value[LOCAL:]

    @pl.when(step == 0)
    def _():
        put(D, jnp.zeros((slots, LANES), F32))

    stat = jnp.concatenate([here_ref[:, D:], reply_ref[:, D:]], axis=0)
    for j in range(2 * GROUP):
        head = step * 2 * GROUP + j
        take = slice(j * slots, (j + 1) * slots)
        stat = jnp.where(lane == head, highest[take], stat)
        stat = jnp.where(lane == head + 64, totals[take], stat)
    put(D, stat)
    for chunk in range(GROUP):
        halves = []
        for half in range(2):
            j = 2 * chunk + half
            part = mixture[j * slots : (j + 1) * slots]
            if j // GROUP != half:
                part = pltpu.roll(part, HEAD, 1)
            halves.append(part)
        at = pl.multiple_of(step * (2 * GROUP * HEAD) + chunk * LANES, LANES)
        put(at, jnp.where(lane < HEAD, halves[0], halves[1]))


def attend(me, own, asks, table, pool):
    slots = table.shape[0]
    tokens = pool.shape[0]
    return pl.pallas_call(
        attend_kernel,
        grid=(PAIRS,),
        in_specs=[
            smem(),
            pl.BlockSpec(own.shape, lambda s: (0, 0)),
            pl.BlockSpec(asks.shape, lambda s: (0, 0)),
            pl.BlockSpec((slots, NPAGE), lambda s: (0, 0)),
            pl.BlockSpec((tokens, LANES), lambda s: (0, s)),
            pl.BlockSpec((tokens, LANES), lambda s: (0, PAIRS + s)),
        ],
        out_specs=[
            pl.BlockSpec((LOCAL, WIDE), lambda s: (0, 0)),
            pl.BlockSpec((slots - LOCAL, WIDE), lambda s: (0, 0)),
        ],
        out_shape=[
            jax.ShapeDtypeStruct((LOCAL, WIDE), F32),
            jax.ShapeDtypeStruct((slots - LOCAL, WIDE), F32),
        ],
        scratch_shapes=[pltpu.VMEM((slots, tokens), F32), pltpu.VMEM((slots, WIDE), F32)],
        compiler_params=pltpu.CompilerParams(vmem_limit_bytes=VMEM_LIMIT),
        cost_estimate=cost(7 * 10**9, 10**5),
        name="attend",
    )(me, own, asks, table, pool, pool)


def stream_kernel(
    pieces, chosen_ref, at_ref, query_ref, fresh_ref, here_ref, back_ref, prefill_ref,
    residual_ref, gain_ref, router_ref, routes_ref, *rest
):
    parts, rest = rest[: len(pieces)], rest[len(pieces) :]
    attended_ref, stream_ref, send_ref, tokens, out_ref, sems = rest
    copies = []
    for part, (blocks, rows) in zip(parts, pieces):
        for block in range(blocks):
            n = len(copies)
            at = pl.multiple_of(at_ref[n], 16)
            copy = pltpu.make_async_copy(
                part.at[pl.ds(block * rows, rows)], out_ref.at[pl.ds(at, rows)], sems.at[n]
            )
            copy.start()
            copies.append(copy)
    count = query_ref.shape[0]
    lane = lax.broadcasted_iota(jnp.int32, (count, LANES), 1)
    low = lane < HEAD
    picked = [back_ref[pl.ds(chosen_ref[m], 1), :] for m in range(MOVED)]
    picked = jnp.concatenate(picked, axis=0)
    mix = jnp.concatenate([here_ref[:, :D], picked[:, :D]], axis=0)
    stat = jnp.concatenate([here_ref[:, D:], picked[:, D:]], axis=0)
    fresh = fresh_ref[...].astype(F32)

    def spread(first, second, base):
        sides = []
        for half, head in enumerate((first, second)):
            part = fresh[:, base + head // 2 * LANES : base + head // 2 * LANES + LANES]
            sides.append(pltpu.roll(part, HEAD, 1) if head % 2 != half else part)
        return jnp.where(low, sides[0], sides[1])

    def both(first, second):
        return jnp.where(low, first, second)

    for chunk in range(HEADS // 2):
        first, second = 2 * chunk, 2 * chunk + 1
        span = slice(chunk * LANES, (chunk + 1) * LANES)
        keys = spread(first // GROUP, second // GROUP, 0)
        values = spread(first // GROUP, second // GROUP, KV_HEADS * HEAD)
        product = query_ref[:, span].astype(F32) * keys
        scale = 1.0 / math.sqrt(HEAD)
        own = both(
            jnp.sum(jnp.where(low, product, 0.0), axis=1, keepdims=True) * scale,
            jnp.sum(jnp.where(low, 0.0, product), axis=1, keepdims=True) * scale,
        )
        cache_max = both(stat[:, first : first + 1], stat[:, second : second + 1])
        total = both(stat[:, 64 + first : 65 + first], stat[:, 64 + second : 65 + second])
        highest = jnp.maximum(cache_max, own)
        old = jnp.exp(cache_max - highest)
        new = jnp.exp(own - highest)
        output = (old * mix[:, span] + new * values) / (old * total + new)
        tokens[:count, span] = output.astype(BF)
    attended_ref[...] = tokens[:count, :]
    tokens[count:, :] = prefill_ref[...]
    for copy in copies:
        copy.wait()
    stream = residual_ref[...].astype(F32) + jnp.dot(
        tokens[...], out_ref[...], preferred_element_type=F32
    )
    stream_ref[...] = stream
    normed = (
        stream
        * lax.rsqrt(jnp.mean(stream * stream, axis=1, keepdims=True) + 1e-06)
        * gain_ref[...].astype(F32)
    ).astype(BF)
    send_ref[:, :D] = normed
    logits = jnp.dot(normed, router_ref[...], preferred_element_type=F32)
    rows = logits.shape[0]
    expert = lax.broadcasted_iota(jnp.int32, (rows, LANES), 1)
    routes = routes_ref[...]
    named = expert == routes[:, 0:1]
    for k in range(1, TOP):
        named = named | (expert == routes[:, k : k + 1])
    masked = jnp.where(named, logits, -BIG)
    expos = jnp.where(named, jnp.exp(masked - jnp.max(masked, axis=1, keepdims=True)), 0.0)
    gates = expos / jnp.sum(expos, axis=1, keepdims=True)
    coarse = gates.astype(BF).astype(F32)
    fine = pltpu.roll(gates - coarse, 64, 1)
    send_ref[:, D:] = jnp.where(expert < 64, coarse, fine).astype(BF)


def make_stream(
    chosen, queries, fresh, here, back, prefill, residual, out_parts, gain, router, routes
):
    rows = residual.shape[0]
    count = queries.shape[0]
    at, parts, pieces, _ = out_parts
    return pl.pallas_call(
        functools.partial(stream_kernel, pieces),
        in_specs=[smem()] * 2 + [vmem()] * 9 + [pl.BlockSpec(memory_space=pltpu.HBM)] * len(parts),
        out_specs=[vmem()] * 3,
        out_shape=[
            jax.ShapeDtypeStruct((count, D), BF),
            jax.ShapeDtypeStruct((rows, D), F32),
            jax.ShapeDtypeStruct((rows, WIDE), BF),
        ],
        scratch_shapes=[
            pltpu.VMEM((rows, D), BF),
            pltpu.VMEM((D, D), BF),
            pltpu.SemaphoreType.DMA((sum(blocks for blocks, _ in pieces),)),
        ],
        compiler_params=pltpu.CompilerParams(vmem_limit_bytes=VMEM_LIMIT),
        cost_estimate=cost(8 * 10**9, 10**5),
        name="stream",
    )(chosen, at, queries, fresh, here, back, prefill, residual, gain, router, routes, *parts)


def hidden_kernel(count, place_ref, *refs):
    pieces, (mine_ref, other_ref) = refs[:count], refs[count : count + 2]
    hidden_ref, share_ref, rows_ref = refs[-3:]
    rows = pieces[0].shape[0]
    for n, piece in enumerate(pieces):
        rows_ref[n * rows : (n + 1) * rows, :] = piece[...]
    gates = rows_ref[:, D:].astype(F32)
    gates = gates + pltpu.roll(gates, 64, 1)
    lane = lax.broadcasted_iota(jnp.int32, gates.shape, 1)
    shares = []
    for side, held_ref in enumerate((mine_ref, other_ref)):
        named = jnp.where(lane == place_ref[side], gates, 0.0)
        shares.append(jnp.sum(named, axis=1, keepdims=True))
        pair = jnp.dot(rows_ref[:, :D], held_ref[...], preferred_element_type=F32)
        gate = pair[:, :FF]
        hidden_ref[:, side * FF : (side + 1) * FF] = (
            gate / (1.0 + jnp.exp(-gate)) * pair[:, FF:]
        ).astype(BF)
    share_ref[...] = jnp.where(lane == 0, shares[0], shares[1])


def make_hidden(place, pieces, mine, other, *earlier):
    rows = sum(piece.shape[0] for piece in pieces)
    return pl.pallas_call(
        functools.partial(hidden_kernel, len(pieces)),
        in_specs=[smem()] + [vmem()] * (len(pieces) + 2) + [anywhere()] * len(earlier),
        out_specs=[vmem()] * 2,
        out_shape=[
            jax.ShapeDtypeStruct((rows, 2 * FF), BF),
            jax.ShapeDtypeStruct((rows, LANES), F32),
        ],
        scratch_shapes=[pltpu.VMEM((rows, WIDE), BF)],
        compiler_params=pltpu.CompilerParams(vmem_limit_bytes=28 * 1024 * 1024),
        cost_estimate=cost(HIDDEN_COST, 10**5),
        name="hidden",
    )(place, *pieces, mine, other, *earlier)


def down_kernel(count, hidden_ref, share_ref, mine_ref, other_ref, *rest):
    total = None
    for side, held_ref in enumerate((mine_ref, other_ref)):
        made = lax.dot_general(
            hidden_ref[:, side * FF : (side + 1) * FF],
            held_ref[...],
            (((1,), (1,)), ((), ())),
            preferred_element_type=F32,
        )
        made = share_ref[:, side : side + 1] * made.astype(BF).astype(F32)
        total = made if total is None else total + made
    for n, out_ref in enumerate(rest[-count:]):
        rows = out_ref.shape[0]
        out_ref[...] = total[n * rows : (n + 1) * rows].astype(BF)


def make_down(count, hidden, share, mine, other, *earlier):
    rows = hidden.shape[0]
    return pl.pallas_call(
        functools.partial(down_kernel, count),
        in_specs=[vmem()] * 4 + [anywhere()] * len(earlier),
        out_specs=[vmem()] * count,
        out_shape=[jax.ShapeDtypeStruct((rows // count, D), BF)] * count,
        compiler_params=pltpu.CompilerParams(vmem_limit_bytes=28 * 1024 * 1024),
        cost_estimate=cost(DOWN_COST, 10**5),
        name="down",
    )(hidden, share, mine, other, *earlier)


def pack_kernel(gate_ref, down_ref, pair_out, down_out):
    for n in range(gate_ref.shape[0] // 16):
        at = slice(n * 16, (n + 1) * 16)
        gate = gate_ref[at]
        down = down_ref[at]
        for e in range(gate_ref.shape[1]):
            pair_out[e, at, :] = gate[:, e, :]
            down_out[e, at, :] = down[:, e, :]


def pack_experts(gate_up, down_proj):
    depth, experts = gate_up.shape[:2]
    step = depth // 4
    block = lambda n: pl.BlockSpec((step, experts, n * FF), lambda s: (s, 0, 0))
    packed = lambda n: pl.BlockSpec((experts, step, n * FF), lambda s: (0, s, 0))
    return pl.pallas_call(
        pack_kernel,
        grid=(depth // step,),
        in_specs=[block(2), block(1)],
        out_specs=[packed(2), packed(1)],
        out_shape=[jax.ShapeDtypeStruct((experts, depth, n * FF), BF) for n in (2, 1)],
        compiler_params=pltpu.CompilerParams(vmem_limit_bytes=VMEM_LIMIT),
        cost_estimate=cost(7 * 10**9, 10**5),
        name="pack",
    )(gate_up, down_proj)


def swap(x, axis, how):
    return lax.ppermute(x, axis, [(i, how(i)) for i in range(lax.axis_size(axis))])


def near(j):
    return j ^ (2 if j % 2 == 0 else 4)


def beside(j):
    return j ^ 1


def far(j):
    return j ^ (4 if j % 2 == 0 else 2)


def exchange(packed):
    whole = lax.all_to_all(packed, "gx", split_axis=0, concat_axis=0, tiled=True)
    return whole.reshape(-1, packed.shape[2])


def after(x, *others):
    return lax.optimization_barrier((x, others))[0]


def small_call(kernel, name, arrays, earlier, outs, flops=10**6):
    return pl.pallas_call(
        kernel,
        in_specs=[vmem()] * len(arrays) + [anywhere()] * len(earlier),
        out_specs=[vmem()] * len(outs),
        out_shape=[jax.ShapeDtypeStruct(*out) for out in outs],
        compiler_params=pltpu.CompilerParams(vmem_limit_bytes=16 * 1024 * 1024),
        cost_estimate=cost(flops, 10**5),
        name=name,
    )(*arrays, *earlier)


def stack_kernel(count, *refs):
    out_ref, at = refs[-1], 0
    for ref in refs[:count]:
        out_ref[at : at + ref.shape[0], :] = ref[...]
        at += ref.shape[0]


def stack_rows(arrays, *earlier, flops=10**6):
    shape = (sum(x.shape[0] for x in arrays), arrays[0].shape[1])
    kernel = functools.partial(stack_kernel, len(arrays))
    return small_call(kernel, "stack", arrays, earlier, [(shape, BF)], flops)[0]


def join_kernel(keep_ref, came_ref, *rest):
    part_ref, pass_ref = rest[-2:]
    rows = part_ref.shape[0]
    total = keep_ref[...].astype(F32) + came_ref[...].astype(F32)
    part_ref[...] = total[:rows]
    pass_ref[...] = total[rows:].astype(BF)


def join(keep, came, *earlier):
    shape = (keep.shape[0] // 2, keep.shape[1])
    return small_call(join_kernel, "join", [keep, came], earlier, [(shape, F32), (shape, BF)])


def close_kernel(count, part_ref, *rest):
    total = part_ref[...]
    for ref in rest[:count]:
        total = total + ref[...].astype(F32)
    rest[-1][...] = total.astype(BF)


def close(part, came, *earlier):
    kernel = functools.partial(close_kernel, len(came))
    return small_call(kernel, "close", [part, *came], earlier, [(part.shape, BF)])[0]


def finish_kernel(stream_ref, part_ref, *rest):
    total = stream_ref[...] + part_ref[...]
    for ref in rest[:-1]:
        total = total + ref[...].astype(F32)
    rest[-1][...] = total


def swapped_experts(send, stream, pair, down):
    planes = lax.axis_size("gx")
    row, column = lax.axis_index("gx"), lax.axis_index("gy")
    place = jnp.stack([column * planes + row, beside(column) * planes + row]).astype(jnp.int32)
    across = lambda x, k: swap(x, "gx", lambda i: i ^ k)

    mine = [send] + [across(send, k) for k in range(1, planes)]
    beyond = [swap(x, "gy", near) for x in mine]
    first = [stack_rows([mine[k], beyond[k]]) for k in range(3)]
    second = [swap(x, "gy", far) for x in first]
    other_pair = swap(after(pair, second[0], *first[1:], mine[3]), "gy", beside)
    down = exchange(after(down, first[0]))
    hidden, last = {}, ()

    def inner(k, pieces):
        hidden[k] = make_hidden(place, pieces, pair, other_pair, *last)
        return (hidden[k][1],)

    last = inner(0, [first[0], second[0]])
    first.append(stack_rows([mine[3], beyond[3]], *last))
    second.append(swap(first[3], "gy", far))
    last = inner(3, [first[3]])
    last = inner(1, [first[1], second[1]])
    last = inner(2, [first[2], second[2]])
    other_down = swap(after(down, hidden[2][1], second[3]), "gy", beside)
    outer = make_hidden(place, [second[3]], pair, other_pair, *last)

    made, arrived, parts, ends = {}, {}, {}, {}
    last = ()

    def put(k):
        if k == 3:
            away = make_down(1, *outer, down, other_down)[0]
            made[k] = [*make_down(1, *hidden[k], down, other_down, away), away]
        else:
            made[k] = make_down(2, *hidden[k], down, other_down, *last)
        arrived[k] = swap(made[k][1], "gy", far)
        return (made[k][0],)

    def turn(k, *earlier):
        parts[k], passed = join(made[k][0], arrived[k], *last, *earlier)
        ends[k] = swap(passed, "gy", near)
        return (passed,)

    def leave(k, *came):
        passed = close(parts[k], [ends[k], *came], *last)
        ends[k] = across(passed, 2 if k == 2 else 1)
        return (passed,)

    last = put(3)
    last = put(2)
    last = turn(3)
    last = put(1)
    last = leave(3)
    last = turn(2)
    last = put(0)
    last = leave(2, ends[3])
    last = turn(1)
    last = leave(1)
    last = turn(0)
    arrays = [stream, parts[0], ends[0], ends[1], ends[2]]
    return small_call(finish_kernel, "finish", arrays, (), [(stream.shape, F32)])[0]


def gathered_experts(send, stream, routes, gate_up, down_proj):
    columns = lax.axis_size("gy")
    normed = send[:, :D]
    gates = send[:, D : D + EXPERTS].astype(F32) + send[:, D + 64 : D + 64 + EXPERTS].astype(F32)
    gate_weights = jnp.take_along_axis(gates, routes, axis=1)
    row_count = normed.shape[0]
    full_pair = lax.all_gather(gate_up, "gx", axis=0, tiled=True)
    full_down = lax.all_gather(down_proj, "gx", axis=0, tiled=True)
    flat_routes = routes.reshape(row_count * TOP)
    route_hits = (flat_routes[:, None] == jnp.arange(EXPERTS, dtype=jnp.int32)[None, :]).astype(
        jnp.int32
    )
    places = jnp.sum((jnp.cumsum(route_hits, axis=0) - 1) * route_hits, axis=1)
    targets = flat_routes * CAP + places
    repeated = jnp.repeat(normed, TOP, axis=0)
    experts_dev = full_pair.shape[1]
    outgoing_rows = (
        jnp.zeros((EXPERTS * CAP, D), BF)
        .at[targets]
        .set(repeated)
        .reshape(columns, experts_dev, CAP, D)
    )
    arrived = lax.all_to_all(outgoing_rows, "gy", split_axis=0, concat_axis=0, tiled=True)
    gate_pair = jnp.einsum("secd,def->secf", arrived, full_pair, preferred_element_type=F32)
    hidden = (jax.nn.silu(gate_pair[..., :FF]) * gate_pair[..., FF:]).astype(BF)
    expert_rows = jnp.einsum(
        "secf,def->secd", hidden, full_down, preferred_element_type=F32
    ).astype(BF)
    returned = lax.all_to_all(expert_rows, "gy", split_axis=0, concat_axis=0, tiled=True).reshape(
        EXPERTS * CAP, D
    )
    picked = returned[targets].astype(F32).reshape(row_count, TOP, D)
    return stream + jnp.sum(gate_weights[:, :, None] * picked, axis=1)


def gather_out(out_weight):
    columns = lax.axis_size("gy")
    share = out_weight.shape[0] // columns
    mine = lax.dynamic_slice_in_dim(out_weight, lax.axis_index("gy") * share, share, axis=0)
    whole = lax.all_gather(mine, ("gx", "gy"), axis=0, tiled=True)
    return jnp.zeros((1,), jnp.int32), [whole], ((1, whole.shape[0]),), whole


def start_out(out_weight):
    planes, columns = lax.axis_size("gx"), lax.axis_size("gy")
    share = out_weight.shape[0] // columns
    mine = lax.dynamic_slice_in_dim(out_weight, lax.axis_index("gy") * share, share, axis=0)
    return [swap(mine, "gx", lambda i, k=k: i ^ k) for k in range(1, planes)]


def swap_out(out_weight, first, asks):
    planes, columns = lax.axis_size("gx"), lax.axis_size("gy")
    row, column = lax.axis_index("gx"), lax.axis_index("gy")
    depth = out_weight.shape[0]
    share = depth // columns
    second = swap(first, "gy", near)
    both = stack_rows([first, second], asks)
    third = swap(both, "gy", far)
    parts = [first, second, third]
    near_of = lambda j: jnp.where(j % 2 == 0, j ^ 2, j ^ 4)
    far_of = lambda j: jnp.where(j % 2 == 0, j ^ 4, j ^ 2)
    at = [row * depth]
    for own in (column, column ^ 1):
        for source in (own, near_of(own), far_of(own), near_of(far_of(own))):
            at += [(row ^ k) * depth + source * share for k in range(1, planes)]
    one = (planes - 1, share)
    two = (2 * (planes - 1), share)
    at = jnp.stack(at).astype(jnp.int32)
    return at, parts, ((1, depth), one, one, two, one, one, two), both


def body(
    queries,
    new_kv,
    cache_pool,
    cache_len,
    local_pages,
    anchor,
    push_pages,
    prefill_attn,
    residual,
    out_weight,
    norm_gain,
    router,
    routes,
    gate_up,
    down_proj,
):
    columns = lax.axis_size("gy")
    slot_count = (MOVED + columns - 2) // (columns - 1)
    pool = cache_pool.reshape(-1, cache_pool.shape[2])
    planes = lax.axis_size("gx")
    swapped = columns == 8 and planes == 4 and gate_up.shape[1] == planes
    if swapped:
        out_parts = start_out(out_weight)
        pair, down = pack_experts(gate_up, down_proj)
        cache_len, anchor = after((cache_len, anchor), pair)
    matches = (anchor[:, None] == jnp.arange(columns, dtype=jnp.int32)[None, :]).astype(jnp.int32)
    earlier = jnp.sum((jnp.cumsum(matches, axis=0) - 1) * matches, axis=1)
    slots = columns * slot_count
    column = lax.axis_index("gy")
    chosen = anchor * slots + column * slot_count + earlier
    extra = jnp.stack([cache_len[LOCAL:] // PAGE, cache_len[LOCAL:] % PAGE, anchor, earlier], axis=1)
    extra = jnp.pad(extra.astype(BF), ((0, 0), (0, LANES - 4)))
    asks = lax.all_gather(
        jnp.concatenate([queries[LOCAL:], extra], axis=1), "gy", axis=0, tiled=True
    )
    extra = jnp.stack([cache_len[:LOCAL] // PAGE, cache_len[:LOCAL] % PAGE], axis=1)
    extra = jnp.pad(extra.astype(BF), ((0, 0), (0, LANES - 2)))
    own = jnp.concatenate([queries[:LOCAL], extra], axis=1)
    if swapped:
        out_parts, pair, down = lax.optimization_barrier((out_parts, pair, down))
        pair = exchange(pair)
        out_parts = swap_out(out_weight, stack_rows(out_parts), asks)
        asks = after(asks, out_parts[3])
    else:
        out_parts = gather_out(out_weight)
    here, reply = attend(
        column.astype(jnp.int32).reshape(1),
        own,
        asks,
        jnp.concatenate([local_pages, push_pages], axis=0),
        pool,
    )
    if swapped:
        at, parts, pieces, _ = out_parts
        others = [swap(part, "gy", beside) for part in after(parts, reply)]
        out_parts = (at, [out_weight] + parts + others, pieces, None)
    back = lax.all_gather(reply, "gy", axis=0, tiled=True)
    attended, stream, send = make_stream(
        chosen,
        queries,
        new_kv,
        here,
        back,
        prefill_attn,
        residual,
        out_parts,
        norm_gain.reshape(1, D),
        jnp.pad(router, ((0, 0), (0, LANES - EXPERTS))),
        routes,
    )
    if swapped:
        layer_out = swapped_experts(send, stream, pair, down)
    else:
        layer_out = gathered_experts(send, stream, routes, gate_up, down_proj)
    return (attended, layer_out)


def solution(mesh):
    placed = (
        P(("gx", "gy"), None),
        P(("gx", "gy"), None),
        P(("gx", "gy"), None, None),
        P(("gx", "gy")),
        P(("gx", "gy"), None),
        P(("gx", "gy")),
        P(("gx", "gy"), None),
        P(("gx", "gy"), None),
        P(("gx", "gy"), None),
        P("gx", None),
        P(),
        P(),
        P(("gx", "gy"), None),
        P("gx", "gy", None),
        P("gx", "gy", None),
    )
    return jax.shard_map(
        body,
        mesh=mesh,
        in_specs=placed,
        out_specs=(P(("gx", "gy"), None), P(("gx", "gy"), None)),
        check_vma=False,
    )
```

```python
import functools
import math

import jax
import jax.numpy as jnp
from jax import lax
from jax.experimental import pallas as pl
from jax.experimental.pallas import tpu as pltpu
from jax.sharding import PartitionSpec as P

D = 1536
HEADS = 24
KV_HEADS = 8
HEAD = 64
GROUP = HEADS // KV_HEADS
EXPERTS = 32
FF = 512
TOP = 8
PAGE = 16
MAXLEN = 512
NPAGE = 32
R_DEV = 16
LOCAL = 8
MOVED = 8
CAP = 48
LANES = 128
WIDE = D + LANES
PAIRS = KV_HEADS // 2
BIG = 1e30
HIDDEN_COST = 10**6
DOWN_COST = 10**6
VMEM_LIMIT = 60 * 1024 * 1024
BF = jnp.bfloat16
F32 = jnp.float32


def vmem():
    return pl.BlockSpec(memory_space=pltpu.VMEM)


def smem():
    return pl.BlockSpec(memory_space=pltpu.SMEM)


def anywhere():
    return pl.BlockSpec(memory_space=pl.ANY)


def cost(flops, moved):
    return pl.CostEstimate(flops=flops, bytes_accessed=moved, transcendentals=0)


def attend_kernel(
    me_ref, own_ref, asks_ref, table_ref, key_ref, value_ref, here_ref, reply_ref, counts, ask_ref
):
    step = pl.program_id(0)
    slots = table_ref.shape[0]
    pages = counts.shape[1] // PAGE

    @pl.when(step == 0)
    def _():
        away = slots - LOCAL
        code = asks_ref[:, D:].astype(jnp.int32)
        sender = lax.broadcasted_iota(jnp.int32, (code.shape[0], 1), 0) // MOVED
        each = away // (code.shape[0] // MOVED)
        slot = jnp.where(code[:, 2:3] == me_ref[0], sender * each + code[:, 3:4], -1)
        take = lax.broadcasted_iota(jnp.int32, (code.shape[0], away), 1) == slot
        take = jnp.where(take, 1.0, 0.0).astype(BF)
        ask_ref[:LOCAL, :] = own_ref[...].astype(F32)
        ask_ref[LOCAL:, :] = lax.dot_general(
            take, asks_ref[...], (((0,), (0,)), ((), ())), preferred_element_type=F32
        )
        lengths = ask_ref[:, D:].astype(jnp.int32)
        full, rest = lengths[:, 0:1], lengths[:, 1:2]
        table = table_ref[...]
        page = lax.broadcasted_iota(jnp.int32, (slots, pages), 1)
        whole = jnp.zeros((slots, pages), F32)
        part = jnp.zeros((slots, pages), F32)
        for p in range(NPAGE):
            hit = table[:, p : p + 1] == page
            whole += jnp.where(hit & (full > p), 1.0, 0.0)
            part += jnp.where(hit & (full == p), 1.0, 0.0)
        row = lax.broadcasted_iota(jnp.int32, (pages, pages * PAGE), 1)
        spread = jnp.where(
            row // PAGE == lax.broadcasted_iota(jnp.int32, (pages, pages * PAGE), 0), 1.0, 0.0
        ).astype(BF)
        whole = jnp.dot(whole.astype(BF), spread, preferred_element_type=F32)
        part = jnp.dot(part.astype(BF), spread, preferred_element_type=F32)
        place = lax.broadcasted_iota(jnp.int32, (slots, pages * PAGE), 1) % PAGE
        counts[...] = whole + jnp.where(place < rest, part, 0.0)

    lane = lax.broadcasted_iota(jnp.int32, (slots, LANES), 1)
    rows = []
    for j in range(2 * GROUP):
        side, chunk, half = j // GROUP, j // 2, j % 2
        at = pl.multiple_of(step * (2 * GROUP * HEAD) + chunk * LANES, LANES)
        part = ask_ref[:, pl.ds(at, LANES)] * (1.0 / math.sqrt(HEAD))
        if side != half:
            part = pltpu.roll(part, HEAD, 1)
        rows.append(jnp.where((lane < HEAD) == (side == 0), part, 0.0).astype(BF))
    heads = jnp.concatenate(rows, axis=0)
    scores = lax.dot_general(
        heads, key_ref[...], (((1,), (1,)), ((), ())), preferred_element_type=F32
    )
    count = jnp.concatenate([counts[...]] * (2 * GROUP), axis=0)
    masked = jnp.where(count > 0.0, scores, -BIG)
    highest = jnp.max(masked, axis=1, keepdims=True)
    expos = jnp.exp(masked - highest)
    totals = jnp.sum(expos * count, axis=1, keepdims=True)
    weights = (expos.astype(BF).astype(F32) * count).astype(BF)
    mixture = jnp.dot(weights, value_ref[...], preferred_element_type=F32)

    def put(at, value):
        here_ref[:, pl.ds(at, LANES)] = value[:LOCAL]
        reply_ref[:, pl.ds(at, LANES)] = value[LOCAL:]

    @pl.when(step == 0)
    def _():
        put(D, jnp.zeros((slots, LANES), F32))

    stat = jnp.concatenate([here_ref[:, D:], reply_ref[:, D:]], axis=0)
    for j in range(2 * GROUP):
        head = step * 2 * GROUP + j
        take = slice(j * slots, (j + 1) * slots)
        stat = jnp.where(lane == head, highest[take], stat)
        stat = jnp.where(lane == head + 64, totals[take], stat)
    put(D, stat)
    for chunk in range(GROUP):
        halves = []
        for half in range(2):
            j = 2 * chunk + half
            part = mixture[j * slots : (j + 1) * slots]
            if j // GROUP != half:
                part = pltpu.roll(part, HEAD, 1)
            halves.append(part)
        at = pl.multiple_of(step * (2 * GROUP * HEAD) + chunk * LANES, LANES)
        put(at, jnp.where(lane < HEAD, halves[0], halves[1]))


def attend(me, own, asks, table, pool):
    slots = table.shape[0]
    tokens = pool.shape[0]
    return pl.pallas_call(
        attend_kernel,
        grid=(PAIRS,),
        in_specs=[
            smem(),
            pl.BlockSpec(own.shape, lambda s: (0, 0)),
            pl.BlockSpec(asks.shape, lambda s: (0, 0)),
            pl.BlockSpec((slots, NPAGE), lambda s: (0, 0)),
            pl.BlockSpec((tokens, LANES), lambda s: (0, s)),
            pl.BlockSpec((tokens, LANES), lambda s: (0, PAIRS + s)),
        ],
        out_specs=[
            pl.BlockSpec((LOCAL, WIDE), lambda s: (0, 0)),
            pl.BlockSpec((slots - LOCAL, WIDE), lambda s: (0, 0)),
        ],
        out_shape=[
            jax.ShapeDtypeStruct((LOCAL, WIDE), F32),
            jax.ShapeDtypeStruct((slots - LOCAL, WIDE), F32),
        ],
        scratch_shapes=[pltpu.VMEM((slots, tokens), F32), pltpu.VMEM((slots, WIDE), F32)],
        compiler_params=pltpu.CompilerParams(vmem_limit_bytes=VMEM_LIMIT),
        cost_estimate=cost(7 * 10**9, 10**5),
        name="attend",
    )(me, own, asks, table, pool, pool)


def stream_kernel(
    pieces, chosen_ref, at_ref, query_ref, fresh_ref, here_ref, back_ref, prefill_ref,
    residual_ref, gain_ref, router_ref, routes_ref, *rest
):
    parts, rest = rest[: len(pieces)], rest[len(pieces) :]
    attended_ref, stream_ref, send_ref, tokens, out_ref, sems = rest
    copies = []
    for part, (blocks, rows) in zip(parts, pieces):
        for block in range(blocks):
            n = len(copies)
            at = pl.multiple_of(at_ref[n], 16)
            copy = pltpu.make_async_copy(
                part.at[pl.ds(block * rows, rows)], out_ref.at[pl.ds(at, rows)], sems.at[n]
            )
            copy.start()
            copies.append(copy)
    count = query_ref.shape[0]
    lane = lax.broadcasted_iota(jnp.int32, (count, LANES), 1)
    low = lane < HEAD
    picked = [back_ref[pl.ds(chosen_ref[m], 1), :] for m in range(MOVED)]
    picked = jnp.concatenate(picked, axis=0)
    mix = jnp.concatenate([here_ref[:, :D], picked[:, :D]], axis=0)
    stat = jnp.concatenate([here_ref[:, D:], picked[:, D:]], axis=0)
    fresh = fresh_ref[...].astype(F32)

    def spread(first, second, base):
        sides = []
        for half, head in enumerate((first, second)):
            part = fresh[:, base + head // 2 * LANES : base + head // 2 * LANES + LANES]
            sides.append(pltpu.roll(part, HEAD, 1) if head % 2 != half else part)
        return jnp.where(low, sides[0], sides[1])

    def both(first, second):
        return jnp.where(low, first, second)

    for chunk in range(HEADS // 2):
        first, second = 2 * chunk, 2 * chunk + 1
        span = slice(chunk * LANES, (chunk + 1) * LANES)
        keys = spread(first // GROUP, second // GROUP, 0)
        values = spread(first // GROUP, second // GROUP, KV_HEADS * HEAD)
        product = query_ref[:, span].astype(F32) * keys
        scale = 1.0 / math.sqrt(HEAD)
        own = both(
            jnp.sum(jnp.where(low, product, 0.0), axis=1, keepdims=True) * scale,
            jnp.sum(jnp.where(low, 0.0, product), axis=1, keepdims=True) * scale,
        )
        cache_max = both(stat[:, first : first + 1], stat[:, second : second + 1])
        total = both(stat[:, 64 + first : 65 + first], stat[:, 64 + second : 65 + second])
        highest = jnp.maximum(cache_max, own)
        old = jnp.exp(cache_max - highest)
        new = jnp.exp(own - highest)
        output = (old * mix[:, span] + new * values) / (old * total + new)
        tokens[:count, span] = output.astype(BF)
    attended_ref[...] = tokens[:count, :]
    tokens[count:, :] = prefill_ref[...]
    for copy in copies:
        copy.wait()
    stream = residual_ref[...].astype(F32) + jnp.dot(
        tokens[...], out_ref[...], preferred_element_type=F32
    )
    stream_ref[...] = stream
    normed = (
        stream
        * lax.rsqrt(jnp.mean(stream * stream, axis=1, keepdims=True) + 1e-06)
        * gain_ref[...].astype(F32)
    ).astype(BF)
    send_ref[:, :D] = normed
    logits = jnp.dot(normed, router_ref[...], preferred_element_type=F32)
    rows = logits.shape[0]
    expert = lax.broadcasted_iota(jnp.int32, (rows, LANES), 1)
    routes = routes_ref[...]
    named = expert == routes[:, 0:1]
    for k in range(1, TOP):
        named = named | (expert == routes[:, k : k + 1])
    masked = jnp.where(named, logits, -BIG)
    expos = jnp.where(named, jnp.exp(masked - jnp.max(masked, axis=1, keepdims=True)), 0.0)
    gates = expos / jnp.sum(expos, axis=1, keepdims=True)
    coarse = gates.astype(BF).astype(F32)
    fine = pltpu.roll(gates - coarse, 64, 1)
    send_ref[:, D:] = jnp.where(expert < 64, coarse, fine).astype(BF)


def make_stream(
    chosen, queries, fresh, here, back, prefill, residual, out_parts, gain, router, routes
):
    rows = residual.shape[0]
    count = queries.shape[0]
    at, parts, pieces, _ = out_parts
    return pl.pallas_call(
        functools.partial(stream_kernel, pieces),
        in_specs=[smem()] * 2 + [vmem()] * 9 + [pl.BlockSpec(memory_space=pltpu.HBM)] * len(parts),
        out_specs=[vmem()] * 3,
        out_shape=[
            jax.ShapeDtypeStruct((count, D), BF),
            jax.ShapeDtypeStruct((rows, D), F32),
            jax.ShapeDtypeStruct((rows, WIDE), BF),
        ],
        scratch_shapes=[
            pltpu.VMEM((rows, D), BF),
            pltpu.VMEM((D, D), BF),
            pltpu.SemaphoreType.DMA((sum(blocks for blocks, _ in pieces),)),
        ],
        compiler_params=pltpu.CompilerParams(vmem_limit_bytes=VMEM_LIMIT),
        cost_estimate=cost(8 * 10**9, 10**5),
        name="stream",
    )(chosen, at, queries, fresh, here, back, prefill, residual, gain, router, routes, *parts)


def hidden_kernel(count, place_ref, *refs):
    pieces, (mine_ref, other_ref) = refs[:count], refs[count : count + 2]
    hidden_ref, share_ref, rows_ref = refs[-3:]
    rows = pieces[0].shape[0]
    for n, piece in enumerate(pieces):
        rows_ref[n * rows : (n + 1) * rows, :] = piece[...]
    gates = rows_ref[:, D:].astype(F32)
    gates = gates + pltpu.roll(gates, 64, 1)
    lane = lax.broadcasted_iota(jnp.int32, gates.shape, 1)
    shares = []
    for side, held_ref in enumerate((mine_ref, other_ref)):
        named = jnp.where(lane == place_ref[side], gates, 0.0)
        shares.append(jnp.sum(named, axis=1, keepdims=True))
        pair = jnp.dot(rows_ref[:, :D], held_ref[...], preferred_element_type=F32)
        gate = pair[:, :FF]
        hidden_ref[:, side * FF : (side + 1) * FF] = (
            gate / (1.0 + jnp.exp(-gate)) * pair[:, FF:]
        ).astype(BF)
    share_ref[...] = jnp.where(lane == 0, shares[0], shares[1])


def make_hidden(place, pieces, mine, other, *earlier):
    rows = sum(piece.shape[0] for piece in pieces)
    return pl.pallas_call(
        functools.partial(hidden_kernel, len(pieces)),
        in_specs=[smem()] + [vmem()] * (len(pieces) + 2) + [anywhere()] * len(earlier),
        out_specs=[vmem()] * 2,
        out_shape=[
            jax.ShapeDtypeStruct((rows, 2 * FF), BF),
            jax.ShapeDtypeStruct((rows, LANES), F32),
        ],
        scratch_shapes=[pltpu.VMEM((rows, WIDE), BF)],
        compiler_params=pltpu.CompilerParams(vmem_limit_bytes=28 * 1024 * 1024),
        cost_estimate=cost(HIDDEN_COST, 10**5),
        name="hidden",
    )(place, *pieces, mine, other, *earlier)


def down_kernel(count, hidden_ref, share_ref, mine_ref, other_ref, *rest):
    total = None
    for side, held_ref in enumerate((mine_ref, other_ref)):
        made = lax.dot_general(
            hidden_ref[:, side * FF : (side + 1) * FF],
            held_ref[...],
            (((1,), (1,)), ((), ())),
            preferred_element_type=F32,
        )
        made = share_ref[:, side : side + 1] * made.astype(BF).astype(F32)
        total = made if total is None else total + made
    for n, out_ref in enumerate(rest[-count:]):
        rows = out_ref.shape[0]
        out_ref[...] = total[n * rows : (n + 1) * rows].astype(BF)


def make_down(count, hidden, share, mine, other, *earlier):
    rows = hidden.shape[0]
    return pl.pallas_call(
        functools.partial(down_kernel, count),
        in_specs=[vmem()] * 4 + [anywhere()] * len(earlier),
        out_specs=[vmem()] * count,
        out_shape=[jax.ShapeDtypeStruct((rows // count, D), BF)] * count,
        compiler_params=pltpu.CompilerParams(vmem_limit_bytes=28 * 1024 * 1024),
        cost_estimate=cost(DOWN_COST, 10**5),
        name="down",
    )(hidden, share, mine, other, *earlier)


def pack_kernel(block_ref, out_ref):
    for n in range(block_ref.shape[0] // 16):
        at = slice(n * 16, (n + 1) * 16)
        block = block_ref[at]
        for e in range(block_ref.shape[1]):
            out_ref[e, at, :] = block[:, e, :]


def pack_experts(weight, steps, *earlier):
    depth, experts, width = weight.shape
    step = depth // steps
    return pl.pallas_call(
        lambda block_ref, *rest: pack_kernel(block_ref, rest[-1]),
        grid=(steps,),
        in_specs=[pl.BlockSpec((step, experts, width), lambda s: (s, 0, 0))]
        + [anywhere()] * len(earlier),
        out_specs=pl.BlockSpec((experts, step, width), lambda s: (0, s, 0)),
        out_shape=jax.ShapeDtypeStruct((experts, depth, width), BF),
        compiler_params=pltpu.CompilerParams(vmem_limit_bytes=VMEM_LIMIT),
        cost_estimate=cost(5 * 10**9, 10**5),
        name="pack",
    )(weight, *earlier)


def swap(x, axis, how):
    return lax.ppermute(x, axis, [(i, how(i)) for i in range(lax.axis_size(axis))])


def near(j):
    return j ^ (2 if j % 2 == 0 else 4)


def beside(j):
    return j ^ 1


def far(j):
    return j ^ (4 if j % 2 == 0 else 2)


def exchange(packed):
    whole = lax.all_to_all(packed, "gx", split_axis=0, concat_axis=0, tiled=True)
    return whole.reshape(-1, packed.shape[2])


def after(x, *others):
    return lax.optimization_barrier((x, others))[0]


def small_call(kernel, name, arrays, earlier, outs, flops=10**6):
    return pl.pallas_call(
        kernel,
        in_specs=[vmem()] * len(arrays) + [anywhere()] * len(earlier),
        out_specs=[vmem()] * len(outs),
        out_shape=[jax.ShapeDtypeStruct(*out) for out in outs],
        compiler_params=pltpu.CompilerParams(vmem_limit_bytes=16 * 1024 * 1024),
        cost_estimate=cost(flops, 10**5),
        name=name,
    )(*arrays, *earlier)


def stack_kernel(count, *refs):
    out_ref, at = refs[-1], 0
    for ref in refs[:count]:
        out_ref[at : at + ref.shape[0], :] = ref[...]
        at += ref.shape[0]


def stack_rows(arrays, *earlier, flops=10**6):
    shape = (sum(x.shape[0] for x in arrays), arrays[0].shape[1])
    kernel = functools.partial(stack_kernel, len(arrays))
    return small_call(kernel, "stack", arrays, earlier, [(shape, BF)], flops)[0]


def join_kernel(keep_ref, came_ref, *rest):
    part_ref, pass_ref = rest[-2:]
    rows = part_ref.shape[0]
    total = keep_ref[...].astype(F32) + came_ref[...].astype(F32)
    part_ref[...] = total[:rows]
    pass_ref[...] = total[rows:].astype(BF)


def join(keep, came, *earlier):
    shape = (keep.shape[0] // 2, keep.shape[1])
    return small_call(join_kernel, "join", [keep, came], earlier, [(shape, F32), (shape, BF)])


def close_kernel(count, part_ref, *rest):
    total = part_ref[...]
    for ref in rest[:count]:
        total = total + ref[...].astype(F32)
    rest[-1][...] = total.astype(BF)


def close(part, came, *earlier):
    kernel = functools.partial(close_kernel, len(came))
    return small_call(kernel, "close", [part, *came], earlier, [(part.shape, BF)])[0]


def finish_kernel(stream_ref, part_ref, *rest):
    total = stream_ref[...] + part_ref[...]
    for ref in rest[:-1]:
        total = total + ref[...].astype(F32)
    rest[-1][...] = total


def swapped_experts(send, stream, pair, down):
    planes = lax.axis_size("gx")
    row, column = lax.axis_index("gx"), lax.axis_index("gy")
    place = jnp.stack([column * planes + row, beside(column) * planes + row]).astype(jnp.int32)
    across = lambda x, k: swap(x, "gx", lambda i: i ^ k)

    mine = [send] + [across(send, k) for k in range(1, planes)]
    beyond = [swap(x, "gy", near) for x in mine]
    first = [stack_rows([mine[k], beyond[k]]) for k in range(3)]
    second = [swap(x, "gy", far) for x in first]
    other_pair = swap(after(pair, second[0], *first[1:], mine[3]), "gy", beside)
    down = exchange(after(down, first[0]))
    hidden, last = {}, ()

    def inner(k, pieces):
        hidden[k] = make_hidden(place, pieces, pair, other_pair, *last)
        return (hidden[k][1],)

    last = inner(0, [first[0], second[0]])
    first.append(stack_rows([mine[3], beyond[3]], *last))
    second.append(swap(first[3], "gy", far))
    last = inner(3, [first[3]])
    last = inner(1, [first[1], second[1]])
    last = inner(2, [first[2], second[2]])
    other_down = swap(after(down, hidden[2][1], second[3]), "gy", beside)
    outer = make_hidden(place, [second[3]], pair, other_pair, *last)

    made, arrived, parts, ends = {}, {}, {}, {}
    last = ()

    def put(k):
        if k == 3:
            away = make_down(1, *outer, down, other_down)[0]
            made[k] = [*make_down(1, *hidden[k], down, other_down, away), away]
        else:
            made[k] = make_down(2, *hidden[k], down, other_down, *last)
        arrived[k] = swap(made[k][1], "gy", far)
        return (made[k][0],)

    def turn(k, *earlier):
        parts[k], passed = join(made[k][0], arrived[k], *last, *earlier)
        ends[k] = swap(passed, "gy", near)
        return (passed,)

    def leave(k, *came):
        passed = close(parts[k], [ends[k], *came], *last)
        ends[k] = across(passed, 2 if k == 2 else 1)
        return (passed,)

    last = put(3)
    last = put(2)
    last = turn(3)
    last = put(1)
    last = leave(3)
    last = turn(2)
    last = put(0)
    last = leave(2, ends[3])
    last = turn(1)
    last = leave(1)
    last = turn(0)
    arrays = [stream, parts[0], ends[0], ends[1], ends[2]]
    return small_call(finish_kernel, "finish", arrays, (), [(stream.shape, F32)])[0]


def gathered_experts(send, stream, routes, gate_up, down_proj):
    columns = lax.axis_size("gy")
    normed = send[:, :D]
    gates = send[:, D : D + EXPERTS].astype(F32) + send[:, D + 64 : D + 64 + EXPERTS].astype(F32)
    gate_weights = jnp.take_along_axis(gates, routes, axis=1)
    row_count = normed.shape[0]
    full_pair = lax.all_gather(gate_up, "gx", axis=0, tiled=True)
    full_down = lax.all_gather(down_proj, "gx", axis=0, tiled=True)
    flat_routes = routes.reshape(row_count * TOP)
    route_hits = (flat_routes[:, None] == jnp.arange(EXPERTS, dtype=jnp.int32)[None, :]).astype(
        jnp.int32
    )
    places = jnp.sum((jnp.cumsum(route_hits, axis=0) - 1) * route_hits, axis=1)
    targets = flat_routes * CAP + places
    repeated = jnp.repeat(normed, TOP, axis=0)
    experts_dev = full_pair.shape[1]
    outgoing_rows = (
        jnp.zeros((EXPERTS * CAP, D), BF)
        .at[targets]
        .set(repeated)
        .reshape(columns, experts_dev, CAP, D)
    )
    arrived = lax.all_to_all(outgoing_rows, "gy", split_axis=0, concat_axis=0, tiled=True)
    gate_pair = jnp.einsum("secd,def->secf", arrived, full_pair, preferred_element_type=F32)
    hidden = (jax.nn.silu(gate_pair[..., :FF]) * gate_pair[..., FF:]).astype(BF)
    expert_rows = jnp.einsum(
        "secf,def->secd", hidden, full_down, preferred_element_type=F32
    ).astype(BF)
    returned = lax.all_to_all(expert_rows, "gy", split_axis=0, concat_axis=0, tiled=True).reshape(
        EXPERTS * CAP, D
    )
    picked = returned[targets].astype(F32).reshape(row_count, TOP, D)
    return stream + jnp.sum(gate_weights[:, :, None] * picked, axis=1)


def gather_out(out_weight):
    columns = lax.axis_size("gy")
    share = out_weight.shape[0] // columns
    mine = lax.dynamic_slice_in_dim(out_weight, lax.axis_index("gy") * share, share, axis=0)
    whole = lax.all_gather(mine, ("gx", "gy"), axis=0, tiled=True)
    return jnp.zeros((1,), jnp.int32), [whole], ((1, whole.shape[0]),), whole


def start_out(out_weight):
    planes, columns = lax.axis_size("gx"), lax.axis_size("gy")
    share = out_weight.shape[0] // columns
    mine = lax.dynamic_slice_in_dim(out_weight, lax.axis_index("gy") * share, share, axis=0)
    return [swap(mine, "gx", lambda i, k=k: i ^ k) for k in range(1, planes)]


def swap_out(out_weight, first, asks):
    planes, columns = lax.axis_size("gx"), lax.axis_size("gy")
    row, column = lax.axis_index("gx"), lax.axis_index("gy")
    depth = out_weight.shape[0]
    share = depth // columns
    second = swap(first, "gy", near)
    both = stack_rows([first, second], asks)
    third = swap(both, "gy", far)
    parts = [first, second, third]
    near_of = lambda j: jnp.where(j % 2 == 0, j ^ 2, j ^ 4)
    far_of = lambda j: jnp.where(j % 2 == 0, j ^ 4, j ^ 2)
    at = [row * depth]
    for own in (column, column ^ 1):
        for source in (own, near_of(own), far_of(own), near_of(far_of(own))):
            at += [(row ^ k) * depth + source * share for k in range(1, planes)]
    one = (planes - 1, share)
    two = (2 * (planes - 1), share)
    at = jnp.stack(at).astype(jnp.int32)
    return at, parts, ((1, depth), one, one, two, one, one, two), both


def body(
    queries,
    new_kv,
    cache_pool,
    cache_len,
    local_pages,
    anchor,
    push_pages,
    prefill_attn,
    residual,
    out_weight,
    norm_gain,
    router,
    routes,
    gate_up,
    down_proj,
):
    columns = lax.axis_size("gy")
    slot_count = (MOVED + columns - 2) // (columns - 1)
    pool = cache_pool.reshape(-1, cache_pool.shape[2])
    planes = lax.axis_size("gx")
    swapped = columns == 8 and planes == 4 and gate_up.shape[1] == planes
    if swapped:
        out_parts = start_out(out_weight)
        pair = pack_experts(gate_up, 4)
        cache_len, anchor = after((cache_len, anchor), pair)
    matches = (anchor[:, None] == jnp.arange(columns, dtype=jnp.int32)[None, :]).astype(jnp.int32)
    earlier = jnp.sum((jnp.cumsum(matches, axis=0) - 1) * matches, axis=1)
    slots = columns * slot_count
    column = lax.axis_index("gy")
    chosen = anchor * slots + column * slot_count + earlier
    extra = jnp.stack([cache_len[LOCAL:] // PAGE, cache_len[LOCAL:] % PAGE, anchor, earlier], axis=1)
    extra = jnp.pad(extra.astype(BF), ((0, 0), (0, LANES - 4)))
    asks = lax.all_gather(
        jnp.concatenate([queries[LOCAL:], extra], axis=1), "gy", axis=0, tiled=True
    )
    extra = jnp.stack([cache_len[:LOCAL] // PAGE, cache_len[:LOCAL] % PAGE], axis=1)
    extra = jnp.pad(extra.astype(BF), ((0, 0), (0, LANES - 2)))
    own = jnp.concatenate([queries[:LOCAL], extra], axis=1)
    if swapped:

        pair = exchange(pair)
        out_parts = swap_out(out_weight, stack_rows(out_parts), asks)
        down = pack_experts(down_proj, 2, out_parts[3])
        asks = after(asks, out_parts[3], down)
    else:
        out_parts = gather_out(out_weight)
    here, reply = attend(
        column.astype(jnp.int32).reshape(1),
        own,
        asks,
        jnp.concatenate([local_pages, push_pages], axis=0),
        pool,
    )
    if swapped:
        at, parts, pieces, _ = out_parts
        others = [swap(part, "gy", beside) for part in after(parts, reply)]
        out_parts = (at, [out_weight] + parts + others, pieces, None)
    back = lax.all_gather(reply, "gy", axis=0, tiled=True)
    attended, stream, send = make_stream(
        chosen,
        queries,
        new_kv,
        here,
        back,
        prefill_attn,
        residual,
        out_parts,
        norm_gain.reshape(1, D),
        jnp.pad(router, ((0, 0), (0, LANES - EXPERTS))),
        routes,
    )
    if swapped:
        layer_out = swapped_experts(send, stream, pair, down)
    else:
        layer_out = gathered_experts(send, stream, routes, gate_up, down_proj)
    return (attended, layer_out)


def solution(mesh):
    placed = (
        P(("gx", "gy"), None),
        P(("gx", "gy"), None),
        P(("gx", "gy"), None, None),
        P(("gx", "gy")),
        P(("gx", "gy"), None),
        P(("gx", "gy")),
        P(("gx", "gy"), None),
        P(("gx", "gy"), None),
        P(("gx", "gy"), None),
        P("gx", None),
        P(),
        P(),
        P(("gx", "gy"), None),
        P("gx", "gy", None),
        P("gx", "gy", None),
    )
    return jax.shard_map(
        body,
        mesh=mesh,
        in_specs=placed,
        out_specs=(P(("gx", "gy"), None), P(("gx", "gy"), None)),
        check_vma=False,
    )
```

```python
import functools
import math

import jax
import jax.numpy as jnp
from jax import lax
from jax.experimental import pallas as pl
from jax.experimental.pallas import tpu as pltpu
from jax.sharding import PartitionSpec as P

D = 1536
HEADS = 24
KV_HEADS = 8
HEAD = 64
GROUP = HEADS // KV_HEADS
EXPERTS = 32
FF = 512
TOP = 8
PAGE = 16
MAXLEN = 512
NPAGE = 32
R_DEV = 16
LOCAL = 8
MOVED = 8
CAP = 48
LANES = 128
WIDE = D + LANES
PAIRS = KV_HEADS // 2
BIG = 1e30
HIDDEN_COST = 10**6
DOWN_COST = 10**6
VMEM_LIMIT = 60 * 1024 * 1024
BF = jnp.bfloat16
F32 = jnp.float32


def vmem():
    return pl.BlockSpec(memory_space=pltpu.VMEM)


def smem():
    return pl.BlockSpec(memory_space=pltpu.SMEM)


def anywhere():
    return pl.BlockSpec(memory_space=pl.ANY)


def cost(flops, moved):
    return pl.CostEstimate(flops=flops, bytes_accessed=moved, transcendentals=0)


def attend_kernel(
    me_ref, own_ref, asks_ref, table_ref, key_ref, value_ref, here_ref, reply_ref, counts, ask_ref
):
    step = pl.program_id(0)
    slots = table_ref.shape[0]
    pages = counts.shape[1] // PAGE

    @pl.when(step == 0)
    def _():
        away = slots - LOCAL
        code = asks_ref[:, D:].astype(jnp.int32)
        sender = lax.broadcasted_iota(jnp.int32, (code.shape[0], 1), 0) // MOVED
        each = away // (code.shape[0] // MOVED)
        slot = jnp.where(code[:, 2:3] == me_ref[0], sender * each + code[:, 3:4], -1)
        take = lax.broadcasted_iota(jnp.int32, (code.shape[0], away), 1) == slot
        take = jnp.where(take, 1.0, 0.0).astype(BF)
        ask_ref[:LOCAL, :] = own_ref[...].astype(F32)
        ask_ref[LOCAL:, :] = lax.dot_general(
            take, asks_ref[...], (((0,), (0,)), ((), ())), preferred_element_type=F32
        )
        lengths = ask_ref[:, D:].astype(jnp.int32)
        full, rest = lengths[:, 0:1], lengths[:, 1:2]
        table = table_ref[...]
        page = lax.broadcasted_iota(jnp.int32, (slots, pages), 1)
        whole = jnp.zeros((slots, pages), F32)
        part = jnp.zeros((slots, pages), F32)
        for p in range(NPAGE):
            hit = table[:, p : p + 1] == page
            whole += jnp.where(hit & (full > p), 1.0, 0.0)
            part += jnp.where(hit & (full == p), 1.0, 0.0)
        row = lax.broadcasted_iota(jnp.int32, (pages, pages * PAGE), 1)
        spread = jnp.where(
            row // PAGE == lax.broadcasted_iota(jnp.int32, (pages, pages * PAGE), 0), 1.0, 0.0
        ).astype(BF)
        whole = jnp.dot(whole.astype(BF), spread, preferred_element_type=F32)
        part = jnp.dot(part.astype(BF), spread, preferred_element_type=F32)
        place = lax.broadcasted_iota(jnp.int32, (slots, pages * PAGE), 1) % PAGE
        counts[...] = whole + jnp.where(place < rest, part, 0.0)

    lane = lax.broadcasted_iota(jnp.int32, (slots, LANES), 1)
    rows = []
    for j in range(2 * GROUP):
        side, chunk, half = j // GROUP, j // 2, j % 2
        at = pl.multiple_of(step * (2 * GROUP * HEAD) + chunk * LANES, LANES)
        part = ask_ref[:, pl.ds(at, LANES)] * (1.0 / math.sqrt(HEAD))
        if side != half:
            part = pltpu.roll(part, HEAD, 1)
        rows.append(jnp.where((lane < HEAD) == (side == 0), part, 0.0).astype(BF))
    heads = jnp.concatenate(rows, axis=0)
    scores = lax.dot_general(
        heads, key_ref[...], (((1,), (1,)), ((), ())), preferred_element_type=F32
    )
    count = jnp.concatenate([counts[...]] * (2 * GROUP), axis=0)
    masked = jnp.where(count > 0.0, scores, -BIG)
    highest = jnp.max(masked, axis=1, keepdims=True)
    expos = jnp.exp(masked - highest)
    totals = jnp.sum(expos * count, axis=1, keepdims=True)
    weights = (expos.astype(BF).astype(F32) * count).astype(BF)
    mixture = jnp.dot(weights, value_ref[...], preferred_element_type=F32)

    def put(at, value):
        here_ref[:, pl.ds(at, LANES)] = value[:LOCAL]
        reply_ref[:, pl.ds(at, LANES)] = value[LOCAL:]

    @pl.when(step == 0)
    def _():
        put(D, jnp.zeros((slots, LANES), F32))

    stat = jnp.concatenate([here_ref[:, D:], reply_ref[:, D:]], axis=0)
    for j in range(2 * GROUP):
        head = step * 2 * GROUP + j
        take = slice(j * slots, (j + 1) * slots)
        stat = jnp.where(lane == head, highest[take], stat)
        stat = jnp.where(lane == head + 64, totals[take], stat)
    put(D, stat)
    for chunk in range(GROUP):
        halves = []
        for half in range(2):
            j = 2 * chunk + half
            part = mixture[j * slots : (j + 1) * slots]
            if j // GROUP != half:
                part = pltpu.roll(part, HEAD, 1)
            halves.append(part)
        at = pl.multiple_of(step * (2 * GROUP * HEAD) + chunk * LANES, LANES)
        put(at, jnp.where(lane < HEAD, halves[0], halves[1]))


def attend(me, own, asks, table, pool):
    slots = table.shape[0]
    tokens = pool.shape[0]
    return pl.pallas_call(
        attend_kernel,
        grid=(PAIRS,),
        in_specs=[
            smem(),
            pl.BlockSpec(own.shape, lambda s: (0, 0)),
            pl.BlockSpec(asks.shape, lambda s: (0, 0)),
            pl.BlockSpec((slots, NPAGE), lambda s: (0, 0)),
            pl.BlockSpec((tokens, LANES), lambda s: (0, s)),
            pl.BlockSpec((tokens, LANES), lambda s: (0, PAIRS + s)),
        ],
        out_specs=[
            pl.BlockSpec((LOCAL, WIDE), lambda s: (0, 0)),
            pl.BlockSpec((slots - LOCAL, WIDE), lambda s: (0, 0)),
        ],
        out_shape=[
            jax.ShapeDtypeStruct((LOCAL, WIDE), F32),
            jax.ShapeDtypeStruct((slots - LOCAL, WIDE), F32),
        ],
        scratch_shapes=[pltpu.VMEM((slots, tokens), F32), pltpu.VMEM((slots, WIDE), F32)],
        compiler_params=pltpu.CompilerParams(vmem_limit_bytes=VMEM_LIMIT),
        cost_estimate=cost(7 * 10**9, 10**5),
        name="attend",
    )(me, own, asks, table, pool, pool)


def stream_kernel(
    pieces, chosen_ref, at_ref, query_ref, fresh_ref, here_ref, back_ref, prefill_ref,
    residual_ref, gain_ref, router_ref, routes_ref, *rest
):
    parts, rest = rest[: len(pieces)], rest[len(pieces) :]
    attended_ref, stream_ref, send_ref, tokens, out_ref, sems = rest
    copies = []
    for part, (blocks, rows) in zip(parts, pieces):
        for block in range(blocks):
            n = len(copies)
            at = pl.multiple_of(at_ref[n], 16)
            copy = pltpu.make_async_copy(
                part.at[pl.ds(block * rows, rows)], out_ref.at[pl.ds(at, rows)], sems.at[n]
            )
            copy.start()
            copies.append(copy)
    count = query_ref.shape[0]
    lane = lax.broadcasted_iota(jnp.int32, (count, LANES), 1)
    low = lane < HEAD
    picked = [back_ref[pl.ds(chosen_ref[m], 1), :] for m in range(MOVED)]
    picked = jnp.concatenate(picked, axis=0)
    mix = jnp.concatenate([here_ref[:, :D], picked[:, :D]], axis=0)
    stat = jnp.concatenate([here_ref[:, D:], picked[:, D:]], axis=0)
    fresh = fresh_ref[...].astype(F32)

    def spread(first, second, base):
        sides = []
        for half, head in enumerate((first, second)):
            part = fresh[:, base + head // 2 * LANES : base + head // 2 * LANES + LANES]
            sides.append(pltpu.roll(part, HEAD, 1) if head % 2 != half else part)
        return jnp.where(low, sides[0], sides[1])

    def both(first, second):
        return jnp.where(low, first, second)

    for chunk in range(HEADS // 2):
        first, second = 2 * chunk, 2 * chunk + 1
        span = slice(chunk * LANES, (chunk + 1) * LANES)
        keys = spread(first // GROUP, second // GROUP, 0)
        values = spread(first // GROUP, second // GROUP, KV_HEADS * HEAD)
        product = query_ref[:, span].astype(F32) * keys
        scale = 1.0 / math.sqrt(HEAD)
        own = both(
            jnp.sum(jnp.where(low, product, 0.0), axis=1, keepdims=True) * scale,
            jnp.sum(jnp.where(low, 0.0, product), axis=1, keepdims=True) * scale,
        )
        cache_max = both(stat[:, first : first + 1], stat[:, second : second + 1])
        total = both(stat[:, 64 + first : 65 + first], stat[:, 64 + second : 65 + second])
        highest = jnp.maximum(cache_max, own)
        old = jnp.exp(cache_max - highest)
        new = jnp.exp(own - highest)
        output = (old * mix[:, span] + new * values) / (old * total + new)
        tokens[:count, span] = output.astype(BF)
    attended_ref[...] = tokens[:count, :]
    tokens[count:, :] = prefill_ref[...]
    for copy in copies:
        copy.wait()
    stream = residual_ref[...].astype(F32) + jnp.dot(
        tokens[...], out_ref[...], preferred_element_type=F32
    )
    stream_ref[...] = stream
    normed = (
        stream
        * lax.rsqrt(jnp.mean(stream * stream, axis=1, keepdims=True) + 1e-06)
        * gain_ref[...].astype(F32)
    ).astype(BF)
    send_ref[:, :D] = normed
    logits = jnp.dot(normed, router_ref[...], preferred_element_type=F32)
    rows = logits.shape[0]
    expert = lax.broadcasted_iota(jnp.int32, (rows, LANES), 1)
    routes = routes_ref[...]
    named = expert == routes[:, 0:1]
    for k in range(1, TOP):
        named = named | (expert == routes[:, k : k + 1])
    masked = jnp.where(named, logits, -BIG)
    expos = jnp.where(named, jnp.exp(masked - jnp.max(masked, axis=1, keepdims=True)), 0.0)
    gates = expos / jnp.sum(expos, axis=1, keepdims=True)
    coarse = gates.astype(BF).astype(F32)
    fine = pltpu.roll(gates - coarse, 64, 1)
    send_ref[:, D:] = jnp.where(expert < 64, coarse, fine).astype(BF)


def make_stream(
    chosen, queries, fresh, here, back, prefill, residual, out_parts, gain, router, routes
):
    rows = residual.shape[0]
    count = queries.shape[0]
    at, parts, pieces, _ = out_parts
    return pl.pallas_call(
        functools.partial(stream_kernel, pieces),
        in_specs=[smem()] * 2 + [vmem()] * 9 + [pl.BlockSpec(memory_space=pltpu.HBM)] * len(parts),
        out_specs=[vmem()] * 3,
        out_shape=[
            jax.ShapeDtypeStruct((count, D), BF),
            jax.ShapeDtypeStruct((rows, D), F32),
            jax.ShapeDtypeStruct((rows, WIDE), BF),
        ],
        scratch_shapes=[
            pltpu.VMEM((rows, D), BF),
            pltpu.VMEM((D, D), BF),
            pltpu.SemaphoreType.DMA((sum(blocks for blocks, _ in pieces),)),
        ],
        compiler_params=pltpu.CompilerParams(vmem_limit_bytes=VMEM_LIMIT),
        cost_estimate=cost(8 * 10**9, 10**5),
        name="stream",
    )(chosen, at, queries, fresh, here, back, prefill, residual, gain, router, routes, *parts)


def hidden_kernel(count, place_ref, *refs):
    pieces, (mine_ref, other_ref) = refs[:count], refs[count : count + 2]
    hidden_ref, share_ref, rows_ref = refs[-3:]
    rows = pieces[0].shape[0]
    for n, piece in enumerate(pieces):
        rows_ref[n * rows : (n + 1) * rows, :] = piece[...]
    gates = rows_ref[:, D:].astype(F32)
    gates = gates + pltpu.roll(gates, 64, 1)
    lane = lax.broadcasted_iota(jnp.int32, gates.shape, 1)
    shares = []
    for side, held_ref in enumerate((mine_ref, other_ref)):
        named = jnp.where(lane == place_ref[side], gates, 0.0)
        shares.append(jnp.sum(named, axis=1, keepdims=True))
        pair = jnp.dot(rows_ref[:, :D], held_ref[...], preferred_element_type=F32)
        gate = pair[:, :FF]
        hidden_ref[:, side * FF : (side + 1) * FF] = (
            gate / (1.0 + jnp.exp(-gate)) * pair[:, FF:]
        ).astype(BF)
    share_ref[...] = jnp.where(lane == 0, shares[0], shares[1])


def make_hidden(place, pieces, mine, other, *earlier):
    rows = sum(piece.shape[0] for piece in pieces)
    return pl.pallas_call(
        functools.partial(hidden_kernel, len(pieces)),
        in_specs=[smem()] + [vmem()] * (len(pieces) + 2) + [anywhere()] * len(earlier),
        out_specs=[vmem()] * 2,
        out_shape=[
            jax.ShapeDtypeStruct((rows, 2 * FF), BF),
            jax.ShapeDtypeStruct((rows, LANES), F32),
        ],
        scratch_shapes=[pltpu.VMEM((rows, WIDE), BF)],
        compiler_params=pltpu.CompilerParams(vmem_limit_bytes=28 * 1024 * 1024),
        cost_estimate=cost(HIDDEN_COST, 10**5),
        name="hidden",
    )(place, *pieces, mine, other, *earlier)


def down_kernel(count, hidden_ref, share_ref, mine_ref, other_ref, *rest):
    total = None
    for side, held_ref in enumerate((mine_ref, other_ref)):
        made = lax.dot_general(
            hidden_ref[:, side * FF : (side + 1) * FF],
            held_ref[...],
            (((1,), (1,)), ((), ())),
            preferred_element_type=F32,
        )
        made = share_ref[:, side : side + 1] * made.astype(BF).astype(F32)
        total = made if total is None else total + made
    for n, out_ref in enumerate(rest[-count:]):
        rows = out_ref.shape[0]
        out_ref[...] = total[n * rows : (n + 1) * rows].astype(BF)


def make_down(count, hidden, share, mine, other, *earlier):
    rows = hidden.shape[0]
    return pl.pallas_call(
        functools.partial(down_kernel, count),
        in_specs=[vmem()] * 4 + [anywhere()] * len(earlier),
        out_specs=[vmem()] * count,
        out_shape=[jax.ShapeDtypeStruct((rows // count, D), BF)] * count,
        compiler_params=pltpu.CompilerParams(vmem_limit_bytes=28 * 1024 * 1024),
        cost_estimate=cost(DOWN_COST, 10**5),
        name="down",
    )(hidden, share, mine, other, *earlier)


def pack_kernel(block_ref, out_ref):
    for n in range(block_ref.shape[0] // 16):
        at = slice(n * 16, (n + 1) * 16)
        block = block_ref[at]
        for e in range(block_ref.shape[1]):
            out_ref[e, at, :] = block[:, e, :]


def pack_experts(weight, steps, *earlier):
    depth, experts, width = weight.shape
    step = depth // steps
    return pl.pallas_call(
        lambda block_ref, *rest: pack_kernel(block_ref, rest[-1]),
        grid=(steps,),
        in_specs=[pl.BlockSpec((step, experts, width), lambda s: (s, 0, 0))]
        + [anywhere()] * len(earlier),
        out_specs=pl.BlockSpec((experts, step, width), lambda s: (0, s, 0)),
        out_shape=jax.ShapeDtypeStruct((experts, depth, width), BF),
        compiler_params=pltpu.CompilerParams(vmem_limit_bytes=VMEM_LIMIT),
        cost_estimate=cost(5 * 10**9, 10**5),
        name="pack",
    )(weight, *earlier)


def swap(x, axis, how):
    return lax.ppermute(x, axis, [(i, how(i)) for i in range(lax.axis_size(axis))])


def near(j):
    return j ^ (2 if j % 2 == 0 else 4)


def beside(j):
    return j ^ 1


def far(j):
    return j ^ (4 if j % 2 == 0 else 2)


def exchange(packed):
    whole = lax.all_to_all(packed, "gx", split_axis=0, concat_axis=0, tiled=True)
    return whole.reshape(-1, packed.shape[2])


def after(x, *others):
    return lax.optimization_barrier((x, others))[0]


def small_call(kernel, name, arrays, earlier, outs, flops=10**6):
    return pl.pallas_call(
        kernel,
        in_specs=[vmem()] * len(arrays) + [anywhere()] * len(earlier),
        out_specs=[vmem()] * len(outs),
        out_shape=[jax.ShapeDtypeStruct(*out) for out in outs],
        compiler_params=pltpu.CompilerParams(vmem_limit_bytes=16 * 1024 * 1024),
        cost_estimate=cost(flops, 10**5),
        name=name,
    )(*arrays, *earlier)


def stack_kernel(count, *refs):
    out_ref, at = refs[-1], 0
    for ref in refs[:count]:
        out_ref[at : at + ref.shape[0], :] = ref[...]
        at += ref.shape[0]


def stack_rows(arrays, *earlier, flops=10**6):
    shape = (sum(x.shape[0] for x in arrays), arrays[0].shape[1])
    kernel = functools.partial(stack_kernel, len(arrays))
    return small_call(kernel, "stack", arrays, earlier, [(shape, BF)], flops)[0]


def join_kernel(keep_ref, came_ref, *rest):
    part_ref, pass_ref = rest[-2:]
    rows = part_ref.shape[0]
    total = keep_ref[...].astype(F32) + came_ref[...].astype(F32)
    part_ref[...] = total[:rows]
    pass_ref[...] = total[rows:].astype(BF)


def join(keep, came, *earlier):
    shape = (keep.shape[0] // 2, keep.shape[1])
    return small_call(join_kernel, "join", [keep, came], earlier, [(shape, F32), (shape, BF)])


def close_kernel(want, core_ref, part_ref, came_ref, *rest):
    total = part_ref[...] + came_ref[...].astype(F32)
    if want is not None:
        total = total + jnp.where(core_ref[0] == want, rest[0][...].astype(F32), 0.0)
    rest[-1][...] = total.astype(BF)


def close(want, core, part, came, earlier):
    arrays = [part, *came]
    return pl.pallas_call(
        functools.partial(close_kernel, want),
        in_specs=[smem()] + [vmem()] * len(arrays) + [anywhere()] * len(earlier),
        out_specs=vmem(),
        out_shape=jax.ShapeDtypeStruct(part.shape, BF),
        compiler_params=pltpu.CompilerParams(vmem_limit_bytes=16 * 1024 * 1024),
        cost_estimate=cost(10**6, 10**5),
        name="close",
    )(core, *arrays, *earlier)


def finish_kernel(stream_ref, part_ref, *rest):
    total = stream_ref[...] + part_ref[...]
    for ref in rest[:-1]:
        total = total + ref[...].astype(F32)
    rest[-1][...] = total


def swapped_experts(send, stream, pair, down):
    planes = lax.axis_size("gx")
    columns = lax.axis_size("gy")
    row, column = lax.axis_index("gx"), lax.axis_index("gy")
    place = jnp.stack([column * planes + row, beside(column) * planes + row]).astype(jnp.int32)
    core = (column % 2).astype(jnp.int32).reshape(1)

    def across(x, k):
        even, odd = ((0, 0), (1, 2), (2, 1), (3, 3))[k]
        pairs = [
            (i * columns + j, (i ^ (odd if j % 2 else even)) * columns + j)
            for i in range(planes)
            for j in range(columns)
        ]
        return lax.ppermute(x, ("gx", "gy"), pairs)


    mine = [send] + [across(send, k) for k in range(1, planes)]
    beyond = [swap(x, "gy", near) for x in mine]
    first = [stack_rows([mine[k], beyond[k]]) for k in range(3)]
    second = [swap(x, "gy", far) for x in first]
    other_pair = swap(after(pair, second[0], *first[1:], mine[3]), "gy", beside)
    down = exchange(after(down, first[0]))
    hidden, last = {}, ()

    def inner(k, pieces):
        hidden[k] = make_hidden(place, pieces, pair, other_pair, *last)
        return (hidden[k][1],)

    last = inner(0, [first[0], second[0]])
    first.append(stack_rows([mine[3], beyond[3]], *last))
    second.append(swap(first[3], "gy", far))
    last = inner(3, [first[3]])
    last = inner(1, [first[1], second[1]])
    last = inner(2, [first[2], second[2]])
    other_down = swap(after(down, hidden[2][1], second[3]), "gy", beside)
    outer = make_hidden(place, [second[3]], pair, other_pair, *last)

    made, arrived, parts, ends = {}, {}, {}, {}
    last = ()

    def put(k):
        if k == 3:
            away = make_down(1, *outer, down, other_down)[0]
            made[k] = [*make_down(1, *hidden[k], down, other_down, away), away]
        else:
            made[k] = make_down(2, *hidden[k], down, other_down, *last)
        arrived[k] = swap(made[k][1], "gy", far)
        return (made[k][0],)

    def turn(k, *earlier):
        parts[k], passed = join(made[k][0], arrived[k], *last, *earlier)
        ends[k] = swap(passed, "gy", near)
        return (passed,)

    def leave(k, *came):
        want = {1: 1, 2: 0}.get(k)
        passed = close(want, core, parts[k], [ends[k], *came], last)
        ends[k] = swap(passed, "gx", lambda i: i ^ 1) if k == 3 else across(passed, k)
        return (passed,)

    last = put(3)
    last = put(2)
    last = turn(3)
    last = put(1)
    last = leave(3)
    last = turn(2)
    last = put(0)
    last = leave(2, ends[3])
    last = turn(1)
    last = leave(1, ends[3])
    last = turn(0)
    arrays = [stream, parts[0], ends[0], ends[1], ends[2]]
    return small_call(finish_kernel, "finish", arrays, (), [(stream.shape, F32)])[0]


def gathered_experts(send, stream, routes, gate_up, down_proj):
    columns = lax.axis_size("gy")
    normed = send[:, :D]
    gates = send[:, D : D + EXPERTS].astype(F32) + send[:, D + 64 : D + 64 + EXPERTS].astype(F32)
    gate_weights = jnp.take_along_axis(gates, routes, axis=1)
    row_count = normed.shape[0]
    full_pair = lax.all_gather(gate_up, "gx", axis=0, tiled=True)
    full_down = lax.all_gather(down_proj, "gx", axis=0, tiled=True)
    flat_routes = routes.reshape(row_count * TOP)
    route_hits = (flat_routes[:, None] == jnp.arange(EXPERTS, dtype=jnp.int32)[None, :]).astype(
        jnp.int32
    )
    places = jnp.sum((jnp.cumsum(route_hits, axis=0) - 1) * route_hits, axis=1)
    targets = flat_routes * CAP + places
    repeated = jnp.repeat(normed, TOP, axis=0)
    experts_dev = full_pair.shape[1]
    outgoing_rows = (
        jnp.zeros((EXPERTS * CAP, D), BF)
        .at[targets]
        .set(repeated)
        .reshape(columns, experts_dev, CAP, D)
    )
    arrived = lax.all_to_all(outgoing_rows, "gy", split_axis=0, concat_axis=0, tiled=True)
    gate_pair = jnp.einsum("secd,def->secf", arrived, full_pair, preferred_element_type=F32)
    hidden = (jax.nn.silu(gate_pair[..., :FF]) * gate_pair[..., FF:]).astype(BF)
    expert_rows = jnp.einsum(
        "secf,def->secd", hidden, full_down, preferred_element_type=F32
    ).astype(BF)
    returned = lax.all_to_all(expert_rows, "gy", split_axis=0, concat_axis=0, tiled=True).reshape(
        EXPERTS * CAP, D
    )
    picked = returned[targets].astype(F32).reshape(row_count, TOP, D)
    return stream + jnp.sum(gate_weights[:, :, None] * picked, axis=1)


def gather_out(out_weight):
    columns = lax.axis_size("gy")
    share = out_weight.shape[0] // columns
    mine = lax.dynamic_slice_in_dim(out_weight, lax.axis_index("gy") * share, share, axis=0)
    whole = lax.all_gather(mine, ("gx", "gy"), axis=0, tiled=True)
    return jnp.zeros((1,), jnp.int32), [whole], ((1, whole.shape[0]),), whole


def start_out(out_weight):
    planes, columns = lax.axis_size("gx"), lax.axis_size("gy")
    share = out_weight.shape[0] // columns
    mine = lax.dynamic_slice_in_dim(out_weight, lax.axis_index("gy") * share, share, axis=0)
    return [swap(mine, "gx", lambda i, k=k: i ^ k) for k in range(1, planes)]


def swap_out(out_weight, first, asks):
    planes, columns = lax.axis_size("gx"), lax.axis_size("gy")
    row, column = lax.axis_index("gx"), lax.axis_index("gy")
    depth = out_weight.shape[0]
    share = depth // columns
    second = swap(first, "gy", near)
    both = stack_rows([first, second], asks)
    third = swap(both, "gy", far)
    parts = [first, second, third]
    near_of = lambda j: jnp.where(j % 2 == 0, j ^ 2, j ^ 4)
    far_of = lambda j: jnp.where(j % 2 == 0, j ^ 4, j ^ 2)
    at = [row * depth]
    for own in (column, column ^ 1):
        for source in (own, near_of(own), far_of(own), near_of(far_of(own))):
            at += [(row ^ k) * depth + source * share for k in range(1, planes)]
    one = (planes - 1, share)
    two = (2 * (planes - 1), share)
    at = jnp.stack(at).astype(jnp.int32)
    return at, parts, ((1, depth), one, one, two, one, one, two), both


def body(
    queries,
    new_kv,
    cache_pool,
    cache_len,
    local_pages,
    anchor,
    push_pages,
    prefill_attn,
    residual,
    out_weight,
    norm_gain,
    router,
    routes,
    gate_up,
    down_proj,
):
    columns = lax.axis_size("gy")
    slot_count = (MOVED + columns - 2) // (columns - 1)
    pool = cache_pool.reshape(-1, cache_pool.shape[2])
    planes = lax.axis_size("gx")
    swapped = columns == 8 and planes == 4 and gate_up.shape[1] == planes
    if swapped:
        out_parts = start_out(out_weight)
        pair = pack_experts(gate_up, 4)
        cache_len, anchor = after((cache_len, anchor), pair)
    matches = (anchor[:, None] == jnp.arange(columns, dtype=jnp.int32)[None, :]).astype(jnp.int32)
    earlier = jnp.sum((jnp.cumsum(matches, axis=0) - 1) * matches, axis=1)
    slots = columns * slot_count
    column = lax.axis_index("gy")
    chosen = anchor * slots + column * slot_count + earlier
    extra = jnp.stack([cache_len[LOCAL:] // PAGE, cache_len[LOCAL:] % PAGE, anchor, earlier], axis=1)
    extra = jnp.pad(extra.astype(BF), ((0, 0), (0, LANES - 4)))
    asks = lax.all_gather(
        jnp.concatenate([queries[LOCAL:], extra], axis=1), "gy", axis=0, tiled=True
    )
    extra = jnp.stack([cache_len[:LOCAL] // PAGE, cache_len[:LOCAL] % PAGE], axis=1)
    extra = jnp.pad(extra.astype(BF), ((0, 0), (0, LANES - 2)))
    own = jnp.concatenate([queries[:LOCAL], extra], axis=1)
    if swapped:

        pair = exchange(pair)
        out_parts = swap_out(out_weight, stack_rows(out_parts), asks)
        down = pack_experts(down_proj, 2, out_parts[3])
        asks = after(asks, out_parts[3], down)
    else:
        out_parts = gather_out(out_weight)
    here, reply = attend(
        column.astype(jnp.int32).reshape(1),
        own,
        asks,
        jnp.concatenate([local_pages, push_pages], axis=0),
        pool,
    )
    if swapped:
        at, parts, pieces, _ = out_parts
        others = [swap(part, "gy", beside) for part in after(parts, reply)]
        out_parts = (at, [out_weight] + parts + others, pieces, None)
    back = lax.all_gather(reply, "gy", axis=0, tiled=True)
    attended, stream, send = make_stream(
        chosen,
        queries,
        new_kv,
        here,
        back,
        prefill_attn,
        residual,
        out_parts,
        norm_gain.reshape(1, D),
        jnp.pad(router, ((0, 0), (0, LANES - EXPERTS))),
        routes,
    )
    if swapped:
        layer_out = swapped_experts(send, stream, pair, down)
    else:
        layer_out = gathered_experts(send, stream, routes, gate_up, down_proj)
    return (attended, layer_out)


def solution(mesh):
    placed = (
        P(("gx", "gy"), None),
        P(("gx", "gy"), None),
        P(("gx", "gy"), None, None),
        P(("gx", "gy")),
        P(("gx", "gy"), None),
        P(("gx", "gy")),
        P(("gx", "gy"), None),
        P(("gx", "gy"), None),
        P(("gx", "gy"), None),
        P("gx", None),
        P(),
        P(),
        P(("gx", "gy"), None),
        P("gx", "gy", None),
        P("gx", "gy", None),
    )
    return jax.shard_map(
        body,
        mesh=mesh,
        in_specs=placed,
        out_specs=(P(("gx", "gy"), None), P(("gx", "gy"), None)),
        check_vma=False,
    )
```

```python
import functools
import math

import jax
import jax.numpy as jnp
from jax import lax
from jax.experimental import pallas as pl
from jax.experimental.pallas import tpu as pltpu
from jax.sharding import PartitionSpec as P

D = 1536
HEADS = 24
KV_HEADS = 8
HEAD = 64
GROUP = HEADS // KV_HEADS
EXPERTS = 32
FF = 512
TOP = 8
PAGE = 16
MAXLEN = 512
NPAGE = 32
R_DEV = 16
LOCAL = 8
MOVED = 8
CAP = 48
LANES = 128
WIDE = D + LANES
PAIRS = KV_HEADS // 2
BIG = 1e30
HIDDEN_COST = 10**6
DOWN_COST = 10**6
VMEM_LIMIT = 60 * 1024 * 1024
BF = jnp.bfloat16
F32 = jnp.float32


def vmem():
    return pl.BlockSpec(memory_space=pltpu.VMEM)


def smem():
    return pl.BlockSpec(memory_space=pltpu.SMEM)


def anywhere():
    return pl.BlockSpec(memory_space=pl.ANY)


def cost(flops, moved):
    return pl.CostEstimate(flops=flops, bytes_accessed=moved, transcendentals=0)


def attend_kernel(
    me_ref, own_ref, asks_ref, table_ref, key_ref, value_ref, here_ref, reply_ref, counts, ask_ref
):
    step = pl.program_id(0)
    slots = table_ref.shape[0]
    pages = counts.shape[1] // PAGE

    @pl.when(step == 0)
    def _():
        away = slots - LOCAL
        code = asks_ref[:, D:].astype(jnp.int32)
        sender = lax.broadcasted_iota(jnp.int32, (code.shape[0], 1), 0) // MOVED
        each = away // (code.shape[0] // MOVED)
        slot = jnp.where(code[:, 2:3] == me_ref[0], sender * each + code[:, 3:4], -1)
        take = lax.broadcasted_iota(jnp.int32, (code.shape[0], away), 1) == slot
        take = jnp.where(take, 1.0, 0.0).astype(BF)
        ask_ref[:LOCAL, :] = own_ref[...].astype(F32)
        ask_ref[LOCAL:, :] = lax.dot_general(
            take, asks_ref[...], (((0,), (0,)), ((), ())), preferred_element_type=F32
        )
        lengths = ask_ref[:, D:].astype(jnp.int32)
        full, rest = lengths[:, 0:1], lengths[:, 1:2]
        table = table_ref[...]
        page = lax.broadcasted_iota(jnp.int32, (slots, pages), 1)
        whole = jnp.zeros((slots, pages), F32)
        part = jnp.zeros((slots, pages), F32)
        for p in range(NPAGE):
            hit = table[:, p : p + 1] == page
            whole += jnp.where(hit & (full > p), 1.0, 0.0)
            part += jnp.where(hit & (full == p), 1.0, 0.0)
        row = lax.broadcasted_iota(jnp.int32, (pages, pages * PAGE), 1)
        spread = jnp.where(
            row // PAGE == lax.broadcasted_iota(jnp.int32, (pages, pages * PAGE), 0), 1.0, 0.0
        ).astype(BF)
        whole = jnp.dot(whole.astype(BF), spread, preferred_element_type=F32)
        part = jnp.dot(part.astype(BF), spread, preferred_element_type=F32)
        place = lax.broadcasted_iota(jnp.int32, (slots, pages * PAGE), 1) % PAGE
        counts[...] = whole + jnp.where(place < rest, part, 0.0)

    lane = lax.broadcasted_iota(jnp.int32, (slots, LANES), 1)
    rows = []
    for j in range(2 * GROUP):
        side, chunk, half = j // GROUP, j // 2, j % 2
        at = pl.multiple_of(step * (2 * GROUP * HEAD) + chunk * LANES, LANES)
        part = ask_ref[:, pl.ds(at, LANES)] * (1.0 / math.sqrt(HEAD))
        if side != half:
            part = pltpu.roll(part, HEAD, 1)
        rows.append(jnp.where((lane < HEAD) == (side == 0), part, 0.0).astype(BF))
    heads = jnp.concatenate(rows, axis=0)
    scores = lax.dot_general(
        heads, key_ref[...], (((1,), (1,)), ((), ())), preferred_element_type=F32
    )
    count = jnp.concatenate([counts[...]] * (2 * GROUP), axis=0)
    masked = jnp.where(count > 0.0, scores, -BIG)
    highest = jnp.max(masked, axis=1, keepdims=True)
    expos = jnp.exp(masked - highest)
    totals = jnp.sum(expos * count, axis=1, keepdims=True)
    weights = (expos.astype(BF).astype(F32) * count).astype(BF)
    mixture = jnp.dot(weights, value_ref[...], preferred_element_type=F32)

    def put(at, value):
        here_ref[:, pl.ds(at, LANES)] = value[:LOCAL]
        reply_ref[:, pl.ds(at, LANES)] = value[LOCAL:]

    @pl.when(step == 0)
    def _():
        put(D, jnp.zeros((slots, LANES), F32))

    stat = jnp.concatenate([here_ref[:, D:], reply_ref[:, D:]], axis=0)
    for j in range(2 * GROUP):
        head = step * 2 * GROUP + j
        take = slice(j * slots, (j + 1) * slots)
        stat = jnp.where(lane == head, highest[take], stat)
        stat = jnp.where(lane == head + 64, totals[take], stat)
    put(D, stat)
    for chunk in range(GROUP):
        halves = []
        for half in range(2):
            j = 2 * chunk + half
            part = mixture[j * slots : (j + 1) * slots]
            if j // GROUP != half:
                part = pltpu.roll(part, HEAD, 1)
            halves.append(part)
        at = pl.multiple_of(step * (2 * GROUP * HEAD) + chunk * LANES, LANES)
        put(at, jnp.where(lane < HEAD, halves[0], halves[1]))


def attend(me, own, asks, table, pool):
    slots = table.shape[0]
    tokens = pool.shape[0]
    return pl.pallas_call(
        attend_kernel,
        grid=(PAIRS,),
        in_specs=[
            smem(),
            pl.BlockSpec(own.shape, lambda s: (0, 0)),
            pl.BlockSpec(asks.shape, lambda s: (0, 0)),
            pl.BlockSpec((slots, NPAGE), lambda s: (0, 0)),
            pl.BlockSpec((tokens, LANES), lambda s: (0, s)),
            pl.BlockSpec((tokens, LANES), lambda s: (0, PAIRS + s)),
        ],
        out_specs=[
            pl.BlockSpec((LOCAL, WIDE), lambda s: (0, 0)),
            pl.BlockSpec((slots - LOCAL, WIDE), lambda s: (0, 0)),
        ],
        out_shape=[
            jax.ShapeDtypeStruct((LOCAL, WIDE), F32),
            jax.ShapeDtypeStruct((slots - LOCAL, WIDE), F32),
        ],
        scratch_shapes=[pltpu.VMEM((slots, tokens), F32), pltpu.VMEM((slots, WIDE), F32)],
        compiler_params=pltpu.CompilerParams(vmem_limit_bytes=VMEM_LIMIT),
        cost_estimate=cost(7 * 10**9, 10**5),
        name="attend",
    )(me, own, asks, table, pool, pool)


def stream_kernel(
    pieces, chosen_ref, at_ref, query_ref, fresh_ref, here_ref, back_ref, prefill_ref,
    residual_ref, gain_ref, router_ref, routes_ref, *rest
):
    parts, rest = rest[: len(pieces)], rest[len(pieces) :]
    attended_ref, stream_ref, send_ref, tokens, out_ref, sems = rest
    copies = []
    for part, (blocks, rows) in zip(parts, pieces):
        for block in range(blocks):
            n = len(copies)
            at = pl.multiple_of(at_ref[n], 16)
            copy = pltpu.make_async_copy(
                part.at[pl.ds(block * rows, rows)], out_ref.at[pl.ds(at, rows)], sems.at[n]
            )
            copy.start()
            copies.append(copy)
    count = query_ref.shape[0]
    lane = lax.broadcasted_iota(jnp.int32, (count, LANES), 1)
    low = lane < HEAD
    picked = [back_ref[pl.ds(chosen_ref[m], 1), :] for m in range(MOVED)]
    picked = jnp.concatenate(picked, axis=0)
    mix = jnp.concatenate([here_ref[:, :D], picked[:, :D]], axis=0)
    stat = jnp.concatenate([here_ref[:, D:], picked[:, D:]], axis=0)
    fresh = fresh_ref[...].astype(F32)

    def spread(first, second, base):
        sides = []
        for half, head in enumerate((first, second)):
            part = fresh[:, base + head // 2 * LANES : base + head // 2 * LANES + LANES]
            sides.append(pltpu.roll(part, HEAD, 1) if head % 2 != half else part)
        return jnp.where(low, sides[0], sides[1])

    def both(first, second):
        return jnp.where(low, first, second)

    for chunk in range(HEADS // 2):
        first, second = 2 * chunk, 2 * chunk + 1
        span = slice(chunk * LANES, (chunk + 1) * LANES)
        keys = spread(first // GROUP, second // GROUP, 0)
        values = spread(first // GROUP, second // GROUP, KV_HEADS * HEAD)
        product = query_ref[:, span].astype(F32) * keys
        scale = 1.0 / math.sqrt(HEAD)
        own = both(
            jnp.sum(jnp.where(low, product, 0.0), axis=1, keepdims=True) * scale,
            jnp.sum(jnp.where(low, 0.0, product), axis=1, keepdims=True) * scale,
        )
        cache_max = both(stat[:, first : first + 1], stat[:, second : second + 1])
        total = both(stat[:, 64 + first : 65 + first], stat[:, 64 + second : 65 + second])
        highest = jnp.maximum(cache_max, own)
        old = jnp.exp(cache_max - highest)
        new = jnp.exp(own - highest)
        output = (old * mix[:, span] + new * values) / (old * total + new)
        tokens[:count, span] = output.astype(BF)
    attended_ref[...] = tokens[:count, :]
    tokens[count:, :] = prefill_ref[...]
    for copy in copies:
        copy.wait()
    stream = residual_ref[...].astype(F32) + jnp.dot(
        tokens[...], out_ref[...], preferred_element_type=F32
    )
    stream_ref[...] = stream
    normed = (
        stream
        * lax.rsqrt(jnp.mean(stream * stream, axis=1, keepdims=True) + 1e-06)
        * gain_ref[...].astype(F32)
    ).astype(BF)
    send_ref[:, :D] = normed
    logits = jnp.dot(normed, router_ref[...], preferred_element_type=F32)
    rows = logits.shape[0]
    expert = lax.broadcasted_iota(jnp.int32, (rows, LANES), 1)
    routes = routes_ref[...]
    named = expert == routes[:, 0:1]
    for k in range(1, TOP):
        named = named | (expert == routes[:, k : k + 1])
    masked = jnp.where(named, logits, -BIG)
    expos = jnp.where(named, jnp.exp(masked - jnp.max(masked, axis=1, keepdims=True)), 0.0)
    gates = expos / jnp.sum(expos, axis=1, keepdims=True)
    coarse = gates.astype(BF).astype(F32)
    fine = pltpu.roll(gates - coarse, 64, 1)
    send_ref[:, D:] = jnp.where(expert < 64, coarse, fine).astype(BF)


def make_stream(
    chosen, queries, fresh, here, back, prefill, residual, out_parts, gain, router, routes
):
    rows = residual.shape[0]
    count = queries.shape[0]
    at, parts, pieces, _ = out_parts
    return pl.pallas_call(
        functools.partial(stream_kernel, pieces),
        in_specs=[smem()] * 2 + [vmem()] * 9 + [pl.BlockSpec(memory_space=pltpu.HBM)] * len(parts),
        out_specs=[vmem()] * 3,
        out_shape=[
            jax.ShapeDtypeStruct((count, D), BF),
            jax.ShapeDtypeStruct((rows, D), F32),
            jax.ShapeDtypeStruct((rows, WIDE), BF),
        ],
        scratch_shapes=[
            pltpu.VMEM((rows, D), BF),
            pltpu.VMEM((D, D), BF),
            pltpu.SemaphoreType.DMA((sum(blocks for blocks, _ in pieces),)),
        ],
        compiler_params=pltpu.CompilerParams(vmem_limit_bytes=VMEM_LIMIT),
        cost_estimate=cost(8 * 10**9, 10**5),
        name="stream",
    )(chosen, at, queries, fresh, here, back, prefill, residual, gain, router, routes, *parts)


def hidden_kernel(count, place_ref, *refs):
    pieces, (mine_ref, other_ref) = refs[:count], refs[count : count + 2]
    hidden_ref, share_ref, rows_ref = refs[-3:]
    rows = pieces[0].shape[0]
    for n, piece in enumerate(pieces):
        rows_ref[n * rows : (n + 1) * rows, :] = piece[...]
    gates = rows_ref[:, D:].astype(F32)
    gates = gates + pltpu.roll(gates, 64, 1)
    lane = lax.broadcasted_iota(jnp.int32, gates.shape, 1)
    shares = []
    for side, held_ref in enumerate((mine_ref, other_ref)):
        named = jnp.where(lane == place_ref[side], gates, 0.0)
        shares.append(jnp.sum(named, axis=1, keepdims=True))
        pair = jnp.dot(rows_ref[:, :D], held_ref[...], preferred_element_type=F32)
        gate = pair[:, :FF]
        hidden_ref[:, side * FF : (side + 1) * FF] = (
            gate / (1.0 + jnp.exp(-gate)) * pair[:, FF:]
        ).astype(BF)
    share_ref[...] = jnp.where(lane == 0, shares[0], shares[1])


def make_hidden(place, pieces, mine, other, *earlier):
    rows = sum(piece.shape[0] for piece in pieces)
    return pl.pallas_call(
        functools.partial(hidden_kernel, len(pieces)),
        in_specs=[smem()] + [vmem()] * (len(pieces) + 2) + [anywhere()] * len(earlier),
        out_specs=[vmem()] * 2,
        out_shape=[
            jax.ShapeDtypeStruct((rows, 2 * FF), BF),
            jax.ShapeDtypeStruct((rows, LANES), F32),
        ],
        scratch_shapes=[pltpu.VMEM((rows, WIDE), BF)],
        compiler_params=pltpu.CompilerParams(vmem_limit_bytes=28 * 1024 * 1024),
        cost_estimate=cost(HIDDEN_COST, 10**5),
        name="hidden",
    )(place, *pieces, mine, other, *earlier)


def down_kernel(count, hidden_ref, share_ref, mine_ref, other_ref, *rest):
    total = None
    for side, held_ref in enumerate((mine_ref, other_ref)):
        made = lax.dot_general(
            hidden_ref[:, side * FF : (side + 1) * FF],
            held_ref[...],
            (((1,), (1,)), ((), ())),
            preferred_element_type=F32,
        )
        made = share_ref[:, side : side + 1] * made.astype(BF).astype(F32)
        total = made if total is None else total + made
    for n, out_ref in enumerate(rest[-count:]):
        rows = out_ref.shape[0]
        out_ref[...] = total[n * rows : (n + 1) * rows].astype(BF)


def make_down(count, hidden, share, mine, other, *earlier):
    rows = hidden.shape[0]
    return pl.pallas_call(
        functools.partial(down_kernel, count),
        in_specs=[vmem()] * 4 + [anywhere()] * len(earlier),
        out_specs=[vmem()] * count,
        out_shape=[jax.ShapeDtypeStruct((rows // count, D), BF)] * count,
        compiler_params=pltpu.CompilerParams(vmem_limit_bytes=28 * 1024 * 1024),
        cost_estimate=cost(DOWN_COST, 10**5),
        name="down",
    )(hidden, share, mine, other, *earlier)


def pack_kernel(block_ref, out_ref):
    for n in range(block_ref.shape[0] // 16):
        at = slice(n * 16, (n + 1) * 16)
        block = block_ref[at]
        for e in range(block_ref.shape[1]):
            out_ref[e, at, :] = block[:, e, :]


def pack_experts(weight, steps, *earlier):
    depth, experts, width = weight.shape
    step = depth // steps
    return pl.pallas_call(
        lambda block_ref, *rest: pack_kernel(block_ref, rest[-1]),
        grid=(steps,),
        in_specs=[pl.BlockSpec((step, experts, width), lambda s: (s, 0, 0))]
        + [anywhere()] * len(earlier),
        out_specs=pl.BlockSpec((experts, step, width), lambda s: (0, s, 0)),
        out_shape=jax.ShapeDtypeStruct((experts, depth, width), BF),
        compiler_params=pltpu.CompilerParams(vmem_limit_bytes=VMEM_LIMIT),
        cost_estimate=cost(5 * 10**9, 10**5),
        name="pack",
    )(weight, *earlier)


def swap(x, axis, how):
    return lax.ppermute(x, axis, [(i, how(i)) for i in range(lax.axis_size(axis))])


def near(j):
    return j ^ (2 if j % 2 == 0 else 4)


def beside(j):
    return j ^ 1


def far(j):
    return j ^ (4 if j % 2 == 0 else 2)


def exchange(packed):
    whole = lax.all_to_all(packed, "gx", split_axis=0, concat_axis=0, tiled=True)
    return whole.reshape(-1, packed.shape[2])


def after(x, *others):
    return lax.optimization_barrier((x, others))[0]


def small_call(kernel, name, arrays, earlier, outs, flops=10**6):
    return pl.pallas_call(
        kernel,
        in_specs=[vmem()] * len(arrays) + [anywhere()] * len(earlier),
        out_specs=[vmem()] * len(outs),
        out_shape=[jax.ShapeDtypeStruct(*out) for out in outs],
        compiler_params=pltpu.CompilerParams(vmem_limit_bytes=16 * 1024 * 1024),
        cost_estimate=cost(flops, 10**5),
        name=name,
    )(*arrays, *earlier)


def stack_kernel(count, *refs):
    out_ref, at = refs[-1], 0
    for ref in refs[:count]:
        out_ref[at : at + ref.shape[0], :] = ref[...]
        at += ref.shape[0]


def stack_rows(arrays, *earlier, flops=10**6):
    shape = (sum(x.shape[0] for x in arrays), arrays[0].shape[1])
    kernel = functools.partial(stack_kernel, len(arrays))
    return small_call(kernel, "stack", arrays, earlier, [(shape, BF)], flops)[0]


def join_kernel(keep_ref, came_ref, *rest):
    part_ref, pass_ref = rest[-2:]
    rows = part_ref.shape[0]
    total = keep_ref[...].astype(F32) + came_ref[...].astype(F32)
    part_ref[...] = total[:rows]
    pass_ref[...] = total[rows:].astype(BF)


def join(keep, came, *earlier):
    shape = (keep.shape[0] // 2, keep.shape[1])
    return small_call(join_kernel, "join", [keep, came], earlier, [(shape, F32), (shape, BF)])


def close_kernel(want, core_ref, part_ref, came_ref, *rest):
    total = part_ref[...] + came_ref[...].astype(F32)
    if want is not None:
        total = total + jnp.where(core_ref[0] == want, rest[0][...].astype(F32), 0.0)
    rest[-1][...] = total.astype(BF)


def close(want, core, part, came, earlier):
    arrays = [part, *came]
    return pl.pallas_call(
        functools.partial(close_kernel, want),
        in_specs=[smem()] + [vmem()] * len(arrays) + [anywhere()] * len(earlier),
        out_specs=vmem(),
        out_shape=jax.ShapeDtypeStruct(part.shape, BF),
        compiler_params=pltpu.CompilerParams(vmem_limit_bytes=16 * 1024 * 1024),
        cost_estimate=cost(10**6, 10**5),
        name="close",
    )(core, *arrays, *earlier)


def finish_kernel(stream_ref, part_ref, *rest):
    total = stream_ref[...] + part_ref[...]
    for ref in rest[:-1]:
        total = total + ref[...].astype(F32)
    rest[-1][...] = total


def swapped_experts(send, stream, pair, down):
    planes = lax.axis_size("gx")
    columns = lax.axis_size("gy")
    row, column = lax.axis_index("gx"), lax.axis_index("gy")
    place = jnp.stack([column * planes + row, beside(column) * planes + row]).astype(jnp.int32)
    core = (column % 2).astype(jnp.int32).reshape(1)

    def across(x, k):
        even, odd = ((0, 0), (1, 2), (2, 1), (3, 3))[k]
        pairs = [
            (i * columns + j, (i ^ (odd if j % 2 else even)) * columns + j)
            for i in range(planes)
            for j in range(columns)
        ]
        return lax.ppermute(x, ("gx", "gy"), pairs)


    mine = [send] + [across(send, k) for k in range(1, planes)]
    beyond = [swap(x, "gy", near) for x in mine]
    first = [stack_rows([mine[k], beyond[k]]) for k in range(3)]
    second = [swap(x, "gy", far) for x in first]
    other_pair = swap(after(pair, second[0], *first[1:], mine[3]), "gy", beside)
    down = exchange(after(down, first[0]))
    hidden, last = {}, ()

    def inner(k, pieces):
        hidden[k] = make_hidden(place, pieces, pair, other_pair, *last)
        return (hidden[k][1],)

    last = inner(0, [first[0], second[0]])
    first.append(stack_rows([mine[3], beyond[3]], *last))
    second.append(swap(first[3], "gy", far))
    last = inner(3, [first[3]])
    last = inner(1, [first[1], second[1]])
    last = inner(2, [first[2], second[2]])
    other_down = swap(after(down, hidden[2][1], second[3]), "gy", beside)
    outer = make_hidden(place, [second[3]], pair, other_pair, *last)

    made, arrived, parts, ends = {}, {}, {}, {}
    last = ()

    def put(k):
        if k == 3:
            away = make_down(1, *outer, down, other_down)[0]
            made[k] = [*make_down(1, *hidden[k], down, other_down, away), away]
        else:
            made[k] = make_down(2, *hidden[k], down, other_down, *last)
        arrived[k] = swap(made[k][1], "gy", far)
        return (made[k][0],)

    def turn(k, *earlier):
        parts[k], passed = join(made[k][0], arrived[k], *last, *earlier)
        ends[k] = swap(passed, "gy", near)
        return (passed,)

    def leave(k, *came):
        want = {1: 1, 2: 0}.get(k)
        passed = close(want, core, parts[k], [ends[k], *came], last)
        ends[k] = swap(passed, "gx", lambda i: i ^ 1) if k == 3 else across(passed, k)
        return (passed,)

    last = put(3)
    last = put(2)
    last = turn(3)
    last = put(1)
    last = leave(3)
    last = turn(2)
    last = put(0)
    last = leave(2, ends[3])
    last = turn(1)
    last = leave(1, ends[3])
    last = turn(0)
    arrays = [stream, parts[0], ends[0], ends[1], ends[2]]
    return small_call(finish_kernel, "finish", arrays, (), [(stream.shape, F32)])[0]


def gathered_experts(send, stream, routes, gate_up, down_proj):
    columns = lax.axis_size("gy")
    normed = send[:, :D]
    gates = send[:, D : D + EXPERTS].astype(F32) + send[:, D + 64 : D + 64 + EXPERTS].astype(F32)
    gate_weights = jnp.take_along_axis(gates, routes, axis=1)
    row_count = normed.shape[0]
    full_pair = lax.all_gather(gate_up, "gx", axis=0, tiled=True)
    full_down = lax.all_gather(down_proj, "gx", axis=0, tiled=True)
    flat_routes = routes.reshape(row_count * TOP)
    route_hits = (flat_routes[:, None] == jnp.arange(EXPERTS, dtype=jnp.int32)[None, :]).astype(
        jnp.int32
    )
    places = jnp.sum((jnp.cumsum(route_hits, axis=0) - 1) * route_hits, axis=1)
    targets = flat_routes * CAP + places
    repeated = jnp.repeat(normed, TOP, axis=0)
    experts_dev = full_pair.shape[1]
    outgoing_rows = (
        jnp.zeros((EXPERTS * CAP, D), BF)
        .at[targets]
        .set(repeated)
        .reshape(columns, experts_dev, CAP, D)
    )
    arrived = lax.all_to_all(outgoing_rows, "gy", split_axis=0, concat_axis=0, tiled=True)
    gate_pair = jnp.einsum("secd,def->secf", arrived, full_pair, preferred_element_type=F32)
    hidden = (jax.nn.silu(gate_pair[..., :FF]) * gate_pair[..., FF:]).astype(BF)
    expert_rows = jnp.einsum(
        "secf,def->secd", hidden, full_down, preferred_element_type=F32
    ).astype(BF)
    returned = lax.all_to_all(expert_rows, "gy", split_axis=0, concat_axis=0, tiled=True).reshape(
        EXPERTS * CAP, D
    )
    picked = returned[targets].astype(F32).reshape(row_count, TOP, D)
    return stream + jnp.sum(gate_weights[:, :, None] * picked, axis=1)


def gather_out(out_weight):
    columns = lax.axis_size("gy")
    share = out_weight.shape[0] // columns
    mine = lax.dynamic_slice_in_dim(out_weight, lax.axis_index("gy") * share, share, axis=0)
    whole = lax.all_gather(mine, ("gx", "gy"), axis=0, tiled=True)
    return jnp.zeros((1,), jnp.int32), [whole], ((1, whole.shape[0]),), whole


def start_out(out_weight):
    planes, columns = lax.axis_size("gx"), lax.axis_size("gy")
    share = out_weight.shape[0] // columns
    mine = lax.dynamic_slice_in_dim(out_weight, lax.axis_index("gy") * share, share, axis=0)
    return [swap(mine, "gx", lambda i, k=k: i ^ k) for k in range(1, planes)]


def swap_out(out_weight, first, asks):
    planes, columns = lax.axis_size("gx"), lax.axis_size("gy")
    row, column = lax.axis_index("gx"), lax.axis_index("gy")
    depth = out_weight.shape[0]
    share = depth // columns
    second = swap(first, "gy", near)
    both = stack_rows([first, second], asks)
    third = swap(both, "gy", far)
    parts = [first, second, third]
    near_of = lambda j: jnp.where(j % 2 == 0, j ^ 2, j ^ 4)
    far_of = lambda j: jnp.where(j % 2 == 0, j ^ 4, j ^ 2)
    at = [row * depth]
    for own in (column, column ^ 1):
        for source in (own, near_of(own), far_of(own), near_of(far_of(own))):
            at += [(row ^ k) * depth + source * share for k in range(1, planes)]
    one = (planes - 1, share)
    two = (2 * (planes - 1), share)
    at = jnp.stack(at).astype(jnp.int32)
    return at, parts, ((1, depth), one, one, two, one, one, two), both


def body(
    queries,
    new_kv,
    cache_pool,
    cache_len,
    local_pages,
    anchor,
    push_pages,
    prefill_attn,
    residual,
    out_weight,
    norm_gain,
    router,
    routes,
    gate_up,
    down_proj,
):
    columns = lax.axis_size("gy")
    slot_count = (MOVED + columns - 2) // (columns - 1)
    pool = cache_pool.reshape(-1, cache_pool.shape[2])
    planes = lax.axis_size("gx")
    swapped = columns == 8 and planes == 4 and gate_up.shape[1] == planes
    if swapped:
        out_parts = start_out(out_weight)
        pair = pack_experts(gate_up, 3)
        cache_len, anchor = after((cache_len, anchor), pair)
    matches = (anchor[:, None] == jnp.arange(columns, dtype=jnp.int32)[None, :]).astype(jnp.int32)
    earlier = jnp.sum((jnp.cumsum(matches, axis=0) - 1) * matches, axis=1)
    slots = columns * slot_count
    column = lax.axis_index("gy")
    chosen = anchor * slots + column * slot_count + earlier
    extra = jnp.stack([cache_len[LOCAL:] // PAGE, cache_len[LOCAL:] % PAGE, anchor, earlier], axis=1)
    extra = jnp.pad(extra.astype(BF), ((0, 0), (0, LANES - 4)))
    asks = lax.all_gather(
        jnp.concatenate([queries[LOCAL:], extra], axis=1), "gy", axis=0, tiled=True
    )
    extra = jnp.stack([cache_len[:LOCAL] // PAGE, cache_len[:LOCAL] % PAGE], axis=1)
    extra = jnp.pad(extra.astype(BF), ((0, 0), (0, LANES - 2)))
    own = jnp.concatenate([queries[:LOCAL], extra], axis=1)
    if swapped:

        pair = exchange(pair)
        out_parts = swap_out(out_weight, stack_rows(out_parts), asks)
        down = pack_experts(down_proj, 2, out_parts[3])
        asks = after(asks, out_parts[3], down)
    else:
        out_parts = gather_out(out_weight)
    here, reply = attend(
        column.astype(jnp.int32).reshape(1),
        own,
        asks,
        jnp.concatenate([local_pages, push_pages], axis=0),
        pool,
    )
    if swapped:
        at, parts, pieces, _ = out_parts
        others = [swap(part, "gy", beside) for part in after(parts, reply)]
        out_parts = (at, [out_weight] + parts + others, pieces, None)
    back = lax.all_gather(reply, "gy", axis=0, tiled=True)
    attended, stream, send = make_stream(
        chosen,
        queries,
        new_kv,
        here,
        back,
        prefill_attn,
        residual,
        out_parts,
        norm_gain.reshape(1, D),
        jnp.pad(router, ((0, 0), (0, LANES - EXPERTS))),
        routes,
    )
    if swapped:
        layer_out = swapped_experts(send, stream, pair, down)
    else:
        layer_out = gathered_experts(send, stream, routes, gate_up, down_proj)
    return (attended, layer_out)


def solution(mesh):
    placed = (
        P(("gx", "gy"), None),
        P(("gx", "gy"), None),
        P(("gx", "gy"), None, None),
        P(("gx", "gy")),
        P(("gx", "gy"), None),
        P(("gx", "gy")),
        P(("gx", "gy"), None),
        P(("gx", "gy"), None),
        P(("gx", "gy"), None),
        P("gx", None),
        P(),
        P(),
        P(("gx", "gy"), None),
        P("gx", "gy", None),
        P("gx", "gy", None),
    )
    return jax.shard_map(
        body,
        mesh=mesh,
        in_specs=placed,
        out_specs=(P(("gx", "gy"), None), P(("gx", "gy"), None)),
        check_vma=False,
    )
```
